32 devices in a mesh: seg: 4 (over y, x), expert: 8 (over z, core).
Axes of the slice: x: 2, y: 2, z: 4, core: 2. Of those that a mesh axis runs over, the one named last changes fastest.
Arguments:
- frames: bfloat16 [8192, 1536], P(('seg', 'expert')), may hold values from -6 to 6
- expert_ids: int32 [8192, 2], P(('seg', 'expert')), may hold values from 0 to 7, all different within a row; in each aligned block of 256 rows (0 to 255, 256 to 511, ...) at most 96 rows name the same one
- gate_weights: float32 [8192, 2], P(('seg', 'expert')), may hold values from 0.2 to 1
- up_weight: bfloat16 [8, 1536, 2048], P('expert'), may hold values from -0.15625 to 0.15625
- down_weight: bfloat16 [8, 2048, 1536], P('expert'), may hold values from -0.125 to 0.125
- out_weight: bfloat16 [1536, 64], replicated, may hold values from -0.15625 to 0.15625
- in_conv: bfloat16 [7, 64, 2048], replicated, may hold values from -0.25 to 0.25
- snake_first: float32 [2048], replicated, may hold values from 0.5 to 2
- first_up: bfloat16 [16, 2048, 512], P(None, None, 'seg'), may hold values from -0.09375 to 0.09375
Outputs:
- features: float32 [4, 16384, 512], P(None, 'expert', 'seg')
The draws below stay inside these ranges and needn't reach their ends.
Inputs may be any that keep to these rules, and one draw needn't show every extreme that they name: `expert_ids`: in each aligned block of 256 rows (the rows of one device) no expert is named by more than 96 of the block's choices, and some block reaches 96; the two ids of a token differ.
All inputs are finite; a program needn't handle non-finite values.
Results may differ from the reference program's by a relative error of at most 0.005.
Values may be sent and summed in bfloat16 or wider, within the bound.
No kernel may reach another device: no remote copies, remote signals or barrier semaphores. Data moves between devices by JAX's collectives and lax.ppermute only.
A program may use at most 128 MiB of HBM per device.

```python
import math
import jax
import jax.numpy as jnp
import numpy as np
from jax import lax

D = 1536
HID = 2048
LAT = 64
C1 = 2048
C2 = 512
TOK_DEV = 256
EXPERTS = 8
CAP = 96
SEQ_LEN = 2048
TOKENS = 8192
N_SEG = 4


def shard_levels(rng, extent, shards, low, largest):
    loudness, own = 1.0, jax.random.fold_in(rng, 6)
    for position, blocks in shards:
        steps = jnp.exp(jax.random.uniform(jax.random.fold_in(own, position), (blocks,), jnp.float32, low / len(shards), largest / len(shards)))
        loudness = loudness * jnp.repeat(steps, extent[position] // blocks).reshape([-1 if axis == position else 1 for axis in range(len(extent))])
    return loudness


def deal_out(stream_key, own, number, rows, number_of, top, limit, lean):
    ranking = jax.random.permutation(stream_key, number_of)
    crowded, usual = portions_of(number_of, rows * top, limit, lean, True), portions_of(number_of, rows * top, limit, lean, False)
    places = jnp.arange(number_of)

    def named(lengths, turn):
        used = int((lengths > 0).sum())
        fixed = max(1, used // 4)
        shifted = fixed + (places - fixed + turn * (used - fixed)) % max(1, number_of - fixed)
        return jnp.zeros((number_of,), jnp.int32).at[ranking[jnp.where(places < fixed, places, shifted)]].set(jnp.asarray(lengths, jnp.int32))

    lengths = jnp.where(number % 4 == 0, named(crowded, number // 4), named(usual, number - number // 4 - 1))
    mixed = jax.random.permutation(jax.random.fold_in(own, 3), number_of)
    donor, receiver = mixed[0:number_of // 2 * 2:2], mixed[1:number_of // 2 * 2:2]
    margin = jnp.minimum(lengths[donor] - 1, limit - lengths[receiver]) // 2
    margin = jnp.where((donor == ranking[0]) | (receiver == ranking[0]) | (lengths[receiver] == 0), 0, jnp.maximum(margin, 0))
    shifted = jax.random.randint(jax.random.fold_in(own, 4), (number_of // 2,), 0, 1 << 20) % (margin + 1)
    lengths = lengths.at[donor].add(-shifted).at[receiver].add(shifted)
    labels = jnp.searchsorted(jnp.cumsum(lengths), jnp.arange(rows * top), side="right").astype(jnp.int32)
    table = labels.reshape(top, rows).T
    table = table[jax.random.permutation(jax.random.fold_in(own, 1), rows)]
    turn = jax.random.randint(jax.random.fold_in(own, 2), (rows, 1), 0, top)
    return jnp.take_along_axis(table, (jnp.arange(top)[None, :] + turn) % top, axis=1)


def portions_of(number_of, total, bound, skew, full):
    portions = [(1 << 20) // math.isqrt(rank ** skew) + 1 for rank in range(1, number_of + 1)]
    largest = bound if full else min(bound, max(-(-total // number_of), total * portions[0] // sum(portions)))
    least = 1 if total - largest >= number_of - 1 else 0
    holding, surplus = [largest] + [least] * (number_of - 1), total - largest - least * (number_of - 1)
    while surplus > 0:
        free = [i for i in range(1, number_of) if holding[i] < largest] or [i for i in range(1, number_of) if holding[i] < bound]
        mass, left = sum([portions[i] for i in free]), surplus
        for i in free:
            extra = min(bound - holding[i], max(1, left * portions[i] // mass), surplus)
            holding[i] = holding[i] + extra
            surplus = surplus - extra
    return np.array(holding)


def scatter_about(rng, dims, width, bound, shards=(), kind=jnp.bfloat16):
    entries = jax.random.normal(rng, dims, jnp.float32) * width
    if len(shards) > 0:
        entries = shard_levels(rng, dims, shards, -0.22, 0.18) * entries
    return jnp.clip(entries, min=-bound, max=bound).astype(kind)


def setup_inputs(seed: int = 0) -> dict:
    splits = jax.random.split(jax.random.key(seed), 10)
    frames = scatter_about(splits[0], (TOKENS, D), 1.0, 6.0, ((0, 32),))
    expert_ids_keys = jax.random.split(jax.random.fold_in(splits[1], 1), TOKENS // TOK_DEV)
    expert_ids_turns = jax.random.permutation(jax.random.fold_in(splits[1], 3), TOKENS // TOK_DEV)
    expert_ids = jax.vmap(lambda own, number: deal_out(jax.random.fold_in(splits[1], 2), own, number, TOK_DEV, EXPERTS, 2, CAP, 2))(expert_ids_keys, expert_ids_turns).reshape((TOKENS, 2))
    gate_weights = jnp.clip(0.2 + 0.8 * jax.random.uniform(splits[2], (TOKENS, 2), jnp.float32) ** shard_levels(splits[2], (TOKENS, 2), ((0, 32),), -0.2, 0.2), 0.2, 1.0)
    up_weight = scatter_about(splits[3], (EXPERTS, D, HID), D ** -0.5, 0.15625, ((0, 8),))
    down_weight = scatter_about(splits[4], (EXPERTS, HID, D), HID ** -0.5, 0.125, ((0, 8),))
    out_weight = scatter_about(splits[5], (D, LAT), D ** -0.5, 0.15625)
    in_conv = scatter_about(splits[6], (7, LAT, C1), (7 * LAT) ** -0.5, 0.25)
    snake_first = jnp.clip(jnp.exp(jax.random.uniform(splits[7], (C1,), jnp.float32, math.log(0.5), math.log(2.0))), 0.5, 2.0)
    first_up = scatter_about(splits[8], (16, C1, C2), (2 * C1) ** -0.5, 0.09375, ((2, 4),))
    return dict(frames=frames, expert_ids=expert_ids, gate_weights=gate_weights, up_weight=up_weight, down_weight=down_weight, out_weight=out_weight, in_conv=in_conv, snake_first=snake_first, first_up=first_up)


def snake_act(values, alpha_row):
    return values + jnp.sin(alpha_row * values) ** 2 / alpha_row


def conv_seven(values, weights):
    length = values.shape[0]
    padded = jnp.pad(values, ((3, 3), (0, 0)))
    total = jnp.zeros((length, weights.shape[2]), jnp.float32)
    for tap_index in range(7):
        window = lax.slice_in_dim(padded, tap_index, tap_index + length, axis=0)
        total = total + jnp.dot(window, weights[tap_index], preferred_element_type=jnp.float32)
    return total


def upsample(values, weights):
    length = values.shape[0]
    padded = jnp.pad(values, ((1, 1), (0, 0))).astype(jnp.float32)
    wide = weights.astype(jnp.float32)
    prev_rows = padded[0:length]
    here_rows = padded[1:length + 1]
    next_rows = padded[2:length + 2]
    middle = jnp.einsum("lc,rco->lro", here_rows, wide[4:12])
    early_part = jnp.einsum("lc,rco->lro", prev_rows, wide[12:16])
    later_part = jnp.einsum("lc,rco->lro", next_rows, wide[0:4])
    joined = middle + jnp.concatenate([early_part, later_part], axis=1)
    return joined.reshape(length * 8, weights.shape[2])


def reference(frames, expert_ids, gate_weights, up_weight, down_weight, out_weight, in_conv, snake_first, first_up):
    devices_total = TOKENS // TOK_DEV
    flat_ids = expert_ids.reshape(devices_total, 2 * TOK_DEV)
    one_hot = (flat_ids[:, :, None] == jnp.arange(EXPERTS, dtype=jnp.int32)[None, None, :]).astype(jnp.int32)
    before = jnp.cumsum(one_hot, axis=1) - one_hot
    slot_pos = jnp.sum(before * one_hot, axis=2)
    dest_index = flat_ids * CAP + slot_pos
    local_index = jnp.arange(2 * TOK_DEV, dtype=jnp.int32)
    device_index = jnp.arange(devices_total, dtype=jnp.int32)
    global_index = device_index[:, None] * (2 * TOK_DEV) + local_index[None, :]
    table = jnp.full((devices_total, EXPERTS * CAP), -1, jnp.int32)
    table = table.at[device_index[:, None], dest_index].set(global_index)
    flat_gates = gate_weights.reshape(-1)

    def one_expert(carry, expert_index):
        assigned = lax.dynamic_slice_in_dim(table, expert_index * CAP, CAP, axis=1).reshape(-1)
        present = assigned >= 0
        safe_index = jnp.where(present, assigned, 0)
        token_index = safe_index // 2
        rows_in = frames[token_index]
        hidden_units = jax.nn.gelu(jnp.dot(rows_in, up_weight[expert_index], preferred_element_type=jnp.float32), approximate=True).astype(jnp.bfloat16)
        expert_out = jnp.dot(hidden_units, down_weight[expert_index], preferred_element_type=jnp.float32).astype(jnp.bfloat16)
        projected = jnp.dot(expert_out, out_weight, preferred_element_type=jnp.float32)
        weighting = jnp.where(present, flat_gates[safe_index], jnp.zeros_like(flat_gates[safe_index]))
        carry = carry.at[token_index].add(projected * weighting[:, None])
        return carry, None

    base = jnp.dot(frames, out_weight, preferred_element_type=jnp.float32)
    latent, _ = lax.scan(one_expert, base, jnp.arange(EXPERTS, dtype=jnp.int32))
    latent_low = latent.astype(jnp.bfloat16)
    results = []
    for sequence in range(N_SEG):
        rows = latent_low[sequence * SEQ_LEN:(sequence + 1) * SEQ_LEN]
        first_in = conv_seven(rows, in_conv)
        act_first = snake_act(first_in, snake_first).astype(jnp.bfloat16)
        results.append(upsample(act_first, first_up))
    return jnp.stack(results, axis=0)
```

```python
import functools
import math

import jax
import jax.numpy as jnp
from jax import lax
from jax.experimental import pallas as pl
from jax.experimental.pallas import tpu as pltpu
from jax.sharding import PartitionSpec as P

F32 = jnp.float32
BF16 = jnp.bfloat16
VMEM = pltpu.VMEM
SIN2 = (
    9.869603157043457,
    -32.469581604003906,
    42.72538375854492,
    -30.085954666137695,
    12.99073314666748,
    -3.2729504108428955,
)
ROUNDER = 12582912.0


def whole():
    return pl.BlockSpec(memory_space=VMEM)


def params(mib):
    return pltpu.CompilerParams(vmem_limit_bytes=mib * 1024 * 1024)


def slots_kernel(me_ref, ids_ref, frames_ref, *out_refs):
    n = len(out_refs)
    rows = frames_ref.shape[0]
    capacity = out_refs[0].shape[0]
    ids = ids_ref[...] ^ me_ref[0]
    step = lax.broadcasted_iota(jnp.int32, (max(n, 16), rows), 0)
    named = (ids[0:1] == step) | (ids[1:2] == step)
    earlier = lax.broadcasted_iota(jnp.int32, (rows, rows), 0) < lax.broadcasted_iota(
        jnp.int32, (rows, rows), 1
    )
    rank = jnp.dot(
        named.astype(F32).astype(BF16), earlier.astype(F32).astype(BF16), preferred_element_type=F32
    )
    rank = jnp.where(named, rank, -1.0)
    slot = lax.broadcasted_iota(jnp.int32, (capacity, rows), 0).astype(F32)
    frames = frames_ref[...]
    for k in range(n):
        pick = (slot == rank[k : k + 1]).astype(F32).astype(BF16)
        out_refs[k][...] = jnp.dot(pick, frames, preferred_element_type=F32).astype(BF16)


def make_slots(me, ids_t, frames, n, capacity):
    rows, width = frames.shape
    return pl.pallas_call(
        slots_kernel,
        out_shape=[jax.ShapeDtypeStruct((capacity, width), BF16)] * n,
        in_specs=[pl.BlockSpec(memory_space=pltpu.SMEM), whole(), whole()],
        out_specs=[whole()] * n,
        compiler_params=params(24),
    )(me, ids_t, frames)


def fold_kernel(down_ref, out_w_ref, folded_ref):
    full = lax.dot_general(
        down_ref[...], out_w_ref[...], (((1,), (1,)), ((), ())), preferred_element_type=F32
    )
    high = full.astype(BF16)
    low = (full - high.astype(F32)).astype(BF16)
    folded_ref[...] = jnp.concatenate([high, low], axis=1)


def fold_weights(down, out_w_t):
    hid, width = down.shape
    lat = out_w_t.shape[0]
    block = 512 if hid % 512 == 0 else hid
    return pl.pallas_call(
        fold_kernel,
        grid=(hid // block,),
        out_shape=jax.ShapeDtypeStruct((hid, 2 * lat), BF16),
        in_specs=[
            pl.BlockSpec((block, width), lambda i: (i, 0)),
            pl.BlockSpec((lat, width), lambda i: (0, 0)),
        ],
        out_specs=pl.BlockSpec((block, 2 * lat), lambda i: (i, 0)),
        compiler_params=params(16),
        cost_estimate=pl.CostEstimate(
            flops=2 * hid * width * 2 * lat, bytes_accessed=2 * hid * width, transcendentals=0
        ),
    )(down, out_w_t)


def table_kernel(me_ref, ids_ref, gates_ref, frames_ref, out_w_ref, pick_ref, scale_ref, base_ref):
    n = pick_ref.shape[0]
    rows = frames_ref.shape[0]
    capacity = pick_ref.shape[2]
    base_ref[...] = lax.dot_general(
        frames_ref[...], out_w_ref[...], (((1,), (1,)), ((), ())), preferred_element_type=F32
    )
    ids = ids_ref[...] ^ me_ref[0]
    step = lax.broadcasted_iota(jnp.int32, (rows, 128), 1)
    first = ids[:, 0:1] == step
    second = ids[:, 1:2] == step
    named = first | second
    earlier = lax.broadcasted_iota(jnp.int32, (rows, rows), 0) > lax.broadcasted_iota(
        jnp.int32, (rows, rows), 1
    )
    rank = jnp.dot(
        earlier.astype(F32).astype(BF16), named.astype(F32).astype(BF16), preferred_element_type=F32
    )
    rank = jnp.where(named, rank, -1.0)
    gates = gates_ref[...]
    scale_ref[...] = jnp.where(first, gates[:, 0:1], jnp.where(second, gates[:, 1:2], 0.0))
    slot = lax.broadcasted_iota(jnp.int32, (rows, capacity), 1).astype(F32)
    for k in range(n):
        pick_ref[k] = (slot == rank[:, k : k + 1]).astype(F32).astype(BF16)


def make_table(me, ids, gates, frames, out_w_t, n, capacity):
    rows, width = frames.shape
    lat = out_w_t.shape[0]
    return pl.pallas_call(
        table_kernel,
        out_shape=[
            jax.ShapeDtypeStruct((n, rows, capacity), BF16),
            jax.ShapeDtypeStruct((rows, 128), F32),
            jax.ShapeDtypeStruct((rows, lat), F32),
        ],
        in_specs=[pl.BlockSpec(memory_space=pltpu.SMEM)] + [whole()] * 4,
        out_specs=[whole()] * 3,
        compiler_params=params(16),
        cost_estimate=pl.CostEstimate(
            flops=2 * rows * width * 128, bytes_accessed=2 * rows * width, transcendentals=0
        ),
    )(me, ids, gates, frames, out_w_t)


def expert_kernel(count, *refs):
    chunk_refs = refs[:count]
    up_ref, folded_ref = refs[count : count + 2]
    out_refs = refs[count + 2 : count + 2 + count]
    total_ref = refs[-1]
    capacity = chunk_refs[0].shape[0]
    hid = up_ref.shape[1]
    block = 256 if hid % 256 == 0 else hid
    rows = jnp.concatenate([ref[...] for ref in chunk_refs], axis=0)
    total_ref[...] = jnp.zeros_like(total_ref)

    @pl.loop(0, hid // block)
    def _(i):
        at = pl.multiple_of(i * block, block)
        v = jnp.dot(rows, up_ref[:, pl.ds(at, block)], preferred_element_type=F32)
        inner = v * (0.7978845608 + (0.7978845608 * 0.044715) * (v * v))
        hidden = (0.5 * v * (1.0 + jnp.tanh(inner))).astype(BF16)
        total_ref[...] += jnp.dot(hidden, folded_ref[pl.ds(at, block), :], preferred_element_type=F32)

    lat = folded_ref.shape[1] // 2
    total = total_ref[...]
    value = total[:, :lat] + total[:, lat:]
    high = value.astype(BF16)
    low = (value - high.astype(F32)).astype(BF16)
    both = jnp.concatenate([high, low], axis=1)
    for j in range(count):
        out_refs[j][...] = both[j * capacity : (j + 1) * capacity]


def run_expert(chunks, up, folded):
    count = len(chunks)
    capacity, width = chunks[0].shape
    hid = up.shape[1]
    return pl.pallas_call(
        functools.partial(expert_kernel, count),
        out_shape=[jax.ShapeDtypeStruct((capacity, folded.shape[1]), BF16)] * count,
        in_specs=[whole()] * (count + 2),
        out_specs=[whole()] * count,
        scratch_shapes=[pltpu.VMEM((count * capacity, folded.shape[1]), F32)],
        compiler_params=params(24),
        cost_estimate=pl.CostEstimate(
            flops=2 * count * capacity * hid * (width + 256),
            bytes_accessed=2 * hid * width,
            transcendentals=count * capacity * hid,
        ),
    )(*chunks, up, folded)


def combine_kernel(n, *refs):
    part_refs = refs[:n]
    pick_ref, scale_ref, base_ref, low_ref = refs[n:]
    lat = base_ref.shape[1]
    latent = base_ref[...]
    for k in range(n):
        picked = jnp.dot(pick_ref[k], part_refs[k][...], preferred_element_type=F32)
        latent = latent + scale_ref[:, k : k + 1] * (picked[:, :lat] + picked[:, lat:])
    low_ref[...] = latent.astype(BF16)


def combine(parts, pick, scale, base):
    n = len(parts)
    return pl.pallas_call(
        functools.partial(combine_kernel, n),
        out_shape=jax.ShapeDtypeStruct(base.shape, BF16),
        in_specs=[whole()] * (n + 3),
        out_specs=whole(),
        compiler_params=params(16),
    )(*parts, pick, scale, base)


def decoder_kernel(segs, place_ref, *refs):
    lat_refs = refs[:segs]
    conv_ref, alpha_ref, up_ref, out_ref = refs[segs : segs + 4]
    padded, prev, here, after, rows_out, sems = refs[segs + 4 :]
    length = here.shape[0]
    channels = conv_ref.shape[1]
    width = up_ref.shape[2]
    lat = lat_refs[0].shape[1]
    taps = conv_ref.shape[0] // lat
    halo = lat_refs[0].shape[0]
    span = length + 16
    block = 256
    own = place_ref[0]
    is_first = place_ref[1] == 0
    is_last = place_ref[1] == place_ref[2] - 1
    frame = lax.broadcasted_iota(jnp.int32, (span, block), 0) - 1
    keep = jnp.logical_not(((frame < 0) & is_first) | ((frame >= length) & is_last))

    def out_copy(k):
        return pltpu.make_async_copy(rows_out.at[k % 2], out_ref.at[own ^ k], sems.at[k % 2])

    for k in range(segs):
        padded[0:halo, :] = lat_refs[k][...].astype(F32)
        padded[halo:, :] = jnp.zeros((padded.shape[0] - halo, lat), F32)
        windows = jnp.concatenate(
            [padded[j : j + span, :] for j in range(taps)], axis=1
        ).astype(BF16)

        @pl.loop(0, channels // block)
        def _(i):
            at = pl.multiple_of(i * block, block)
            v = jnp.dot(windows, conv_ref[:, pl.ds(at, block)], preferred_element_type=F32)
            turns = v * alpha_ref[0:1, pl.ds(at, block)]
            part = turns - ((turns + ROUNDER) - ROUNDER)
            s = part * part
            poly = SIN2[-1]
            for c in SIN2[-2::-1]:
                poly = poly * s + c
            act = v + (poly * s) * alpha_ref[1:2, pl.ds(at, block)]
            act = jnp.where(keep, act, 0.0)
            prev[:, pl.ds(at, block)] = act[0:length].astype(BF16)
            here[:, pl.ds(at, block)] = act[1 : length + 1].astype(BF16)
            after[:, pl.ds(at, block)] = act[2 : length + 2].astype(BF16)

        if k >= 2:
            out_copy(k - 2).wait()
        for r in range(0, 8, 2):
            side, far = (prev, r + 12) if r < 4 else (after, r - 4)
            near_w = jnp.concatenate([up_ref[r + 4], up_ref[r + 5]], axis=1)
            far_w = jnp.concatenate([up_ref[far], up_ref[far + 1]], axis=1)
            res = jnp.dot(here[...], near_w, preferred_element_type=F32) + jnp.dot(
                side[...], far_w, preferred_element_type=F32
            )
            rows_out[k % 2, pl.ds(r, length, stride=8), :] = res[:, :width]
            rows_out[k % 2, pl.ds(r + 1, length, stride=8), :] = res[:, width:]
        out_copy(k).start()
    for k in range(max(0, segs - 2), segs):
        out_copy(k).wait()


def decode(place, slabs, conv, alpha, first_up):
    segs = len(slabs)
    length = slabs[0].shape[0] - 8
    channels = conv.shape[1]
    width = first_up.shape[2]
    lat = slabs[0].shape[1]
    return pl.pallas_call(
        functools.partial(decoder_kernel, segs),
        out_shape=jax.ShapeDtypeStruct((segs, 8 * length, width), F32),
        in_specs=[pl.BlockSpec(memory_space=pltpu.SMEM)] + [whole()] * (segs + 3),
        out_specs=pl.BlockSpec(memory_space=pl.ANY),
        scratch_shapes=[
            pltpu.VMEM((length + 32, lat), F32),
            pltpu.VMEM((length, channels), BF16),
            pltpu.VMEM((length, channels), BF16),
            pltpu.VMEM((length, channels), BF16),
            pltpu.VMEM((2, 8 * length, width), F32),
            pltpu.SemaphoreType.DMA((2,)),
        ],
        compiler_params=params(32),
        cost_estimate=pl.CostEstimate(
            flops=2 * segs * length * channels * (16 * width + 512),
            bytes_accessed=4 * segs * 8 * length * width,
            transcendentals=0,
        ),
    )(place, *slabs, conv, alpha, first_up)


def local(
    frames,
    expert_ids,
    gate_weights,
    up_weight,
    down_weight,
    out_weight,
    in_conv,
    snake_first,
    first_up,
):
    rows, _ = frames.shape
    n = lax.axis_size("expert")
    segs = lax.axis_size("seg")
    capacity = -(-(3 * rows // n) // 16) * 16
    me = lax.axis_index("expert")
    me_array = jnp.full((1,), me, jnp.int32)

    def partner(axis, size, k):
        return [(i, i ^ k) for i in range(size)]

    chunks = make_slots(me_array, expert_ids.T, frames, n, capacity)
    arrived = {0: chunks[0]}
    for k in range(n - 1, 0, -1):
        arrived[k] = lax.ppermute(chunks[k], "expert", partner("expert", n, k))
    out_w_t = out_weight.T
    folded = fold_weights(down_weight[0], out_w_t)
    pick, scale, base = make_table(
        me_array, expert_ids, gate_weights, frames, out_w_t, n, capacity
    )
    parts = {}
    groups = [(0, 1), (2, 3)] + [tuple(range(j, min(j + 4, n))) for j in range(4, n, 4)]
    for group in groups:
        done = run_expert([arrived[k] for k in group], up_weight[0], folded)
        for k, value in zip(group, done):
            parts[k] = value if k == 0 else lax.ppermute(value, "expert", partner("expert", n, k))
    latent_low = combine([parts[k] for k in range(n)], pick, scale, base)

    up_pairs = [(i, i + 1) for i in range(n - 1)]
    down_pairs = [(i + 1, i) for i in range(n - 1)]
    before = lax.ppermute(latent_low[rows - 4 :], "expert", up_pairs)
    later = lax.ppermute(latent_low[:4], "expert", down_pairs)
    slab = jnp.concatenate([before, latent_low, later], axis=0)
    slabs = [slab] + [
        lax.ppermute(slab, "seg", partner("seg", segs, k)) for k in range(1, segs)
    ]
    place = jnp.stack([lax.axis_index("seg"), me, jnp.int32(n)]).astype(jnp.int32)
    alpha = jnp.stack([snake_first * (1.0 / math.pi), 1.0 / snake_first])
    conv = in_conv.reshape(-1, in_conv.shape[2])
    return decode(place, slabs, conv, alpha, first_up)


def solution(mesh):
    placed = (
        P(("seg", "expert"), None),
        P(("seg", "expert"), None),
        P(("seg", "expert"), None),
        P("expert", None, None),
        P("expert", None, None),
        P(),
        P(),
        P(),
        P(None, None, "seg"),
    )
    return jax.shard_map(
        local, mesh=mesh, in_specs=placed, out_specs=P(None, "expert", "seg"), check_vma=False
    )
```

```python
import functools
import math

import jax
import jax.numpy as jnp
from jax import lax
from jax.experimental import pallas as pl
from jax.experimental.pallas import tpu as pltpu
from jax.sharding import PartitionSpec as P

F32 = jnp.float32
BF16 = jnp.bfloat16
VMEM = pltpu.VMEM
SIN2 = (
    9.869603157043457,
    -32.469581604003906,
    42.72538375854492,
    -30.085954666137695,
    12.99073314666748,
    -3.2729504108428955,
)
ROUNDER = 12582912.0


def whole():
    return pl.BlockSpec(memory_space=VMEM)


def params(mib):
    return pltpu.CompilerParams(vmem_limit_bytes=mib * 1024 * 1024)


def slots_kernel(me_ref, ids_ref, frames_ref, *out_refs):
    n = len(out_refs)
    rows = frames_ref.shape[0]
    capacity = out_refs[0].shape[0]
    ids = ids_ref[...] ^ me_ref[0]
    step = lax.broadcasted_iota(jnp.int32, (max(n, 16), rows), 0)
    named = (ids[0:1] == step) | (ids[1:2] == step)
    earlier = lax.broadcasted_iota(jnp.int32, (rows, rows), 0) < lax.broadcasted_iota(
        jnp.int32, (rows, rows), 1
    )
    rank = jnp.dot(
        named.astype(F32).astype(BF16), earlier.astype(F32).astype(BF16), preferred_element_type=F32
    )
    rank = jnp.where(named, rank, -1.0)
    slot = lax.broadcasted_iota(jnp.int32, (capacity, rows), 0).astype(F32)
    frames = frames_ref[...]
    for k in range(n):
        pick = (slot == rank[k : k + 1]).astype(F32).astype(BF16)
        out_refs[k][...] = jnp.dot(pick, frames, preferred_element_type=F32).astype(BF16)


def make_slots(me, ids_t, frames, n, capacity):
    rows, width = frames.shape
    return pl.pallas_call(
        slots_kernel,
        out_shape=[jax.ShapeDtypeStruct((capacity, width), BF16)] * n,
        in_specs=[pl.BlockSpec(memory_space=pltpu.SMEM), whole(), whole()],
        out_specs=[whole()] * n,
        compiler_params=params(24),
    )(me, ids_t, frames)


def fold_kernel(down_ref, out_w_ref, folded_ref):
    full = lax.dot_general(
        down_ref[...], out_w_ref[...], (((1,), (1,)), ((), ())), preferred_element_type=F32
    )
    high = full.astype(BF16)
    low = (full - high.astype(F32)).astype(BF16)
    folded_ref[...] = jnp.concatenate([high, low], axis=1)


def fold_weights(down, out_w_t):
    hid, width = down.shape
    lat = out_w_t.shape[0]
    block = 512 if hid % 512 == 0 else hid
    return pl.pallas_call(
        fold_kernel,
        grid=(hid // block,),
        out_shape=jax.ShapeDtypeStruct((hid, 2 * lat), BF16),
        in_specs=[
            pl.BlockSpec((block, width), lambda i: (i, 0)),
            pl.BlockSpec((lat, width), lambda i: (0, 0)),
        ],
        out_specs=pl.BlockSpec((block, 2 * lat), lambda i: (i, 0)),
        compiler_params=params(16),
        cost_estimate=pl.CostEstimate(
            flops=2 * hid * width * 2 * lat, bytes_accessed=2 * hid * width, transcendentals=0
        ),
    )(down, out_w_t)


def table_kernel(me_ref, ids_ref, gates_ref, frames_ref, out_w_ref, pick_ref, scale_ref, base_ref):
    n = pick_ref.shape[0]
    rows = frames_ref.shape[0]
    capacity = pick_ref.shape[2]
    base_ref[...] = lax.dot_general(
        frames_ref[...], out_w_ref[...], (((1,), (1,)), ((), ())), preferred_element_type=F32
    )
    ids = ids_ref[...] ^ me_ref[0]
    step = lax.broadcasted_iota(jnp.int32, (rows, 128), 1)
    first = ids[:, 0:1] == step
    second = ids[:, 1:2] == step
    named = first | second
    earlier = lax.broadcasted_iota(jnp.int32, (rows, rows), 0) > lax.broadcasted_iota(
        jnp.int32, (rows, rows), 1
    )
    rank = jnp.dot(
        earlier.astype(F32).astype(BF16), named.astype(F32).astype(BF16), preferred_element_type=F32
    )
    rank = jnp.where(named, rank, -1.0)
    gates = gates_ref[...]
    scale_ref[...] = jnp.where(first, gates[:, 0:1], jnp.where(second, gates[:, 1:2], 0.0))
    slot = lax.broadcasted_iota(jnp.int32, (rows, capacity), 1).astype(F32)
    for k in range(n):
        pick_ref[k] = (slot == rank[:, k : k + 1]).astype(F32).astype(BF16)


def make_table(me, ids, gates, frames, out_w_t, n, capacity):
    rows, width = frames.shape
    lat = out_w_t.shape[0]
    return pl.pallas_call(
        table_kernel,
        out_shape=[
            jax.ShapeDtypeStruct((n, rows, capacity), BF16),
            jax.ShapeDtypeStruct((rows, 128), F32),
            jax.ShapeDtypeStruct((rows, lat), F32),
        ],
        in_specs=[pl.BlockSpec(memory_space=pltpu.SMEM)] + [whole()] * 4,
        out_specs=[whole()] * 3,
        compiler_params=params(16),
        cost_estimate=pl.CostEstimate(
            flops=2 * rows * width * 128, bytes_accessed=2 * rows * width, transcendentals=0
        ),
    )(me, ids, gates, frames, out_w_t)


def expert_kernel(count, *refs):
    chunk_refs = refs[:count]
    up_ref, folded_ref = refs[count : count + 2]
    out_refs = refs[count + 2 : count + 2 + count]
    total_ref = refs[-1]
    capacity = chunk_refs[0].shape[0]
    hid = up_ref.shape[1]
    block = 256 if hid % 256 == 0 else hid
    rows = jnp.concatenate([ref[...] for ref in chunk_refs], axis=0)
    total_ref[...] = jnp.zeros_like(total_ref)

    @pl.loop(0, hid // block)
    def _(i):
        at = pl.multiple_of(i * block, block)
        v = jnp.dot(rows, up_ref[:, pl.ds(at, block)], preferred_element_type=F32)
        inner = v * (0.7978845608 + (0.7978845608 * 0.044715) * (v * v))
        hidden = (0.5 * v * (1.0 + jnp.tanh(inner))).astype(BF16)
        total_ref[...] += jnp.dot(hidden, folded_ref[pl.ds(at, block), :], preferred_element_type=F32)

    lat = folded_ref.shape[1] // 2
    total = total_ref[...]
    value = total[:, :lat] + total[:, lat:]
    high = value.astype(BF16)
    low = (value - high.astype(F32)).astype(BF16)
    both = jnp.concatenate([high, low], axis=1)
    for j in range(count):
        out_refs[j][...] = both[j * capacity : (j + 1) * capacity]


def run_expert(chunks, up, folded):
    count = len(chunks)
    capacity, width = chunks[0].shape
    hid = up.shape[1]
    return pl.pallas_call(
        functools.partial(expert_kernel, count),
        out_shape=[jax.ShapeDtypeStruct((capacity, folded.shape[1]), BF16)] * count,
        in_specs=[whole()] * (count + 2),
        out_specs=[whole()] * count,
        scratch_shapes=[pltpu.VMEM((count * capacity, folded.shape[1]), F32)],
        compiler_params=params(24),
        cost_estimate=pl.CostEstimate(
            flops=2 * count * capacity * hid * (width + 256),
            bytes_accessed=2 * hid * width,
            transcendentals=count * capacity * hid,
        ),
    )(*chunks, up, folded)


def combine_kernel(n, *refs):
    part_refs = refs[:n]
    pick_ref, scale_ref, base_ref, low_ref = refs[n:]
    lat = base_ref.shape[1]
    latent = base_ref[...]
    for k in range(n):
        picked = jnp.dot(pick_ref[k], part_refs[k][...], preferred_element_type=F32)
        latent = latent + scale_ref[:, k : k + 1] * (picked[:, :lat] + picked[:, lat:])
    low_ref[...] = latent.astype(BF16)


def combine(parts, pick, scale, base):
    n = len(parts)
    return pl.pallas_call(
        functools.partial(combine_kernel, n),
        out_shape=jax.ShapeDtypeStruct(base.shape, BF16),
        in_specs=[whole()] * (n + 3),
        out_specs=whole(),
        compiler_params=params(16),
    )(*parts, pick, scale, base)


def snake(v, turns_row, inverse_row):
    turns = v * turns_row
    part = turns - ((turns + ROUNDER) - ROUNDER)
    s = part * part
    poly = SIN2[-1]
    for c in SIN2[-2::-1]:
        poly = poly * s + c
    return v + (poly * s) * inverse_row


def decoder_kernel(segs, place_ref, *refs):
    lat_refs = refs[:segs]
    conv_ref, alpha_ref, up_hbm, out_ref = refs[segs : segs + 4]
    padded, windows, act, up_ref, rows_out, sems, up_sem = refs[segs + 4 :]
    span, channels = act.shape[1:]
    length = span - 16
    width = up_ref.shape[2]
    halo, lat = lat_refs[0].shape
    taps = conv_ref.shape[0] // lat
    block = 256
    own = place_ref[0]
    is_first = place_ref[1] == 0
    is_last = place_ref[1] == place_ref[2] - 1
    up_copy = pltpu.make_async_copy(up_hbm, up_ref, up_sem)
    up_copy.start()

    def out_copy(k):
        return pltpu.make_async_copy(rows_out.at[k], out_ref.at[own ^ k], sems.at[k])

    row = lax.broadcasted_iota(jnp.int32, (16, taps * lat), 0)
    edge_row = lax.broadcasted_iota(jnp.int32, (16, block), 0)
    gone = ((edge_row == 0) & is_first) | ((edge_row == 1) & is_last)
    for k in range(segs):
        padded[0:halo, :] = lat_refs[k][...].astype(F32)

        def window(start, rows):
            return jnp.concatenate([padded[start + j : start + j + rows] for j in range(taps)], axis=1)

        windows[k, 0:length] = window(1, length).astype(BF16)
        edges = jnp.where(row == 0, window(0, 1), jnp.where(row == 1, window(length + 1, 1), 0.0))
        windows[k, length:] = edges.astype(BF16)
        for at in range(0, channels, block):
            cols = slice(at, at + block)
            v = jnp.dot(windows[k], conv_ref[:, cols], preferred_element_type=F32)
            value = snake(v, alpha_ref[0:1, cols], alpha_ref[1:2, cols])
            act[k, 0:length, cols] = value[:length].astype(BF16)
            act[k, length:, cols] = jnp.where(gone, 0.0, value[length:]).astype(BF16)
    up_copy.wait()
    for k in range(segs):
        for r in range(0, 8, 2):
            far = r + 12 if r < 4 else r - 4
            near_w = jnp.concatenate([up_ref[r + 4], up_ref[r + 5]], axis=1)
            far_w = jnp.concatenate([up_ref[far], up_ref[far + 1]], axis=1)
            near = jnp.dot(act[k, 0:length], near_w, preferred_element_type=F32)
            side = jnp.dot(act[k], far_w, preferred_element_type=F32)
            if r < 4:
                moved = [side[length : length + 1], side[: length - 1]]
            else:
                moved = [side[1:length], side[length + 1 : length + 2]]
            res = near + jnp.concatenate(moved, axis=0)
            rows_out[k, pl.ds(r, length, stride=8), :] = res[:, :width]
            rows_out[k, pl.ds(r + 1, length, stride=8), :] = res[:, width:]
        out_copy(k).start()
    for k in range(segs):
        out_copy(k).wait()


def decode(place, slabs, conv, alpha, first_up):
    segs = len(slabs)
    length = slabs[0].shape[0] - 8
    channels = conv.shape[1]
    width = first_up.shape[2]
    lat = slabs[0].shape[1]
    return pl.pallas_call(
        functools.partial(decoder_kernel, segs),
        out_shape=jax.ShapeDtypeStruct((segs, 8 * length, width), F32),
        in_specs=[pl.BlockSpec(memory_space=pltpu.SMEM)]
        + [whole()] * (segs + 2)
        + [pl.BlockSpec(memory_space=pl.ANY)],
        out_specs=pl.BlockSpec(memory_space=pl.ANY),
        scratch_shapes=[
            pltpu.VMEM((length + 16, lat), F32),
            pltpu.VMEM((segs, length + 16, conv.shape[0]), BF16),
            pltpu.VMEM((segs, length + 16, channels), BF16),
            pltpu.VMEM(first_up.shape, BF16),
            pltpu.VMEM((segs, 8 * length, width), F32),
            pltpu.SemaphoreType.DMA((segs,)),
            pltpu.SemaphoreType.DMA,
        ],
        compiler_params=params(52),
        cost_estimate=pl.CostEstimate(
            flops=2 * segs * length * channels * (16 * width + 512),
            bytes_accessed=4 * segs * 8 * length * width,
            transcendentals=0,
        ),
    )(place, *slabs, conv, alpha, first_up)


def local(
    frames,
    expert_ids,
    gate_weights,
    up_weight,
    down_weight,
    out_weight,
    in_conv,
    snake_first,
    first_up,
):
    rows, _ = frames.shape
    n = lax.axis_size("expert")
    segs = lax.axis_size("seg")
    capacity = -(-(3 * rows // n) // 16) * 16
    me = lax.axis_index("expert")
    me_array = jnp.full((1,), me, jnp.int32)

    def partner(axis, size, k):
        return [(i, i ^ k) for i in range(size)]

    chunks = make_slots(me_array, expert_ids.T, frames, n, capacity)
    arrived = {0: chunks[0]}
    for k in range(n - 1, 0, -1):
        arrived[k] = lax.ppermute(chunks[k], "expert", partner("expert", n, k))
    out_w_t = out_weight.T
    pick, scale, base = make_table(
        me_array, expert_ids, gate_weights, frames, out_w_t, n, capacity
    )
    down, pick = lax.optimization_barrier((down_weight[0], pick))
    folded = fold_weights(down, out_w_t)
    parts = {}
    groups = [tuple(range(j, j + 2)) for j in range(0, n, 2)]
    for group in groups:
        done = run_expert([arrived[k] for k in group], up_weight[0], folded)
        for k, value in zip(group, done):
            parts[k] = value if k == 0 else lax.ppermute(value, "expert", partner("expert", n, k))
    latent_low = combine([parts[k] for k in range(n)], pick, scale, base)

    up_pairs = [(i, i + 1) for i in range(n - 1)]
    down_pairs = [(i + 1, i) for i in range(n - 1)]
    before = lax.ppermute(latent_low[rows - 4 :], "expert", up_pairs)
    later = lax.ppermute(latent_low[:4], "expert", down_pairs)
    slab = jnp.concatenate([before, latent_low, later], axis=0)
    slabs = [slab] + [
        lax.ppermute(slab, "seg", partner("seg", segs, k)) for k in range(1, segs)
    ]
    place = jnp.stack([lax.axis_index("seg"), me, jnp.int32(n)]).astype(jnp.int32)
    alpha = jnp.stack([snake_first * (1.0 / math.pi), 1.0 / snake_first])
    conv = in_conv.reshape(-1, in_conv.shape[2])
    return decode(place, slabs, conv, alpha, first_up)


def solution(mesh):
    placed = (
        P(("seg", "expert"), None),
        P(("seg", "expert"), None),
        P(("seg", "expert"), None),
        P("expert", None, None),
        P("expert", None, None),
        P(),
        P(),
        P(),
        P(None, None, "seg"),
    )
    return jax.shard_map(
        local, mesh=mesh, in_specs=placed, out_specs=P(None, "expert", "seg"), check_vma=False
    )
```

```python
import functools
import math

import jax
import jax.numpy as jnp
from jax import lax
from jax.experimental import pallas as pl
from jax.experimental.pallas import tpu as pltpu
from jax.sharding import PartitionSpec as P

F32 = jnp.float32
BF16 = jnp.bfloat16
VMEM = pltpu.VMEM
SIN2 = (
    9.869603157043457,
    -32.469581604003906,
    42.72538375854492,
    -30.085954666137695,
    12.99073314666748,
    -3.2729504108428955,
)
ROUNDER = 12582912.0


FREE = pl.CostEstimate(flops=0, bytes_accessed=0, transcendentals=0)


def whole():
    return pl.BlockSpec(memory_space=VMEM)


def params(mib):
    return pltpu.CompilerParams(vmem_limit_bytes=mib * 1024 * 1024)


EDGE = 4
EDGE_ROWS = 16


def token_key(token, rows):
    rest = jnp.where(token >= rows - EDGE, token - (rows - 2 * EDGE), token + EDGE)
    return jnp.where(token < EDGE, token, rest)


def one_hot(mask):
    return mask.astype(F32).astype(BF16)


def slots_kernel(steps, origin_ref, *refs):
    sources, out_refs = refs[: -len(steps)], refs[-len(steps) :]
    ids, frames = sources[0][...], sources[1][...]
    if len(sources) > 2:
        second = origin_ref[1] == 1
        ids = jnp.where(second, sources[2][...], ids)
        frames = jnp.where(second, sources[3][...], frames)
    rows = frames.shape[0]
    capacity = out_refs[0].shape[0]
    ids = ids ^ origin_ref[0]
    count = -(-len(steps) // 16) * 16
    step = lax.broadcasted_iota(jnp.int32, (count, rows), 0) + steps[0]
    named = (ids[0:1] == step) | (ids[1:2] == step)
    earlier = token_key(lax.broadcasted_iota(jnp.int32, (rows, rows), 0), rows) < token_key(
        lax.broadcasted_iota(jnp.int32, (rows, rows), 1), rows
    )
    rank = jnp.dot(one_hot(named), one_hot(earlier), preferred_element_type=F32)
    rank = jnp.where(named, rank, -1.0)
    slot = lax.broadcasted_iota(jnp.int32, (capacity, rows), 0).astype(F32)
    for j, ref in enumerate(out_refs):
        pick = one_hot(slot == rank[j : j + 1])
        ref[...] = jnp.dot(pick, frames, preferred_element_type=F32).astype(BF16)


def make_slots(origin, steps, sources, capacity):
    width = sources[1].shape[1]
    return pl.pallas_call(
        functools.partial(slots_kernel, steps),
        out_shape=[jax.ShapeDtypeStruct((capacity, width), BF16)] * len(steps),
        in_specs=[pl.BlockSpec(memory_space=pltpu.SMEM)] + [whole()] * len(sources),
        out_specs=[whole()] * len(steps),
        compiler_params=params(24),
        cost_estimate=FREE,
    )(origin, *sources)


def fold_kernel(down_ref, out_w_ref, folded_ref):
    full = lax.dot_general(
        down_ref[...], out_w_ref[...], (((1,), (1,)), ((), ())), preferred_element_type=F32
    )
    high = full.astype(BF16)
    low = (full - high.astype(F32)).astype(BF16)
    folded_ref[...] = jnp.concatenate([high, low], axis=1)


def fold_weights(down, out_w_t):
    hid, width = down.shape
    lat = out_w_t.shape[0]
    block = 512 if hid % 512 == 0 else hid
    return pl.pallas_call(
        fold_kernel,
        grid=(hid // block,),
        out_shape=jax.ShapeDtypeStruct((hid, 2 * lat), BF16),
        in_specs=[
            pl.BlockSpec((block, width), lambda i: (i, 0)),
            pl.BlockSpec((lat, width), lambda i: (0, 0)),
        ],
        out_specs=pl.BlockSpec((block, 2 * lat), lambda i: (i, 0)),
        compiler_params=params(16),
        cost_estimate=FREE,
    )(down, out_w_t)


def table_kernel(place_ref, ids_ref, gates_ref, pick_ref, scale_ref):
    n, span, columns = pick_ref.shape
    rows = span - 4 * EDGE
    capacity = columns - 2 * EDGE_ROWS

    def code(i):
        own = 1024 + token_key(i - EDGE, rows)
        late = jnp.where(i < rows + 3 * EDGE, i - rows - 2 * EDGE, 3072)
        tail = jnp.where(i < rows + 2 * EDGE, 2048 + i - rows - EDGE, late)
        return jnp.where(i < EDGE, i + EDGE, jnp.where(i < rows + EDGE, own, tail))

    line = lax.broadcasted_iota(jnp.int32, (span, 1), 0)
    line_code = code(line)
    other = code(lax.broadcasted_iota(jnp.int32, (span, span), 1))
    earlier = (other < line_code) & (other >= (line_code >> 10) * 1024)
    before = line_code < 1024
    after = (line_code >= 2048) & (line_code < 3072)
    lost = (before & (place_ref[0] == 0)) | (after & (place_ref[0] == place_ref[1] - 1))
    ids = jnp.where(lost | (line_code >= 3072), -1, ids_ref[...] ^ place_ref[0])
    step = lax.broadcasted_iota(jnp.int32, (span, 128), 1)
    first = ids[:, 0:1] == step
    second = ids[:, 1:2] == step
    named = first | second
    rank = jnp.dot(one_hot(earlier), one_hot(named), preferred_element_type=F32)
    rank = rank + jnp.where(before, capacity, jnp.where(after, capacity + EDGE_ROWS, 0)).astype(F32)
    rank = jnp.where(named, rank, -1.0)
    gates = gates_ref[...]
    scale_ref[...] = jnp.where(first, gates[:, 0:1], jnp.where(second, gates[:, 1:2], 0.0))
    slot = lax.broadcasted_iota(jnp.int32, (span, columns), 1).astype(F32)
    for k in range(n):
        pick_ref[k] = one_hot(slot == rank[:, k : k + 1])


def make_table(place, ids, gates, n, capacity):
    span = ids.shape[0]
    return pl.pallas_call(
        table_kernel,
        out_shape=[
            jax.ShapeDtypeStruct((n, span, capacity + 2 * EDGE_ROWS), BF16),
            jax.ShapeDtypeStruct((span, 128), F32),
        ],
        in_specs=[pl.BlockSpec(memory_space=pltpu.SMEM)] + [whole()] * 2,
        out_specs=[whole()] * 2,
        compiler_params=params(16),
        cost_estimate=FREE,
    )(place, ids, gates)


def expert_rows(rows, up_ref, folded_ref):
    hid = up_ref.shape[1]
    block = 256 if hid % 256 == 0 else hid
    total = None
    for at in range(0, hid, block):
        v = jnp.dot(rows, up_ref[:, at : at + block], preferred_element_type=F32)
        inner = v * (0.7978845608 + (0.7978845608 * 0.044715) * (v * v))
        hidden = (0.5 * v * (1.0 + jnp.tanh(inner))).astype(BF16)
        part = jnp.dot(hidden, folded_ref[at : at + block, :], preferred_element_type=F32)
        total = part if total is None else total + part
    lat = folded_ref.shape[1] // 2
    value = total[:, :lat] + total[:, lat:]
    high = value.astype(BF16)
    low = (value - high.astype(F32)).astype(BF16)
    return jnp.concatenate([high, low], axis=1)


def near_kernel(count, *refs):
    chunk_refs = refs[:count]
    up_ref, folded_ref, out_ref = refs[count:]
    capacity = chunk_refs[0].shape[0]
    rows = jnp.concatenate([ref[...] for ref in chunk_refs], axis=0)
    both = expert_rows(rows, up_ref, folded_ref)
    for j in range(count):
        out_ref[j] = both[j * capacity : (j + 1) * capacity]


def near_group(chunks, up, folded):
    count = len(chunks)
    capacity = chunks[0].shape[0]
    return pl.pallas_call(
        functools.partial(near_kernel, count),
        out_shape=jax.ShapeDtypeStruct((count, capacity, folded.shape[1]), BF16),
        in_specs=[whole()] * (count + 2),
        out_specs=whole(),
        compiler_params=params(24),
        cost_estimate=FREE,
    )(*chunks, up, folded)


def far_kernel(n, *refs):
    quarter, half = n // 4, n // 2
    place_ref, local_ref = refs[:2]
    chunk_refs = refs[2 : 2 + half]
    known_refs = refs[2 + half : 4 + half]
    up_ref, folded_ref = refs[4 + half : 6 + half]
    outs, held = refs[6 + half : -1], refs[-1]
    capacity = local_ref.shape[0]
    me = place_ref[0]
    is_inner = (me >= quarter) & (me < 3 * quarter)
    chunks = [ref[...] for ref in chunk_refs]
    chunks[quarter] = jnp.where(is_inner, local_ref[...], chunks[quarter])
    held[0:quarter] = known_refs[0][...]
    held[quarter:half] = known_refs[1][...]
    both = expert_rows(jnp.concatenate(chunks, axis=0), up_ref, folded_ref)
    for j in range(half):
        held[half + j] = both[j * capacity : (j + 1) * capacity]
    for k, ref in enumerate(outs):
        to = me ^ k
        left = me ^ jnp.where(to > 0, to - 1, to)
        right = me ^ jnp.where(to < n - 1, to + 1, to)
        ref[0:capacity] = held[k]
        ref[capacity : capacity + EDGE_ROWS] = held[left, 0:EDGE_ROWS]
        ref[capacity + EDGE_ROWS :] = held[right, 0:EDGE_ROWS]


def far_group(n, place, local_chunk, chunks, known, up, folded):
    capacity = local_chunk.shape[0]
    lanes = folded.shape[1]
    return pl.pallas_call(
        functools.partial(far_kernel, n),
        out_shape=[jax.ShapeDtypeStruct((capacity + 2 * EDGE_ROWS, lanes), BF16)] * n,
        in_specs=[pl.BlockSpec(memory_space=pltpu.SMEM)] + [whole()] * (n // 2 + 5),
        out_specs=[whole()] * n,
        scratch_shapes=[pltpu.VMEM((n, capacity, lanes), BF16)],
        compiler_params=params(24),
        cost_estimate=FREE,
    )(place, local_chunk, *chunks, *known, up, folded)


def combine_kernel(n, *refs):
    part_refs = refs[:n]
    pick_ref, scale_ref, base_ref, low_ref = refs[n:]
    lat = base_ref.shape[1]
    latent = base_ref[...]
    for k in range(n):
        picked = jnp.dot(pick_ref[k], part_refs[k][...], preferred_element_type=F32)
        latent = latent + scale_ref[:, k : k + 1] * (picked[:, :lat] + picked[:, lat:])
    low_ref[...] = latent.astype(BF16)


def combine(parts, pick, scale, base):
    n = len(parts)
    return pl.pallas_call(
        functools.partial(combine_kernel, n),
        out_shape=jax.ShapeDtypeStruct(base.shape, BF16),
        in_specs=[whole()] * (n + 3),
        out_specs=whole(),
        compiler_params=params(16),
    )(*parts, pick, scale, base)


def snake(v, turns_row, inverse_row):
    turns = v * turns_row
    part = turns - ((turns + ROUNDER) - ROUNDER)
    s = part * part
    poly = SIN2[-1]
    for c in SIN2[-2::-1]:
        poly = poly * s + c
    return v + (poly * s) * inverse_row


def decoder_kernel(segs, place_ref, *refs):
    lat_refs = refs[:segs]
    conv_ref, alpha_ref, up_hbm, out_ref = refs[segs : segs + 4]
    padded, windows, act, up_ref, rows_out, sems, up_sem = refs[segs + 4 :]
    span, channels = act.shape[1:]
    length = span - 16
    width = up_ref.shape[2]
    halo, lat = lat_refs[0].shape
    taps = conv_ref.shape[0] // lat
    block = 256
    own = place_ref[0]
    is_first = place_ref[1] == 0
    is_last = place_ref[1] == place_ref[2] - 1
    up_copy = pltpu.make_async_copy(up_hbm, up_ref, up_sem)
    up_copy.start()

    def out_copy(k):
        return pltpu.make_async_copy(rows_out.at[k], out_ref.at[own ^ k], sems.at[k])

    row = lax.broadcasted_iota(jnp.int32, (16, taps * lat), 0)
    edge_row = lax.broadcasted_iota(jnp.int32, (16, block), 0)
    gone = ((edge_row == 0) & is_first) | ((edge_row == 1) & is_last)
    for k in range(segs):
        padded[0:halo, :] = lat_refs[k][...].astype(F32)

        def window(start, rows):
            return jnp.concatenate([padded[start + j : start + j + rows] for j in range(taps)], axis=1)

        windows[k, 0:length] = window(1, length).astype(BF16)
        edges = jnp.where(row == 0, window(0, 1), jnp.where(row == 1, window(length + 1, 1), 0.0))
        windows[k, length:] = edges.astype(BF16)
        for at in range(0, channels, block):
            cols = slice(at, at + block)
            v = jnp.dot(windows[k], conv_ref[:, cols], preferred_element_type=F32)
            value = snake(v, alpha_ref[0:1, cols], alpha_ref[1:2, cols])
            act[k, 0:length, cols] = value[:length].astype(BF16)
            act[k, length:, cols] = jnp.where(gone, 0.0, value[length:]).astype(BF16)
    up_copy.wait()
    for k in range(segs):
        for r in range(0, 8, 2):
            far = r + 12 if r < 4 else r - 4
            near_w = jnp.concatenate([up_ref[r + 4], up_ref[r + 5]], axis=1)
            far_w = jnp.concatenate([up_ref[far], up_ref[far + 1]], axis=1)
            near = jnp.dot(act[k, 0:length], near_w, preferred_element_type=F32)
            side = jnp.dot(act[k], far_w, preferred_element_type=F32)
            if r < 4:
                moved = [side[length : length + 1], side[: length - 1]]
            else:
                moved = [side[1:length], side[length + 1 : length + 2]]
            res = near + jnp.concatenate(moved, axis=0)
            rows_out[k, pl.ds(r, length, stride=8), :] = res[:, :width]
            rows_out[k, pl.ds(r + 1, length, stride=8), :] = res[:, width:]
        out_copy(k).start()
    for k in range(segs):
        out_copy(k).wait()


def decode(place, slabs, conv, alpha, first_up):
    segs = len(slabs)
    length = slabs[0].shape[0] - 4 * EDGE
    channels = conv.shape[1]
    width = first_up.shape[2]
    lat = slabs[0].shape[1]
    return pl.pallas_call(
        functools.partial(decoder_kernel, segs),
        out_shape=jax.ShapeDtypeStruct((segs, 8 * length, width), F32),
        in_specs=[pl.BlockSpec(memory_space=pltpu.SMEM)]
        + [whole()] * (segs + 2)
        + [pl.BlockSpec(memory_space=pl.ANY)],
        out_specs=pl.BlockSpec(memory_space=pl.ANY),
        scratch_shapes=[
            pltpu.VMEM((length + 16, lat), F32),
            pltpu.VMEM((segs, length + 16, conv.shape[0]), BF16),
            pltpu.VMEM((segs, length + 16, channels), BF16),
            pltpu.VMEM(first_up.shape, BF16),
            pltpu.VMEM((segs, 8 * length, width), F32),
            pltpu.SemaphoreType.DMA((segs,)),
            pltpu.SemaphoreType.DMA,
        ],
        compiler_params=params(52),
        cost_estimate=FREE,
    )(place, *slabs, conv, alpha, first_up)


def local(
    frames,
    expert_ids,
    gate_weights,
    up_weight,
    down_weight,
    out_weight,
    in_conv,
    snake_first,
    first_up,
):
    rows, _ = frames.shape
    n = lax.axis_size("expert")
    segs = lax.axis_size("seg")
    quarter, half = n // 4, n // 2
    capacity = -(-(3 * rows // n) // 16) * 16
    me = lax.axis_index("expert")
    place = jnp.stack([me, jnp.int32(n)]).astype(jnp.int32)
    inner = range(quarter, 3 * quarter)
    across_by = 3 * quarter
    is_inner = ((me >= quarter) & (me < across_by)).astype(jnp.int32)

    def swap(value, k, members=range(n)):
        return lax.ppermute(value, "expert", [(i, i ^ k) for i in members])

    across = swap(frames, across_by, inner)
    ids_t = expert_ids.T
    across_ids = swap(ids_t, across_by, inner)
    own = jnp.stack([me, 0]).astype(jnp.int32)
    chunks = make_slots(own, range(half), (ids_t, frames), capacity)
    near = [chunks[0]] + [swap(chunks[k], k) for k in range(1, half)]
    origin = jnp.stack([me ^ (is_inner * across_by), is_inner]).astype(jnp.int32)
    sent = make_slots(
        origin, range(half, n), (ids_t, frames, across_ids, across), capacity
    )
    far = []
    for k, value in zip(range(half, n), sent):
        pairs = [(i, i ^ (k ^ across_by if i in inner else k)) for i in range(n)]
        far.append(lax.ppermute(value, "expert", [(i, j) for i, j in pairs if i != j]))

    base = jnp.dot(frames, out_weight, preferred_element_type=F32)

    def edges(value):
        return jnp.concatenate([value[:EDGE], value[rows - EDGE :]], axis=0)

    lat = base.shape[1]
    packed = jnp.concatenate(
        [edges(base), edges(expert_ids).astype(F32), edges(gate_weights)], axis=1
    )
    left = lax.ppermute(packed, "expert", [(i, i + 1) for i in range(n - 1)])
    right = lax.ppermute(packed, "expert", [(i + 1, i) for i in range(n - 1)])

    def extended(value, columns, fill):
        parts = [left[EDGE:, columns], value.astype(F32), right[:EDGE, columns], left[:EDGE, columns]]
        rest = jnp.full((EDGE, value.shape[1]), fill, F32)
        return jnp.concatenate(parts + [rest], axis=0)

    ids_all = extended(expert_ids, slice(lat, lat + 2), -1).astype(jnp.int32)
    gates_all = extended(gate_weights, slice(lat + 2, lat + 4), 0)
    base_all = extended(base, slice(0, lat), 0)
    pick, scale = make_table(place, ids_all, gates_all, n, capacity)
    folded = fold_weights(down_weight[0], out_weight.T)

    up = up_weight[0]
    known = [near_group(near[:quarter], up, folded), near_group(near[quarter:], up, folded)]
    place, pick, scale, base_all, known = lax.optimization_barrier(
        (place, pick, scale, base_all, known)
    )
    back = far_group(n, place, sent[quarter], far, known, up, folded)
    parts = [back[0]] + [swap(back[k], k) for k in range(1, n)]
    slab = combine(parts, pick, scale, base_all)

    slabs = [slab] + [
        lax.ppermute(slab, "seg", [(i, i ^ k) for i in range(segs)]) for k in range(1, segs)
    ]
    spot = jnp.stack([lax.axis_index("seg"), me, jnp.int32(n)]).astype(jnp.int32)
    alpha = jnp.stack([snake_first * (1.0 / math.pi), 1.0 / snake_first])
    conv = in_conv.reshape(-1, in_conv.shape[2])
    return decode(spot, slabs, conv, alpha, first_up)


def solution(mesh):
    placed = (
        P(("seg", "expert"), None),
        P(("seg", "expert"), None),
        P(("seg", "expert"), None),
        P("expert", None, None),
        P("expert", None, None),
        P(),
        P(),
        P(),
        P(None, None, "seg"),
    )
    return jax.shard_map(
        local, mesh=mesh, in_specs=placed, out_specs=P(None, "expert", "seg"), check_vma=False
    )
```

```python
import functools
import math

import jax
import jax.numpy as jnp
from jax import lax
from jax.experimental import pallas as pl
from jax.experimental.pallas import tpu as pltpu
from jax.sharding import PartitionSpec as P

F32 = jnp.float32
BF16 = jnp.bfloat16
VMEM = pltpu.VMEM
SIN2 = (
    9.869603157043457,
    -32.469581604003906,
    42.72538375854492,
    -30.085954666137695,
    12.99073314666748,
    -3.2729504108428955,
)
ROUNDER = 12582912.0


FREE = pl.CostEstimate(flops=0, bytes_accessed=0, transcendentals=0)


def whole():
    return pl.BlockSpec(memory_space=VMEM)


def params(mib):
    return pltpu.CompilerParams(vmem_limit_bytes=mib * 1024 * 1024)


EDGE = 4
EDGE_ROWS = 16


def token_key(token, rows):
    rest = jnp.where(token >= rows - EDGE, token - (rows - 2 * EDGE), token + EDGE)
    return jnp.where(token < EDGE, token, rest)


def one_hot(mask):
    return mask.astype(F32).astype(BF16)


def slots_kernel(steps, origin_ref, *refs):
    sources, out_refs = refs[: -len(steps)], refs[-len(steps) :]
    ids, frames = sources[0][...], sources[1][...]
    if len(sources) > 2:
        second = origin_ref[1] == 1
        ids = jnp.where(second, sources[2][...], ids)
        frames = jnp.where(second, sources[3][...], frames)
    rows = frames.shape[0]
    capacity = out_refs[0].shape[0]
    ids = ids ^ origin_ref[0]
    count = -(-len(steps) // 16) * 16
    step = lax.broadcasted_iota(jnp.int32, (count, rows), 0) + steps[0]
    named = (ids[0:1] == step) | (ids[1:2] == step)
    earlier = token_key(lax.broadcasted_iota(jnp.int32, (rows, rows), 0), rows) < token_key(
        lax.broadcasted_iota(jnp.int32, (rows, rows), 1), rows
    )
    rank = jnp.dot(one_hot(named), one_hot(earlier), preferred_element_type=F32)
    rank = jnp.where(named, rank, -1.0)
    slot = lax.broadcasted_iota(jnp.int32, (capacity, rows), 0).astype(F32)
    for j, ref in enumerate(out_refs):
        pick = one_hot(slot == rank[j : j + 1])
        ref[...] = jnp.dot(pick, frames, preferred_element_type=F32).astype(BF16)


def make_slots(origin, steps, sources, capacity):
    width = sources[1].shape[1]
    return pl.pallas_call(
        functools.partial(slots_kernel, steps),
        out_shape=[jax.ShapeDtypeStruct((capacity, width), BF16)] * len(steps),
        in_specs=[pl.BlockSpec(memory_space=pltpu.SMEM)] + [whole()] * len(sources),
        out_specs=[whole()] * len(steps),
        compiler_params=params(24),
        cost_estimate=FREE,
    )(origin, *sources)


def fold_kernel(down_ref, out_w_ref, folded_ref):
    full = lax.dot_general(
        down_ref[...], out_w_ref[...], (((1,), (1,)), ((), ())), preferred_element_type=F32
    )
    high = full.astype(BF16)
    low = (full - high.astype(F32)).astype(BF16)
    folded_ref[...] = jnp.concatenate([high, low], axis=1)


def fold_weights(down, out_w_t):
    hid, width = down.shape
    lat = out_w_t.shape[0]
    block = 512 if hid % 512 == 0 else hid
    return pl.pallas_call(
        fold_kernel,
        grid=(hid // block,),
        out_shape=jax.ShapeDtypeStruct((hid, 2 * lat), BF16),
        in_specs=[
            pl.BlockSpec((block, width), lambda i: (i, 0)),
            pl.BlockSpec((lat, width), lambda i: (0, 0)),
        ],
        out_specs=pl.BlockSpec((block, 2 * lat), lambda i: (i, 0)),
        compiler_params=params(16),
        cost_estimate=FREE,
    )(down, out_w_t)


def info_kernel(frames_ref, out_w_ref, ids_ref, gates_ref, info_ref, edge_ref):
    rows = frames_ref.shape[0]
    lat = out_w_ref.shape[0]
    base = lax.dot_general(
        frames_ref[...], out_w_ref[...], (((1,), (1,)), ((), ())), preferred_element_type=F32
    )
    lines = jnp.concatenate(
        [ids_ref[...].astype(F32), gates_ref[...], jnp.zeros((124, rows), F32)], axis=0
    )
    info_ref[...] = jnp.concatenate([base, jnp.transpose(lines)[:, : 128 - lat]], axis=1)
    edge_ref[0:EDGE] = info_ref[0:EDGE]
    edge_ref[EDGE:] = info_ref[rows - EDGE : rows]


def make_info(frames, out_w_t, ids_t, gates_t):
    rows = frames.shape[0]
    return pl.pallas_call(
        info_kernel,
        out_shape=[
            jax.ShapeDtypeStruct((rows, 128), F32),
            jax.ShapeDtypeStruct((2 * EDGE, 128), F32),
        ],
        in_specs=[whole()] * 4,
        out_specs=[whole()] * 2,
        compiler_params=params(16),
        cost_estimate=FREE,
    )(frames, out_w_t, ids_t, gates_t)


def table_kernel(lat, place_ref, info_ref, left_ref, right_ref, pick_ref, scale_ref, base_ref):
    n, span, columns = pick_ref.shape
    rows = info_ref.shape[0]
    capacity = columns - 2 * EDGE_ROWS
    me, size = place_ref[0], place_ref[1]
    info = jnp.concatenate(
        [
            left_ref[EDGE:],
            info_ref[...],
            right_ref[:EDGE],
            left_ref[:EDGE],
            jnp.zeros((EDGE, 128), F32),
        ],
        axis=0,
    )
    base_ref[...] = info[:, :lat]

    def code(i):
        own = 1024 + token_key(i - EDGE, rows)
        late = jnp.where(i < rows + 3 * EDGE, i - rows - 2 * EDGE, 3072)
        tail = jnp.where(i < rows + 2 * EDGE, 2048 + i - rows - EDGE, late)
        return jnp.where(i < EDGE, i + EDGE, jnp.where(i < rows + EDGE, own, tail))

    line = lax.broadcasted_iota(jnp.int32, (span, 1), 0)
    line_code = code(line)
    other = code(lax.broadcasted_iota(jnp.int32, (1, span), 1))
    earlier = (other < line_code) & (other >= (line_code >> 10) * 1024)
    before = line_code < 1024
    after = (line_code >= 2048) & (line_code < 3072)
    lost = (before & ((me == 0) | (me == size // 2))) | (
        after & ((me == size - 1) | (me == size // 2 - 1))
    )
    ids = info[:, lat : lat + 2].astype(jnp.int32) ^ me
    ids = jnp.where(lost | (line_code >= 3072), -1, ids)
    step = lax.broadcasted_iota(jnp.int32, (span, 128), 1)
    first = ids[:, 0:1] == step
    second = ids[:, 1:2] == step
    named = first | second
    rank = jnp.dot(one_hot(earlier), one_hot(named), preferred_element_type=F32)
    rank = rank + jnp.where(before, capacity, jnp.where(after, capacity + EDGE_ROWS, 0)).astype(F32)
    rank = jnp.where(named, rank, -1.0)
    scale_ref[...] = jnp.where(
        first, info[:, lat + 2 : lat + 3], jnp.where(second, info[:, lat + 3 : lat + 4], 0.0)
    )
    slot = lax.broadcasted_iota(jnp.int32, (span, columns), 1).astype(F32)
    for k in range(n):
        pick_ref[k] = one_hot(slot == rank[:, k : k + 1])


def make_table(place, info, left, right, lat, n, capacity):
    span = info.shape[0] + 4 * EDGE
    return pl.pallas_call(
        functools.partial(table_kernel, lat),
        out_shape=[
            jax.ShapeDtypeStruct((n, span, capacity + 2 * EDGE_ROWS), BF16),
            jax.ShapeDtypeStruct((span, 128), F32),
            jax.ShapeDtypeStruct((span, lat), F32),
        ],
        in_specs=[pl.BlockSpec(memory_space=pltpu.SMEM)] + [whole()] * 3,
        out_specs=[whole()] * 3,
        compiler_params=params(16),
        cost_estimate=FREE,
    )(place, info, left, right)


def expert_rows(rows, up_ref, folded_ref):
    hid = up_ref.shape[1]
    block = 256 if hid % 256 == 0 else hid
    total = None
    for at in range(0, hid, block):
        v = jnp.dot(rows, up_ref[:, at : at + block], preferred_element_type=F32)
        inner = v * (0.7978845608 + (0.7978845608 * 0.044715) * (v * v))
        hidden = (0.5 * v * (1.0 + jnp.tanh(inner))).astype(BF16)
        part = jnp.dot(hidden, folded_ref[at : at + block, :], preferred_element_type=F32)
        total = part if total is None else total + part
    lat = folded_ref.shape[1] // 2
    value = total[:, :lat] + total[:, lat:]
    high = value.astype(BF16)
    low = (value - high.astype(F32)).astype(BF16)
    return jnp.concatenate([high, low], axis=1)


def write_returns(n, me, held, first, outs):
    capacity = held.shape[1]
    half = n // 2
    for j, ref in enumerate(outs):
        k = first + j
        to = me ^ k
        place = to % half
        left = me ^ jnp.where(place > 0, to - 1, to)
        right = me ^ jnp.where(place < half - 1, to + 1, to)
        ref[0:capacity] = held[k]
        ref[capacity : capacity + EDGE_ROWS] = held[left, 0:EDGE_ROWS]
        ref[capacity + EDGE_ROWS :] = held[right, 0:EDGE_ROWS]


def group_kernel(n, far, place_ref, local_ref, *refs):
    quarter, half = n // 4, n // 2
    chunk_refs = refs[: half - 1 + far]
    up_ref, folded_ref = refs[half - 1 + far : half + 1 + far]
    outs, held = refs[half + 1 + far : -1], refs[-1]
    capacity = local_ref.shape[0]
    me = place_ref[0]
    chunks = [ref[...] for ref in chunk_refs]
    if far:
        is_inner = (me >= quarter) & (me < 3 * quarter)
        chunks[quarter] = jnp.where(is_inner, local_ref[...], chunks[quarter])
    else:
        chunks = [local_ref[...]] + chunks
    both = expert_rows(jnp.concatenate(chunks, axis=0), up_ref, folded_ref)
    first = half if far else 0
    for j in range(half):
        held[first + j] = both[j * capacity : (j + 1) * capacity]
    write_returns(n, me, held, first, outs)


def run_group(n, far, place, local_chunk, chunks, up, folded):
    capacity = local_chunk.shape[0]
    lanes = folded.shape[1]
    return pl.pallas_call(
        functools.partial(group_kernel, n, far),
        out_shape=[jax.ShapeDtypeStruct((capacity + 2 * EDGE_ROWS, lanes), BF16)] * (n // 2),
        in_specs=[pl.BlockSpec(memory_space=pltpu.SMEM)] + [whole()] * (len(chunks) + 3),
        out_specs=[whole()] * (n // 2),
        scratch_shapes=[pltpu.VMEM((n, capacity, lanes), BF16)],
        compiler_params=params(24),
        cost_estimate=FREE,
    )(place, local_chunk, *chunks, up, folded)


def combine_kernel(n, place_ref, *refs):
    part_refs = refs[:n]
    pick_ref, scale_ref, base_ref, low_ref, middle_ref = refs[n:]
    span, lat = base_ref.shape
    latent = base_ref[...]
    for k in range(n):
        picked = jnp.dot(pick_ref[k], part_refs[k][...], preferred_element_type=F32)
        latent = latent + scale_ref[:, k : k + 1] * (picked[:, :lat] + picked[:, lat:])
    low = latent.astype(BF16)
    low_ref[...] = low
    middle_ref[...] = jnp.where(
        place_ref[0] >= place_ref[1] // 2, low[:EDGE_ROWS], low[span - EDGE_ROWS :]
    )


def combine(place, parts, pick, scale, base):
    n = len(parts)
    return pl.pallas_call(
        functools.partial(combine_kernel, n),
        out_shape=[
            jax.ShapeDtypeStruct(base.shape, BF16),
            jax.ShapeDtypeStruct((EDGE_ROWS, base.shape[1]), BF16),
        ],
        in_specs=[pl.BlockSpec(memory_space=pltpu.SMEM)] + [whole()] * (n + 3),
        out_specs=[whole()] * 2,
        compiler_params=params(16),
        cost_estimate=FREE,
    )(place, *parts, pick, scale, base)


def snake(v, turns_row, inverse_row):
    turns = v * turns_row
    part = turns - ((turns + ROUNDER) - ROUNDER)
    s = part * part
    poly = SIN2[-1]
    for c in SIN2[-2::-1]:
        poly = poly * s + c
    return v + (poly * s) * inverse_row


def decoder_kernel(segs, place_ref, *refs):
    lat_refs = refs[:segs]
    conv_ref, alpha_ref, up_hbm, out_ref = refs[segs : segs + 4]
    padded, windows, act, up_ref, rows_out, sems, up_sem = refs[segs + 4 :]
    span, channels = act.shape[1:]
    length = span - 16
    width = up_ref.shape[2]
    lat = lat_refs[0].shape[1]
    taps = conv_ref.shape[0] // lat
    block = 256
    own = place_ref[0]
    is_first = place_ref[1] == 0
    is_last = place_ref[1] == place_ref[2] - 1
    up_copy = pltpu.make_async_copy(up_hbm, up_ref, up_sem)
    up_copy.start()

    def out_copy(k):
        return pltpu.make_async_copy(rows_out.at[k], out_ref.at[own ^ k], sems.at[k])

    row = lax.broadcasted_iota(jnp.int32, (16, taps * lat), 0)
    edge_row = lax.broadcasted_iota(jnp.int32, (16, block), 0)
    gone = ((edge_row == 0) & is_first) | ((edge_row == 1) & is_last)
    for k in range(segs):
        slab = lat_refs[k][...].astype(F32)
        middle = slab[span:]
        padded[...] = slab[:span]
        before = jnp.where(place_ref[1] == place_ref[2] // 2, middle[:EDGE], slab[:EDGE])
        end = length + EDGE
        after = jnp.where(
            place_ref[1] == place_ref[2] // 2 - 1, middle[EDGE : 2 * EDGE], slab[end : end + EDGE]
        )
        padded[0:EDGE] = before
        padded[end : end + EDGE] = after

        def window(start, rows):
            return jnp.concatenate([padded[start + j : start + j + rows] for j in range(taps)], axis=1)

        windows[k, 0:length] = window(1, length).astype(BF16)
        edges = jnp.where(row == 0, window(0, 1), jnp.where(row == 1, window(length + 1, 1), 0.0))
        windows[k, length:] = edges.astype(BF16)
        for at in range(0, channels, block):
            cols = slice(at, at + block)
            v = jnp.dot(windows[k], conv_ref[:, cols], preferred_element_type=F32)
            value = snake(v, alpha_ref[0:1, cols], alpha_ref[1:2, cols])
            act[k, 0:length, cols] = value[:length].astype(BF16)
            act[k, length:, cols] = jnp.where(gone, 0.0, value[length:]).astype(BF16)
    up_copy.wait()
    for k in range(segs):
        for r in range(0, 8, 2):
            far = r + 12 if r < 4 else r - 4
            near_w = jnp.concatenate([up_ref[r + 4], up_ref[r + 5]], axis=1)
            far_w = jnp.concatenate([up_ref[far], up_ref[far + 1]], axis=1)
            near = jnp.dot(act[k, 0:length], near_w, preferred_element_type=F32)
            side = jnp.dot(act[k], far_w, preferred_element_type=F32)
            if r < 4:
                moved = [side[length : length + 1], side[: length - 1]]
            else:
                moved = [side[1:length], side[length + 1 : length + 2]]
            res = near + jnp.concatenate(moved, axis=0)
            rows_out[k, pl.ds(r, length, stride=8), :] = res[:, :width]
            rows_out[k, pl.ds(r + 1, length, stride=8), :] = res[:, width:]
        out_copy(k).start()
    for k in range(segs):
        out_copy(k).wait()


def decode(place, slabs, conv, alpha, first_up):
    segs = len(slabs)
    length = slabs[0].shape[0] - 4 * EDGE - EDGE_ROWS
    channels = conv.shape[1]
    width = first_up.shape[2]
    lat = slabs[0].shape[1]
    return pl.pallas_call(
        functools.partial(decoder_kernel, segs),
        out_shape=jax.ShapeDtypeStruct((segs, 8 * length, width), F32),
        in_specs=[pl.BlockSpec(memory_space=pltpu.SMEM)]
        + [whole()] * (segs + 2)
        + [pl.BlockSpec(memory_space=pl.ANY)],
        out_specs=pl.BlockSpec(memory_space=pl.ANY),
        scratch_shapes=[
            pltpu.VMEM((length + 16, lat), F32),
            pltpu.VMEM((segs, length + 16, conv.shape[0]), BF16),
            pltpu.VMEM((segs, length + 16, channels), BF16),
            pltpu.VMEM(first_up.shape, BF16),
            pltpu.VMEM((segs, 8 * length, width), F32),
            pltpu.SemaphoreType.DMA((segs,)),
            pltpu.SemaphoreType.DMA,
        ],
        compiler_params=params(52),
        cost_estimate=FREE,
    )(place, *slabs, conv, alpha, first_up)


def local(
    frames,
    expert_ids,
    gate_weights,
    up_weight,
    down_weight,
    out_weight,
    in_conv,
    snake_first,
    first_up,
):
    rows, _ = frames.shape
    n = lax.axis_size("expert")
    segs = lax.axis_size("seg")
    quarter, half = n // 4, n // 2
    capacity = -(-(3 * rows // n) // 16) * 16
    me = lax.axis_index("expert")
    place = jnp.stack([me, jnp.int32(n)]).astype(jnp.int32)
    inner = range(quarter, 3 * quarter)
    across_by = 3 * quarter
    is_inner = ((me >= quarter) & (me < across_by)).astype(jnp.int32)

    def swap(value, k, members=range(n)):
        return lax.ppermute(value, "expert", [(i, i ^ k) for i in members])

    across = swap(frames, across_by, inner)
    ids_t = expert_ids.T
    across_ids = swap(ids_t, across_by, inner)
    own = jnp.stack([me, 0]).astype(jnp.int32)
    chunks = make_slots(own, range(half), (ids_t, frames), capacity)
    near = [swap(chunks[k], k) for k in range(1, half)]
    lat = out_weight.shape[1]
    info, edge = make_info(frames, out_weight.T, ids_t, gate_weights.T)
    left = lax.ppermute(edge, "expert", [(i, i + 1) for i in range(n - 1)])
    right = lax.ppermute(edge, "expert", [(i + 1, i) for i in range(n - 1)])
    folded = fold_weights(down_weight[0], out_weight.T)
    origin = jnp.stack([me ^ (is_inner * across_by), is_inner]).astype(jnp.int32)
    origin, near, left, right, folded = lax.optimization_barrier(
        (origin, near, left, right, folded)
    )
    sent = make_slots(
        origin, range(half, n), (ids_t, frames, across_ids, across), capacity
    )
    far = []
    for k, value in zip(range(half, n), sent):
        pairs = [(i, i ^ (k ^ across_by if i in inner else k)) for i in range(n)]
        far.append(lax.ppermute(value, "expert", [(i, j) for i, j in pairs if i != j]))
    up = up_weight[0]
    info, chunk, _ = lax.optimization_barrier((info, chunks[0], sent))
    pick, scale, base = make_table(place, info, left, right, lat, n, capacity)
    back = run_group(n, False, place, chunk, near, up, folded)
    parts = [back[0]] + [swap(back[k], k) for k in range(1, half)]
    place, pick, scale, base, parts = lax.optimization_barrier((place, pick, scale, base, parts))
    back = run_group(n, True, place, sent[quarter], far, up, folded)
    parts += [swap(back[k], half + k) for k in range(half)]
    slab, middle = combine(place, parts, pick, scale, base)
    middle = lax.ppermute(middle, "expert", [(half - 1, half), (half, half - 1)])
    slab = jnp.concatenate([slab, middle], axis=0)

    slabs = [slab] + [
        lax.ppermute(slab, "seg", [(i, i ^ k) for i in range(segs)]) for k in range(1, segs)
    ]
    spot = jnp.stack([lax.axis_index("seg"), me, jnp.int32(n)]).astype(jnp.int32)
    alpha = jnp.stack([snake_first * (1.0 / math.pi), 1.0 / snake_first])
    conv = in_conv.reshape(-1, in_conv.shape[2])
    return decode(spot, slabs, conv, alpha, first_up)


def solution(mesh):
    placed = (
        P(("seg", "expert"), None),
        P(("seg", "expert"), None),
        P(("seg", "expert"), None),
        P("expert", None, None),
        P("expert", None, None),
        P(),
        P(),
        P(),
        P(None, None, "seg"),
    )
    return jax.shard_map(
        local, mesh=mesh, in_specs=placed, out_specs=P(None, "expert", "seg"), check_vma=False
    )
```

```python
import functools
import math

import jax
import jax.numpy as jnp
from jax import lax
from jax.experimental import pallas as pl
from jax.experimental.pallas import tpu as pltpu
from jax.sharding import PartitionSpec as P

F32 = jnp.float32
BF16 = jnp.bfloat16
VMEM = pltpu.VMEM
SIN2 = (
    9.869603157043457,
    -32.469581604003906,
    42.72538375854492,
    -30.085954666137695,
    12.99073314666748,
    -3.2729504108428955,
)
ROUNDER = 12582912.0


FREE = pl.CostEstimate(flops=0, bytes_accessed=0, transcendentals=0)


def whole():
    return pl.BlockSpec(memory_space=VMEM)


def params(mib):
    return pltpu.CompilerParams(vmem_limit_bytes=mib * 1024 * 1024)


EDGE = 4
EDGE_ROWS = 16


def token_key(token, rows):
    rest = jnp.where(token >= rows - EDGE, token - (rows - 2 * EDGE), token + EDGE)
    return jnp.where(token < EDGE, token, rest)


def one_hot(mask):
    return mask.astype(F32).astype(BF16)


def is_neighbour(k):
    return k & (k + 1) == 0 and k > 0


def edge_rows(frames, ids, gates):
    rows, width = frames.shape
    parts = []
    for choice in range(2):
        rest = gates[choice : choice + 1]
        for _ in range(3):
            part = rest.astype(BF16).astype(F32)
            parts.append(part)
            rest = rest - part
    meta = jnp.concatenate([ids.astype(F32)] + parts, axis=0)
    meta = jnp.concatenate([meta, jnp.zeros((8, width - rows), F32)], axis=1)
    ends = [frames[:16].astype(F32)[:EDGE], frames[rows - 16 :].astype(F32)[16 - EDGE :]]
    return jnp.concatenate(ends + [meta], axis=0).astype(BF16)


def slots_kernel(steps, origin_ref, *refs):
    sources, out_refs = refs[: -len(steps)], refs[-len(steps) :]
    ids, frames = sources[0][...], sources[1][...]
    if len(sources) == 3:
        capacity = out_refs[0].shape[0]
        extra = edge_rows(frames, ids, sources[2][...])
        for k, ref in zip(steps, out_refs):
            if is_neighbour(k):
                ref[capacity:] = extra
    else:
        second = origin_ref[1] == 1
        ids = jnp.where(second, sources[2][...], ids)
        frames = jnp.where(second, sources[3][...], frames)
    rows = frames.shape[0]
    capacity = out_refs[0].shape[0]
    ids = ids ^ origin_ref[0]
    count = -(-len(steps) // 16) * 16
    step = lax.broadcasted_iota(jnp.int32, (count, rows), 0) + steps[0]
    named = (ids[0:1] == step) | (ids[1:2] == step)
    earlier = token_key(lax.broadcasted_iota(jnp.int32, (rows, rows), 0), rows) < token_key(
        lax.broadcasted_iota(jnp.int32, (rows, rows), 1), rows
    )
    rank = jnp.dot(one_hot(named), one_hot(earlier), preferred_element_type=F32)
    rank = jnp.where(named, rank, -1.0)
    slot = lax.broadcasted_iota(jnp.int32, (capacity, rows), 0).astype(F32)
    for j, ref in enumerate(out_refs):
        pick = one_hot(slot == rank[j : j + 1])
        ref[0:capacity] = jnp.dot(pick, frames, preferred_element_type=F32).astype(BF16)


def make_slots(origin, steps, sources, capacity):
    width = sources[1].shape[1]
    return pl.pallas_call(
        functools.partial(slots_kernel, steps),
        out_shape=[
            jax.ShapeDtypeStruct(
                (capacity + EDGE_ROWS * (len(sources) == 3 and is_neighbour(k)), width), BF16
            )
            for k in steps
        ],
        in_specs=[pl.BlockSpec(memory_space=pltpu.SMEM)] + [whole()] * len(sources),
        out_specs=[whole()] * len(steps),
        compiler_params=params(24),
        cost_estimate=FREE,
    )(origin, *sources)


def fold_kernel(down_ref, out_w_ref, folded_ref):
    full = lax.dot_general(
        down_ref[...], out_w_ref[...], (((1,), (1,)), ((), ())), preferred_element_type=F32
    )
    high = full.astype(BF16)
    low = (full - high.astype(F32)).astype(BF16)
    folded_ref[...] = jnp.concatenate([high, low], axis=1)


def fold_weights(down, out_w_t):
    hid, width = down.shape
    lat = out_w_t.shape[0]
    block = 512 if hid % 512 == 0 else hid
    return pl.pallas_call(
        fold_kernel,
        grid=(hid // block,),
        out_shape=jax.ShapeDtypeStruct((hid, 2 * lat), BF16),
        in_specs=[
            pl.BlockSpec((block, width), lambda i: (i, 0)),
            pl.BlockSpec((lat, width), lambda i: (0, 0)),
        ],
        out_specs=pl.BlockSpec((block, 2 * lat), lambda i: (i, 0)),
        compiler_params=params(16),
        cost_estimate=FREE,
    )(down, out_w_t)


def table_kernel(
    links, place_ref, frames_ref, out_w_ref, ids_ref, gates_ref, *refs
):
    link_refs = refs[: len(links)]
    pick_ref, scale_ref, base_ref = refs[len(links) :]
    n, span, columns = pick_ref.shape
    rows, width = frames_ref.shape
    lat = out_w_ref.shape[0]
    capacity = columns - 2 * EDGE_ROWS
    me, size = place_ref[0], place_ref[1]

    def rows_of(frames, lines):
        base = lax.dot_general(
            frames, out_w_ref[...], (((1,), (1,)), ((), ())), preferred_element_type=F32
        )
        lines = jnp.concatenate([lines, jnp.zeros((128 - lines.shape[0], rows), F32)], axis=0)
        return base, jnp.transpose(lines)[:, : 128 - lat]

    def neighbour(other):
        extra = link_refs[0][capacity:]
        for k, ref in zip(links[1:], link_refs[1:]):
            extra = jnp.where((me ^ other) == k, ref[capacity:], extra)
        meta = extra[:, :rows].astype(F32)[2 * EDGE :]
        gates = [meta[j : j + 1] + meta[j + 1 : j + 2] + meta[j + 2 : j + 3] for j in (2, 5)]
        base, lines = rows_of(extra, jnp.concatenate([meta[:2]] + gates, axis=0))
        return jnp.concatenate(
            [
                jnp.concatenate([base[:EDGE], lines[:EDGE]], axis=1),
                jnp.concatenate([base[EDGE : 2 * EDGE], lines[rows - EDGE :]], axis=1),
            ],
            axis=0,
        )

    left, right = neighbour(me - 1), neighbour(me + 1)
    own = rows_of(
        frames_ref[...], jnp.concatenate([ids_ref[...].astype(F32), gates_ref[...]], axis=0)
    )
    info = jnp.concatenate(
        [
            left[EDGE:],
            jnp.concatenate(own, axis=1),
            right[:EDGE],
            left[:EDGE],
            jnp.zeros((EDGE, 128), F32),
        ],
        axis=0,
    )
    def code(i):
        own = 1024 + token_key(i - EDGE, rows)
        late = jnp.where(i < rows + 3 * EDGE, i - rows - 2 * EDGE, 3072)
        tail = jnp.where(i < rows + 2 * EDGE, 2048 + i - rows - EDGE, late)
        return jnp.where(i < EDGE, i + EDGE, jnp.where(i < rows + EDGE, own, tail))

    line = lax.broadcasted_iota(jnp.int32, (span, 1), 0)
    line_code = code(line)
    other = code(lax.broadcasted_iota(jnp.int32, (1, span), 1))
    earlier = (other < line_code) & (other >= (line_code >> 10) * 1024)
    before = line_code < 1024
    after = (line_code >= 2048) & (line_code < 3072)
    lost = (before & ((me == 0) | (me == size // 2))) | (
        after & ((me == size - 1) | (me == size // 2 - 1))
    )
    base_ref[...] = jnp.where(lost, 0.0, info[:, :lat])
    ids = info[:, lat : lat + 2].astype(jnp.int32) ^ me
    ids = jnp.where(lost | (line_code >= 3072), -1, ids)
    step = lax.broadcasted_iota(jnp.int32, (span, 128), 1)
    first = ids[:, 0:1] == step
    second = ids[:, 1:2] == step
    named = first | second
    rank = jnp.dot(one_hot(earlier), one_hot(named), preferred_element_type=F32)
    rank = rank + jnp.where(before, capacity, jnp.where(after, capacity + EDGE_ROWS, 0)).astype(F32)
    rank = jnp.where(named, rank, -1.0)
    scale_ref[...] = jnp.where(
        first, info[:, lat + 2 : lat + 3], jnp.where(second, info[:, lat + 3 : lat + 4], 0.0)
    )
    slot = lax.broadcasted_iota(jnp.int32, (span, columns), 1).astype(F32)
    for k in range(n):
        pick_ref[k] = one_hot(slot == rank[:, k : k + 1])


def make_table(place, frames, out_w_t, ids_t, gates_t, neighbours, n, capacity):
    span = frames.shape[0] + 4 * EDGE
    lat = out_w_t.shape[0]
    links = tuple(neighbours)
    return pl.pallas_call(
        functools.partial(table_kernel, links),
        out_shape=[
            jax.ShapeDtypeStruct((n, span, capacity + 2 * EDGE_ROWS), BF16),
            jax.ShapeDtypeStruct((span, 128), F32),
            jax.ShapeDtypeStruct((span, lat), F32),
        ],
        in_specs=[pl.BlockSpec(memory_space=pltpu.SMEM)] + [whole()] * (4 + len(links)),
        out_specs=[whole()] * 3,
        compiler_params=params(16),
        cost_estimate=FREE,
    )(place, frames, out_w_t, ids_t, gates_t, *[neighbours[k] for k in links])


def expert_rows(rows, up_ref, folded_ref):
    hid = up_ref.shape[1]
    block = 256 if hid % 256 == 0 else hid
    total = None
    for at in range(0, hid, block):
        v = jnp.dot(rows, up_ref[:, at : at + block], preferred_element_type=F32)
        inner = v * (0.7978845608 + (0.7978845608 * 0.044715) * (v * v))
        hidden = (0.5 * v * (1.0 + jnp.tanh(inner))).astype(BF16)
        part = jnp.dot(hidden, folded_ref[at : at + block, :], preferred_element_type=F32)
        total = part if total is None else total + part
    lat = folded_ref.shape[1] // 2
    value = total[:, :lat] + total[:, lat:]
    high = value.astype(BF16)
    low = (value - high.astype(F32)).astype(BF16)
    return jnp.concatenate([high, low], axis=1)


def write_returns(n, me, held, first, outs):
    capacity = held.shape[1]
    half = n // 2
    for j, ref in enumerate(outs):
        k = first + j
        to = me ^ k
        place = to % half
        left = me ^ jnp.where(place > 0, to - 1, to)
        right = me ^ jnp.where(place < half - 1, to + 1, to)
        ref[0:capacity] = held[k]
        ref[capacity : capacity + EDGE_ROWS] = held[left, 0:EDGE_ROWS]
        ref[capacity + EDGE_ROWS :] = held[right, 0:EDGE_ROWS]


def group_kernel(n, far, place_ref, local_ref, *refs):
    quarter, half = n // 4, n // 2
    chunk_refs = refs[: half - 1 + far]
    up_ref, folded_ref = refs[half - 1 + far : half + 1 + far]
    outs, held = refs[half + 1 + far : -1], refs[-1]
    capacity = local_ref.shape[0]
    me = place_ref[0]
    chunks = [ref[...] for ref in chunk_refs]
    if far:
        is_inner = (me >= quarter) & (me < 3 * quarter)
        chunks[quarter] = jnp.where(is_inner, local_ref[...], chunks[quarter])
    else:
        chunks = [local_ref[...]] + [chunk[:capacity] for chunk in chunks]
    both = expert_rows(jnp.concatenate(chunks, axis=0), up_ref, folded_ref)
    first = half if far else 0
    for j in range(half):
        held[first + j] = both[j * capacity : (j + 1) * capacity]
    write_returns(n, me, held, first, outs)


def run_group(n, far, place, local_chunk, chunks, up, folded):
    capacity = local_chunk.shape[0]
    lanes = folded.shape[1]
    return pl.pallas_call(
        functools.partial(group_kernel, n, far),
        out_shape=[jax.ShapeDtypeStruct((capacity + 2 * EDGE_ROWS, lanes), BF16)] * (n // 2),
        in_specs=[pl.BlockSpec(memory_space=pltpu.SMEM)] + [whole()] * (len(chunks) + 3),
        out_specs=[whole()] * (n // 2),
        scratch_shapes=[pltpu.VMEM((n, capacity, lanes), BF16)],
        compiler_params=params(24),
        cost_estimate=FREE,
    )(place, local_chunk, *chunks, up, folded)


def combine_kernel(n, place_ref, *refs):
    part_refs = refs[:n]
    pick_ref, scale_ref, base_ref, low_ref, middle_ref = refs[n:]
    span, lat = base_ref.shape
    latent = base_ref[...]
    for k in range(n):
        picked = jnp.dot(pick_ref[k], part_refs[k][...], preferred_element_type=F32)
        latent = latent + scale_ref[:, k : k + 1] * (picked[:, :lat] + picked[:, lat:])
    low = latent.astype(BF16)
    low_ref[...] = low
    middle_ref[...] = jnp.where(
        place_ref[0] >= place_ref[1] // 2, low[:EDGE_ROWS], low[span - EDGE_ROWS :]
    )


def combine(place, parts, pick, scale, base):
    n = len(parts)
    return pl.pallas_call(
        functools.partial(combine_kernel, n),
        out_shape=[
            jax.ShapeDtypeStruct(base.shape, BF16),
            jax.ShapeDtypeStruct((EDGE_ROWS, base.shape[1]), BF16),
        ],
        in_specs=[pl.BlockSpec(memory_space=pltpu.SMEM)] + [whole()] * (n + 3),
        out_specs=[whole()] * 2,
        compiler_params=params(16),
        cost_estimate=FREE,
    )(place, *parts, pick, scale, base)


def snake(v, turns_row, inverse_row):
    turns = v * turns_row
    part = turns - ((turns + ROUNDER) - ROUNDER)
    s = part * part
    poly = SIN2[-1]
    for c in SIN2[-2::-1]:
        poly = poly * s + c
    return v + (poly * s) * inverse_row


def decoder_kernel(segs, place_ref, *refs):
    lat_refs = refs[:segs]
    conv_ref, alpha_ref, up_hbm, out_ref = refs[segs : segs + 4]
    padded, windows, act, up_ref, rows_out, sems, up_sem = refs[segs + 4 :]
    span, channels = act.shape[1:]
    length = span - 16
    width = up_ref.shape[2]
    lat = lat_refs[0].shape[1]
    taps = conv_ref.shape[0] // lat
    block = 256
    own = place_ref[0]
    is_first = place_ref[1] == 0
    is_last = place_ref[1] == place_ref[2] - 1
    up_copy = pltpu.make_async_copy(up_hbm, up_ref, up_sem)
    up_copy.start()

    def out_copy(k):
        return pltpu.make_async_copy(rows_out.at[k], out_ref.at[own ^ k], sems.at[k])

    row = lax.broadcasted_iota(jnp.int32, (16, taps * lat), 0)
    edge_row = lax.broadcasted_iota(jnp.int32, (16, block), 0)
    gone = ((edge_row == 0) & is_first) | ((edge_row == 1) & is_last)
    for k in range(segs):
        slab = lat_refs[k][...].astype(F32)
        middle = slab[span:]
        padded[...] = slab[:span]
        before = jnp.where(place_ref[1] == place_ref[2] // 2, middle[:EDGE], slab[:EDGE])
        end = length + EDGE
        after = jnp.where(
            place_ref[1] == place_ref[2] // 2 - 1, middle[EDGE : 2 * EDGE], slab[end : end + EDGE]
        )
        padded[0:EDGE] = before
        padded[end : end + EDGE] = after

        def window(start, rows):
            return jnp.concatenate([padded[start + j : start + j + rows] for j in range(taps)], axis=1)

        windows[k, 0:length] = window(1, length).astype(BF16)
        edges = jnp.where(row == 0, window(0, 1), jnp.where(row == 1, window(length + 1, 1), 0.0))
        windows[k, length:] = edges.astype(BF16)
        for at in range(0, channels, block):
            cols = slice(at, at + block)
            v = jnp.dot(windows[k], conv_ref[:, cols], preferred_element_type=F32)
            value = snake(v, alpha_ref[0:1, cols], alpha_ref[1:2, cols])
            act[k, 0:length, cols] = value[:length].astype(BF16)
            act[k, length:, cols] = jnp.where(gone, 0.0, value[length:]).astype(BF16)
    up_copy.wait()
    for k in range(segs):
        for r in range(0, 8, 2):
            far = r + 12 if r < 4 else r - 4
            near_w = jnp.concatenate([up_ref[r + 4], up_ref[r + 5]], axis=1)
            far_w = jnp.concatenate([up_ref[far], up_ref[far + 1]], axis=1)
            near = jnp.dot(act[k, 0:length], near_w, preferred_element_type=F32)
            side = jnp.dot(act[k], far_w, preferred_element_type=F32)
            if r < 4:
                moved = [side[length : length + 1], side[: length - 1]]
            else:
                moved = [side[1:length], side[length + 1 : length + 2]]
            res = near + jnp.concatenate(moved, axis=0)
            rows_out[k, pl.ds(r, length, stride=8), :] = res[:, :width]
            rows_out[k, pl.ds(r + 1, length, stride=8), :] = res[:, width:]
        out_copy(k).start()
    for k in range(segs):
        out_copy(k).wait()


def decode(place, slabs, conv, alpha, first_up):
    segs = len(slabs)
    length = slabs[0].shape[0] - 4 * EDGE - EDGE_ROWS
    channels = conv.shape[1]
    width = first_up.shape[2]
    lat = slabs[0].shape[1]
    return pl.pallas_call(
        functools.partial(decoder_kernel, segs),
        out_shape=jax.ShapeDtypeStruct((segs, 8 * length, width), F32),
        in_specs=[pl.BlockSpec(memory_space=pltpu.SMEM)]
        + [whole()] * (segs + 2)
        + [pl.BlockSpec(memory_space=pl.ANY)],
        out_specs=pl.BlockSpec(memory_space=pl.ANY),
        scratch_shapes=[
            pltpu.VMEM((length + 16, lat), F32),
            pltpu.VMEM((segs, length + 16, conv.shape[0]), BF16),
            pltpu.VMEM((segs, length + 16, channels), BF16),
            pltpu.VMEM(first_up.shape, BF16),
            pltpu.VMEM((segs, 8 * length, width), F32),
            pltpu.SemaphoreType.DMA((segs,)),
            pltpu.SemaphoreType.DMA,
        ],
        compiler_params=params(52),
        cost_estimate=FREE,
    )(place, *slabs, conv, alpha, first_up)


def local(
    frames,
    expert_ids,
    gate_weights,
    up_weight,
    down_weight,
    out_weight,
    in_conv,
    snake_first,
    first_up,
):
    rows, _ = frames.shape
    n = lax.axis_size("expert")
    segs = lax.axis_size("seg")
    quarter, half = n // 4, n // 2
    capacity = -(-(3 * rows // n) // 16) * 16
    me = lax.axis_index("expert")
    place = jnp.stack([me, jnp.int32(n)]).astype(jnp.int32)
    inner = range(quarter, 3 * quarter)
    across_by = 3 * quarter
    is_inner = ((me >= quarter) & (me < across_by)).astype(jnp.int32)

    def swap(value, k, members=range(n)):
        return lax.ppermute(value, "expert", [(i, i ^ k) for i in members])

    across = swap(frames, across_by, inner)
    ids_t = expert_ids.T
    across_ids = swap(ids_t, across_by, inner)
    own = jnp.stack([me, 0]).astype(jnp.int32)
    gates_t, out_w_t = gate_weights.T, out_weight.T
    chunks = make_slots(own, range(half), (ids_t, frames, gates_t), capacity)
    near = [swap(chunks[k], k) for k in range(1, half)]
    folded = fold_weights(down_weight[0], out_w_t)
    origin = jnp.stack([me ^ (is_inner * across_by), is_inner]).astype(jnp.int32)
    origin, folded = lax.optimization_barrier((origin, folded))
    sent = make_slots(
        origin, range(half, n), (ids_t, frames, across_ids, across), capacity
    )
    far = []
    for k, value in zip(range(half, n), sent):
        pairs = [(i, i ^ (k ^ across_by if i in inner else k)) for i in range(n)]
        far.append(lax.ppermute(value, "expert", [(i, j) for i, j in pairs if i != j]))
    up = up_weight[0]
    gates_t, chunk, _ = lax.optimization_barrier((gates_t, chunks[0], sent))
    neighbours = {k: near[k - 1] for k in range(1, half) if is_neighbour(k)}
    pick, scale, base = make_table(
        place, frames, out_w_t, ids_t, gates_t, neighbours, n, capacity
    )
    back = run_group(n, False, place, chunk, near, up, folded)
    parts = [back[0]] + [swap(back[k], k) for k in range(1, half)]
    place, pick, scale, base = lax.optimization_barrier((place, pick, scale, base))
    back = run_group(n, True, place, sent[quarter], far, up, folded)
    parts += [swap(back[k], half + k) for k in range(half)]
    slab, middle = combine(place, parts, pick, scale, base)
    middle = lax.ppermute(middle, "expert", [(half - 1, half), (half, half - 1)])
    slab = jnp.concatenate([slab, middle], axis=0)

    slabs = [slab] + [
        lax.ppermute(slab, "seg", [(i, i ^ k) for i in range(segs)]) for k in range(1, segs)
    ]
    spot = jnp.stack([lax.axis_index("seg"), me, jnp.int32(n)]).astype(jnp.int32)
    alpha = jnp.stack([snake_first * (1.0 / math.pi), 1.0 / snake_first])
    conv = in_conv.reshape(-1, in_conv.shape[2])
    return decode(spot, slabs, conv, alpha, first_up)


def solution(mesh):
    placed = (
        P(("seg", "expert"), None),
        P(("seg", "expert"), None),
        P(("seg", "expert"), None),
        P("expert", None, None),
        P("expert", None, None),
        P(),
        P(),
        P(),
        P(None, None, "seg"),
    )
    return jax.shard_map(
        local, mesh=mesh, in_specs=placed, out_specs=P(None, "expert", "seg"), check_vma=False
    )
```

```python
import functools
import math

import jax
import jax.numpy as jnp
from jax import lax
from jax.experimental import pallas as pl
from jax.experimental.pallas import tpu as pltpu
from jax.sharding import PartitionSpec as P

F32 = jnp.float32
BF16 = jnp.bfloat16
VMEM = pltpu.VMEM
SIN2 = (
    9.869603157043457,
    -32.469581604003906,
    42.72538375854492,
    -30.085954666137695,
    12.99073314666748,
    -3.2729504108428955,
)
ROUNDER = 12582912.0


FREE = pl.CostEstimate(flops=0, bytes_accessed=0, transcendentals=0)


def whole():
    return pl.BlockSpec(memory_space=VMEM)


def params(mib):
    return pltpu.CompilerParams(vmem_limit_bytes=mib * 1024 * 1024)


EDGE = 4
EDGE_ROWS = 16


def token_key(token, rows):
    rest = jnp.where(token >= rows - EDGE, token - (rows - 2 * EDGE), token + EDGE)
    return jnp.where(token < EDGE, token, rest)


def one_hot(mask):
    return mask.astype(F32).astype(BF16)


def is_neighbour(k):
    return k & (k + 1) == 0 and k > 0


def edge_rows(frames, ids, gates):
    rows, width = frames.shape
    parts = []
    for choice in range(2):
        rest = gates[choice : choice + 1]
        for _ in range(3):
            part = rest.astype(BF16).astype(F32)
            parts.append(part)
            rest = rest - part
    meta = jnp.concatenate([ids.astype(F32)] + parts, axis=0)
    meta = jnp.concatenate([meta, jnp.zeros((8, width - rows), F32)], axis=1)
    ends = [frames[:16].astype(F32)[:EDGE], frames[rows - 16 :].astype(F32)[16 - EDGE :]]
    return jnp.concatenate(ends + [meta], axis=0).astype(BF16)


def slots_kernel(steps, origin_ref, *refs):
    sources, out_refs = refs[: -len(steps)], refs[-len(steps) :]
    ids, frames = sources[0][...], sources[1][...]
    if len(sources) == 3:
        capacity = out_refs[0].shape[0]
        extra = edge_rows(frames, ids, sources[2][...])
        for k, ref in zip(steps, out_refs):
            if is_neighbour(k):
                ref[capacity:] = extra
    else:
        second = origin_ref[1] == 1
        ids = jnp.where(second, sources[2][...], ids)
        frames = jnp.where(second, sources[3][...], frames)
    rows = frames.shape[0]
    capacity = out_refs[0].shape[0]
    ids = ids ^ origin_ref[0]
    count = -(-len(steps) // 16) * 16
    step = lax.broadcasted_iota(jnp.int32, (count, rows), 0) + steps[0]
    named = (ids[0:1] == step) | (ids[1:2] == step)
    earlier = token_key(lax.broadcasted_iota(jnp.int32, (rows, rows), 0), rows) < token_key(
        lax.broadcasted_iota(jnp.int32, (rows, rows), 1), rows
    )
    rank = jnp.dot(one_hot(named), one_hot(earlier), preferred_element_type=F32)
    rank = jnp.where(named, rank, -1.0)
    slot = lax.broadcasted_iota(jnp.int32, (capacity, rows), 0).astype(F32)
    for j, ref in enumerate(out_refs):
        pick = one_hot(slot == rank[j : j + 1])
        ref[0:capacity] = jnp.dot(pick, frames, preferred_element_type=F32).astype(BF16)


def make_slots(origin, steps, sources, capacity):
    width = sources[1].shape[1]
    return pl.pallas_call(
        functools.partial(slots_kernel, steps),
        out_shape=[
            jax.ShapeDtypeStruct(
                (capacity + EDGE_ROWS * (len(sources) == 3 and is_neighbour(k)), width), BF16
            )
            for k in steps
        ],
        in_specs=[pl.BlockSpec(memory_space=pltpu.SMEM)] + [whole()] * len(sources),
        out_specs=[whole()] * len(steps),
        compiler_params=params(24),
        cost_estimate=FREE,
    )(origin, *sources)


def fold_kernel(down_ref, out_w_ref, folded_ref):
    full = lax.dot_general(
        down_ref[...], out_w_ref[...], (((1,), (1,)), ((), ())), preferred_element_type=F32
    )
    high = full.astype(BF16)
    low = (full - high.astype(F32)).astype(BF16)
    folded_ref[...] = jnp.concatenate([high, low], axis=1)


def fold_weights(down, out_w_t):
    hid, width = down.shape
    lat = out_w_t.shape[0]
    block = 512 if hid % 512 == 0 else hid
    return pl.pallas_call(
        fold_kernel,
        grid=(hid // block,),
        out_shape=jax.ShapeDtypeStruct((hid, 2 * lat), BF16),
        in_specs=[
            pl.BlockSpec((block, width), lambda i: (i, 0)),
            pl.BlockSpec((lat, width), lambda i: (0, 0)),
        ],
        out_specs=pl.BlockSpec((block, 2 * lat), lambda i: (i, 0)),
        compiler_params=params(16),
        cost_estimate=FREE,
    )(down, out_w_t)


def table_kernel(
    links, place_ref, frames_ref, out_w_ref, ids_ref, gates_ref, *refs
):
    link_refs = refs[: len(links)]
    pick_ref, scale_ref, base_ref = refs[len(links) :]
    n, span, columns = pick_ref.shape
    rows, width = frames_ref.shape
    lat = out_w_ref.shape[0]
    capacity = columns - 2 * EDGE_ROWS
    me, size = place_ref[0], place_ref[1]

    def rows_of(frames, lines):
        base = lax.dot_general(
            frames, out_w_ref[...], (((1,), (1,)), ((), ())), preferred_element_type=F32
        )
        lines = jnp.concatenate([lines, jnp.zeros((128 - lines.shape[0], rows), F32)], axis=0)
        return base, jnp.transpose(lines)[:, : 128 - lat]

    def neighbour(other):
        extra = link_refs[0][capacity:]
        for k, ref in zip(links[1:], link_refs[1:]):
            extra = jnp.where((me ^ other) == k, ref[capacity:], extra)
        meta = extra[:, :rows].astype(F32)[2 * EDGE :]
        gates = [meta[j : j + 1] + meta[j + 1 : j + 2] + meta[j + 2 : j + 3] for j in (2, 5)]
        base, lines = rows_of(extra, jnp.concatenate([meta[:2]] + gates, axis=0))
        return jnp.concatenate(
            [
                jnp.concatenate([base[:EDGE], lines[:EDGE]], axis=1),
                jnp.concatenate([base[EDGE : 2 * EDGE], lines[rows - EDGE :]], axis=1),
            ],
            axis=0,
        )

    left, right = neighbour(me - 1), neighbour(me + 1)
    own = rows_of(
        frames_ref[...], jnp.concatenate([ids_ref[...].astype(F32), gates_ref[...]], axis=0)
    )
    info = jnp.concatenate(
        [
            left[EDGE:],
            jnp.concatenate(own, axis=1),
            right[:EDGE],
            left[:EDGE],
            jnp.zeros((EDGE, 128), F32),
        ],
        axis=0,
    )
    def code(i):
        own = 1024 + token_key(i - EDGE, rows)
        late = jnp.where(i < rows + 3 * EDGE, i - rows - 2 * EDGE, 3072)
        tail = jnp.where(i < rows + 2 * EDGE, 2048 + i - rows - EDGE, late)
        return jnp.where(i < EDGE, i + EDGE, jnp.where(i < rows + EDGE, own, tail))

    line = lax.broadcasted_iota(jnp.int32, (span, 1), 0)
    line_code = code(line)
    other = code(lax.broadcasted_iota(jnp.int32, (1, span), 1))
    earlier = (other < line_code) & (other >= (line_code >> 10) * 1024)
    before = line_code < 1024
    after = (line_code >= 2048) & (line_code < 3072)
    lost = (before & ((me == 0) | (me == size // 2))) | (
        after & ((me == size - 1) | (me == size // 2 - 1))
    )
    base_ref[...] = jnp.where(lost, 0.0, info[:, :lat])
    ids = info[:, lat : lat + 2].astype(jnp.int32) ^ me
    ids = jnp.where(lost | (line_code >= 3072), -1, ids)
    step = lax.broadcasted_iota(jnp.int32, (span, 128), 1)
    first = ids[:, 0:1] == step
    second = ids[:, 1:2] == step
    named = first | second
    rank = jnp.dot(one_hot(earlier), one_hot(named), preferred_element_type=F32)
    rank = rank + jnp.where(before, capacity, jnp.where(after, capacity + EDGE_ROWS, 0)).astype(F32)
    rank = jnp.where(named, rank, -1.0)
    scale_ref[...] = jnp.where(
        first, info[:, lat + 2 : lat + 3], jnp.where(second, info[:, lat + 3 : lat + 4], 0.0)
    )
    slot = lax.broadcasted_iota(jnp.int32, (span, columns), 1).astype(F32)
    for k in range(n):
        pick_ref[k] = one_hot(slot == rank[:, k : k + 1])


def make_table(place, frames, out_w_t, ids_t, gates_t, neighbours, n, capacity):
    span = frames.shape[0] + 4 * EDGE
    lat = out_w_t.shape[0]
    links = tuple(neighbours)
    return pl.pallas_call(
        functools.partial(table_kernel, links),
        out_shape=[
            jax.ShapeDtypeStruct((n, span, capacity + 2 * EDGE_ROWS), BF16),
            jax.ShapeDtypeStruct((span, 128), F32),
            jax.ShapeDtypeStruct((span, lat), F32),
        ],
        in_specs=[pl.BlockSpec(memory_space=pltpu.SMEM)] + [whole()] * (4 + len(links)),
        out_specs=[whole()] * 3,
        compiler_params=params(16),
        cost_estimate=FREE,
    )(place, frames, out_w_t, ids_t, gates_t, *[neighbours[k] for k in links])


def expert_rows(rows, up_ref, folded_ref):
    hid = up_ref.shape[1]
    block = 256 if hid % 256 == 0 else hid
    total = None
    for at in range(0, hid, block):
        v = jnp.dot(rows, up_ref[:, at : at + block], preferred_element_type=F32)
        inner = v * (0.7978845608 + (0.7978845608 * 0.044715) * (v * v))
        hidden = (0.5 * v * (1.0 + jnp.tanh(inner))).astype(BF16)
        part = jnp.dot(hidden, folded_ref[at : at + block, :], preferred_element_type=F32)
        total = part if total is None else total + part
    lat = folded_ref.shape[1] // 2
    value = total[:, :lat] + total[:, lat:]
    high = value.astype(BF16)
    low = (value - high.astype(F32)).astype(BF16)
    return jnp.concatenate([high, low], axis=1)


def write_returns(n, me, held, first, outs):
    capacity = held.shape[1]
    half = n // 2
    for j, ref in enumerate(outs):
        k = first + j
        to = me ^ k
        place = to % half
        left = me ^ jnp.where(place > 0, to - 1, to)
        right = me ^ jnp.where(place < half - 1, to + 1, to)
        ref[0:capacity] = held[k]
        ref[capacity : capacity + EDGE_ROWS] = held[left, 0:EDGE_ROWS]
        ref[capacity + EDGE_ROWS :] = held[right, 0:EDGE_ROWS]


def group_kernel(n, far, place_ref, local_ref, *refs):
    quarter, half = n // 4, n // 2
    chunk_refs = refs[: half - 1 + far]
    up_ref, folded_ref = refs[half - 1 + far : half + 1 + far]
    outs, held = refs[half + 1 + far : -1], refs[-1]
    capacity = local_ref.shape[0]
    me = place_ref[0]
    chunks = [ref[...] for ref in chunk_refs]
    if far:
        is_inner = (me >= quarter) & (me < 3 * quarter)
        chunks[quarter] = jnp.where(is_inner, local_ref[...], chunks[quarter])
    else:
        chunks = [local_ref[...]] + [chunk[:capacity] for chunk in chunks]
    both = expert_rows(jnp.concatenate(chunks, axis=0), up_ref, folded_ref)
    first = half if far else 0
    for j in range(half):
        held[first + j] = both[j * capacity : (j + 1) * capacity]
    write_returns(n, me, held, first, outs)


def run_group(n, far, place, local_chunk, chunks, up, folded):
    capacity = local_chunk.shape[0]
    lanes = folded.shape[1]
    return pl.pallas_call(
        functools.partial(group_kernel, n, far),
        out_shape=[jax.ShapeDtypeStruct((capacity + 2 * EDGE_ROWS, lanes), BF16)] * (n // 2),
        in_specs=[pl.BlockSpec(memory_space=pltpu.SMEM)] + [whole()] * (len(chunks) + 3),
        out_specs=[whole()] * (n // 2),
        scratch_shapes=[pltpu.VMEM((n, capacity, lanes), BF16)],
        compiler_params=params(24),
        cost_estimate=FREE,
    )(place, local_chunk, *chunks, up, folded)


def combine_kernel(n, place_ref, *refs):
    part_refs = refs[:n]
    pick_ref, scale_ref, base_ref, low_ref, middle_ref = refs[n:]
    span, lat = base_ref.shape
    latent = base_ref[...]
    for k in range(n):
        picked = jnp.dot(pick_ref[k], part_refs[k][...], preferred_element_type=F32)
        latent = latent + scale_ref[:, k : k + 1] * (picked[:, :lat] + picked[:, lat:])
    low = latent.astype(BF16)
    low_ref[...] = low
    middle_ref[...] = jnp.where(
        place_ref[0] >= place_ref[1] // 2, low[:EDGE_ROWS], low[span - EDGE_ROWS :]
    )


def combine(place, parts, pick, scale, base):
    n = len(parts)
    return pl.pallas_call(
        functools.partial(combine_kernel, n),
        out_shape=[
            jax.ShapeDtypeStruct(base.shape, BF16),
            jax.ShapeDtypeStruct((EDGE_ROWS, base.shape[1]), BF16),
        ],
        in_specs=[pl.BlockSpec(memory_space=pltpu.SMEM)] + [whole()] * (n + 3),
        out_specs=[whole()] * 2,
        compiler_params=params(16),
        cost_estimate=FREE,
    )(place, *parts, pick, scale, base)


def snake(v, turns_row, inverse_row):
    turns = v * turns_row
    part = turns - ((turns + ROUNDER) - ROUNDER)
    s = part * part
    poly = SIN2[-1]
    for c in SIN2[-2::-1]:
        poly = poly * s + c
    return v + (poly * s) * inverse_row


def decoder_kernel(segs, place_ref, *refs):
    lat_refs = refs[:segs]
    conv_ref, alpha_ref, up_hbm, out_ref = refs[segs : segs + 4]
    padded, windows, act, up_ref, rows_out, sems, up_sem = refs[segs + 4 :]
    span, channels = act.shape[1:]
    length = span - 16
    width = up_ref.shape[2]
    lat = lat_refs[0].shape[1]
    taps = conv_ref.shape[0] // lat
    block = 256
    own = place_ref[0]
    is_first = place_ref[1] == 0
    is_last = place_ref[1] == place_ref[2] - 1
    up_copy = pltpu.make_async_copy(up_hbm, up_ref, up_sem)
    up_copy.start()

    def out_copy(k):
        return pltpu.make_async_copy(rows_out.at[k], out_ref.at[own ^ k], sems.at[k])

    row = lax.broadcasted_iota(jnp.int32, (16, taps * lat), 0)
    edge_row = lax.broadcasted_iota(jnp.int32, (16, block), 0)
    gone = ((edge_row == 0) & is_first) | ((edge_row == 1) & is_last)
    for k in range(segs):
        padded[k] = lat_refs[k][0:span].astype(F32)
    end = length + EDGE

    @pl.when(place_ref[1] == place_ref[2] // 2)
    def _():
        for k in range(segs):
            padded[k, 0:EDGE] = lat_refs[k][span:].astype(F32)[:EDGE]

    @pl.when(place_ref[1] == place_ref[2] // 2 - 1)
    def _():
        for k in range(segs):
            padded[k, end : end + EDGE] = lat_refs[k][span:].astype(F32)[EDGE : 2 * EDGE]

    for k in range(segs):

        def window(start, rows):
            parts = [padded[k, start + j : start + j + rows] for j in range(taps)]
            return jnp.concatenate(parts, axis=1)

        windows[k, 0:length] = window(1, length).astype(BF16)
        edges = jnp.where(row == 0, window(0, 1), jnp.where(row == 1, window(length + 1, 1), 0.0))
        windows[k, length:] = edges.astype(BF16)
        for at in range(0, channels, block):
            cols = slice(at, at + block)
            v = jnp.dot(windows[k], conv_ref[:, cols], preferred_element_type=F32)
            value = snake(v, alpha_ref[0:1, cols], alpha_ref[1:2, cols])
            act[k, 0:length, cols] = value[:length].astype(BF16)
            act[k, length:, cols] = jnp.where(gone, 0.0, value[length:]).astype(BF16)
    up_copy.wait()
    for k in range(segs):
        for r in range(0, 8, 2):
            far = r + 12 if r < 4 else r - 4
            near_w = jnp.concatenate([up_ref[r + 4], up_ref[r + 5]], axis=1)
            far_w = jnp.concatenate([up_ref[far], up_ref[far + 1]], axis=1)
            near = jnp.dot(act[k, 0:length], near_w, preferred_element_type=F32)
            side = jnp.dot(act[k], far_w, preferred_element_type=F32)
            if r < 4:
                moved = [side[length : length + 1], side[: length - 1]]
            else:
                moved = [side[1:length], side[length + 1 : length + 2]]
            res = near + jnp.concatenate(moved, axis=0)
            rows_out[k, pl.ds(r, length, stride=8), :] = res[:, :width]
            rows_out[k, pl.ds(r + 1, length, stride=8), :] = res[:, width:]
        out_copy(k).start()
    for k in range(segs):
        out_copy(k).wait()


def decode(place, slabs, conv, alpha, first_up):
    segs = len(slabs)
    length = slabs[0].shape[0] - 4 * EDGE - EDGE_ROWS
    channels = conv.shape[1]
    width = first_up.shape[2]
    lat = slabs[0].shape[1]
    return pl.pallas_call(
        functools.partial(decoder_kernel, segs),
        out_shape=jax.ShapeDtypeStruct((segs, 8 * length, width), F32),
        in_specs=[pl.BlockSpec(memory_space=pltpu.SMEM)]
        + [whole()] * (segs + 2)
        + [pl.BlockSpec(memory_space=pl.ANY)],
        out_specs=pl.BlockSpec(memory_space=pl.ANY),
        scratch_shapes=[
            pltpu.VMEM((segs, length + 16, lat), F32),
            pltpu.VMEM((segs, length + 16, conv.shape[0]), BF16),
            pltpu.VMEM((segs, length + 16, channels), BF16),
            pltpu.VMEM(first_up.shape, BF16),
            pltpu.VMEM((segs, 8 * length, width), F32),
            pltpu.SemaphoreType.DMA((segs,)),
            pltpu.SemaphoreType.DMA,
        ],
        compiler_params=params(52),
        cost_estimate=FREE,
    )(place, *slabs, conv, alpha, first_up)


def local(
    frames,
    expert_ids,
    gate_weights,
    up_weight,
    down_weight,
    out_weight,
    in_conv,
    snake_first,
    first_up,
):
    rows, _ = frames.shape
    n = lax.axis_size("expert")
    segs = lax.axis_size("seg")
    quarter, half = n // 4, n // 2
    capacity = -(-(3 * rows // n) // 16) * 16
    me = lax.axis_index("expert")
    place = jnp.stack([me, jnp.int32(n)]).astype(jnp.int32)
    inner = range(quarter, 3 * quarter)
    across_by = 3 * quarter
    is_inner = ((me >= quarter) & (me < across_by)).astype(jnp.int32)

    def swap(value, k, members=range(n)):
        return lax.ppermute(value, "expert", [(i, i ^ k) for i in members])

    across = swap(frames, across_by, inner)
    ids_t = expert_ids.T
    across_ids = swap(ids_t, across_by, inner)
    own = jnp.stack([me, 0]).astype(jnp.int32)
    gates_t, out_w_t = gate_weights.T, out_weight.T
    chunks = make_slots(own, range(half), (ids_t, frames, gates_t), capacity)
    near = [swap(chunks[k], k) for k in range(1, half)]
    origin = jnp.stack([me ^ (is_inner * across_by), is_inner]).astype(jnp.int32)
    sent = make_slots(
        origin, range(half, n), (ids_t, frames, across_ids, across), capacity
    )

    def cross(value, k):
        pairs = [(i, i ^ (k ^ across_by if i in inner else k)) for i in range(n)]
        return lax.ppermute(value, "expert", [(i, j) for i, j in pairs if i != j])

    far = [cross(sent[k - half], k) for k in range(across_by, n)]
    late, near = lax.optimization_barrier((sent[:quarter], near))
    far = [cross(late[k - half], k) for k in range(half, across_by)] + far
    up = up_weight[0]
    gates_t, chunk, down, late = lax.optimization_barrier(
        (gates_t, chunks[0], down_weight[0], late)
    )
    folded = fold_weights(down, out_w_t)
    neighbours = {k: near[k - 1] for k in range(1, half) if is_neighbour(k)}
    pick, scale, base = make_table(
        place, frames, out_w_t, ids_t, gates_t, neighbours, n, capacity
    )
    back = run_group(n, False, place, chunk, near, up, folded)
    parts = [back[0]] + [swap(back[k], k) for k in range(1, half)]
    place, pick, scale, base = lax.optimization_barrier((place, pick, scale, base))
    back = run_group(n, True, place, sent[quarter], far, up, folded)
    parts += [swap(back[k], half + k) for k in range(half)]
    slab, middle = combine(place, parts, pick, scale, base)
    middle = lax.ppermute(middle, "expert", [(half - 1, half), (half, half - 1)])
    slab = jnp.concatenate([slab, middle], axis=0)

    slabs = [slab] + [
        lax.ppermute(slab, "seg", [(i, i ^ k) for i in range(segs)]) for k in range(1, segs)
    ]
    spot = jnp.stack([lax.axis_index("seg"), me, jnp.int32(n)]).astype(jnp.int32)
    alpha = jnp.stack([snake_first * (1.0 / math.pi), 1.0 / snake_first])
    conv = in_conv.reshape(-1, in_conv.shape[2])
    return decode(spot, slabs, conv, alpha, first_up)


def solution(mesh):
    placed = (
        P(("seg", "expert"), None),
        P(("seg", "expert"), None),
        P(("seg", "expert"), None),
        P("expert", None, None),
        P("expert", None, None),
        P(),
        P(),
        P(),
        P(None, None, "seg"),
    )
    return jax.shard_map(
        local, mesh=mesh, in_specs=placed, out_specs=P(None, "expert", "seg"), check_vma=False
    )
```

```python
import functools
import math

import jax
import jax.numpy as jnp
from jax import lax
from jax.experimental import pallas as pl
from jax.experimental.pallas import tpu as pltpu
from jax.sharding import PartitionSpec as P

F32 = jnp.float32
BF16 = jnp.bfloat16
VMEM = pltpu.VMEM
SIN2 = (
    9.869603157043457,
    -32.469581604003906,
    42.72538375854492,
    -30.085954666137695,
    12.99073314666748,
    -3.2729504108428955,
)
ROUNDER = 12582912.0


FREE = pl.CostEstimate(flops=0, bytes_accessed=0, transcendentals=0)


def whole():
    return pl.BlockSpec(memory_space=VMEM)


def params(mib):
    return pltpu.CompilerParams(vmem_limit_bytes=mib * 1024 * 1024)


EDGE = 4
EDGE_ROWS = 16


def token_key(token, rows):
    rest = jnp.where(token >= rows - EDGE, token - (rows - 2 * EDGE), token + EDGE)
    return jnp.where(token < EDGE, token, rest)


def one_hot(mask):
    return mask.astype(F32).astype(BF16)


def is_neighbour(k):
    return k & (k + 1) == 0 and k > 0


def edge_rows(frames, ids, gates):
    rows, width = frames.shape
    parts = []
    for choice in range(2):
        rest = gates[choice : choice + 1]
        for _ in range(3):
            part = rest.astype(BF16).astype(F32)
            parts.append(part)
            rest = rest - part
    meta = jnp.concatenate([ids.astype(F32)] + parts, axis=0)
    meta = jnp.concatenate([meta, jnp.zeros((8, width - rows), F32)], axis=1)
    ends = [frames[:16].astype(F32)[:EDGE], frames[rows - 16 :].astype(F32)[16 - EDGE :]]
    return jnp.concatenate(ends + [meta], axis=0).astype(BF16)


def slots_kernel(steps, first, origin_ref, *refs):
    sources, out_refs = refs[: -len(steps)], refs[-len(steps) :]
    ids, frames = sources[0][...], sources[1][...]
    if first:
        capacity = out_refs[0].shape[0]
        extra = edge_rows(frames, ids, sources[2][...])
        for k, ref in zip(steps, out_refs):
            if is_neighbour(k):
                ref[capacity:] = extra
    else:
        second = origin_ref[1] == 1
        ids = jnp.where(second, sources[2][...], ids)
        frames = jnp.where(second, sources[3][...], frames)
    rows = frames.shape[0]
    capacity = out_refs[0].shape[0]
    ids = ids ^ origin_ref[0]
    count = -(-len(steps) // 16) * 16
    step = lax.broadcasted_iota(jnp.int32, (count, rows), 0) + steps[0]
    named = (ids[0:1] == step) | (ids[1:2] == step)
    earlier = token_key(lax.broadcasted_iota(jnp.int32, (rows, rows), 0), rows) < token_key(
        lax.broadcasted_iota(jnp.int32, (rows, rows), 1), rows
    )
    rank = jnp.dot(one_hot(named), one_hot(earlier), preferred_element_type=F32)
    rank = jnp.where(named, rank, -1.0)
    slot = lax.broadcasted_iota(jnp.int32, (capacity, rows), 0).astype(F32)
    for j, ref in enumerate(out_refs):
        pick = one_hot(slot == rank[j : j + 1])
        ref[0:capacity] = jnp.dot(pick, frames, preferred_element_type=F32).astype(BF16)


def make_slots(origin, steps, sources, capacity):
    width = sources[1].shape[1]
    first = len(sources) == 3
    heights = [capacity + EDGE_ROWS * (first and is_neighbour(k)) for k in steps]
    return pl.pallas_call(
        functools.partial(slots_kernel, steps, first),
        out_shape=[jax.ShapeDtypeStruct((height, width), BF16) for height in heights],
        in_specs=[pl.BlockSpec(memory_space=pltpu.SMEM)] + [whole()] * len(sources),
        out_specs=[whole()] * len(heights),
        compiler_params=params(24),
        cost_estimate=FREE,
    )(origin, *sources)


def fold_kernel(down_ref, out_w_ref, folded_ref):
    full = lax.dot_general(
        down_ref[...], out_w_ref[...], (((1,), (1,)), ((), ())), preferred_element_type=F32
    )
    high = full.astype(BF16)
    low = (full - high.astype(F32)).astype(BF16)
    folded_ref[...] = jnp.concatenate([high, low], axis=1)


def fold_weights(down, out_w_t):
    hid, width = down.shape
    lat = out_w_t.shape[0]
    block = 512 if hid % 512 == 0 else hid
    return pl.pallas_call(
        fold_kernel,
        grid=(hid // block,),
        out_shape=jax.ShapeDtypeStruct((hid, 2 * lat), BF16),
        in_specs=[
            pl.BlockSpec((block, width), lambda i: (i, 0)),
            pl.BlockSpec((lat, width), lambda i: (0, 0)),
        ],
        out_specs=pl.BlockSpec((block, 2 * lat), lambda i: (i, 0)),
        compiler_params=params(16),
        cost_estimate=FREE,
    )(down, out_w_t)


def table_kernel(
    links, place_ref, frames_ref, out_w_ref, ids_ref, gates_ref, *refs
):
    link_refs = refs[: len(links)]
    pick_ref, scale_ref, base_ref = refs[len(links) :]
    n, span, columns = pick_ref.shape
    rows, width = frames_ref.shape
    lat = out_w_ref.shape[0]
    capacity = columns - 2 * EDGE_ROWS
    me, size = place_ref[0], place_ref[1]

    def rows_of(frames, lines):
        base = lax.dot_general(
            frames, out_w_ref[...], (((1,), (1,)), ((), ())), preferred_element_type=F32
        )
        lines = jnp.concatenate([lines, jnp.zeros((128 - lines.shape[0], rows), F32)], axis=0)
        return base, jnp.transpose(lines)[:, : 128 - lat]

    def neighbour(other):
        extra = link_refs[0][capacity:]
        for k, ref in zip(links[1:], link_refs[1:]):
            extra = jnp.where((me ^ other) == k, ref[capacity:], extra)
        meta = extra[:, :rows].astype(F32)[2 * EDGE :]
        gates = [meta[j : j + 1] + meta[j + 1 : j + 2] + meta[j + 2 : j + 3] for j in (2, 5)]
        base, lines = rows_of(extra, jnp.concatenate([meta[:2]] + gates, axis=0))
        return jnp.concatenate(
            [
                jnp.concatenate([base[:EDGE], lines[:EDGE]], axis=1),
                jnp.concatenate([base[EDGE : 2 * EDGE], lines[rows - EDGE :]], axis=1),
            ],
            axis=0,
        )

    left, right = neighbour(me - 1), neighbour(me + 1)
    own = rows_of(
        frames_ref[...], jnp.concatenate([ids_ref[...].astype(F32), gates_ref[...]], axis=0)
    )
    info = jnp.concatenate(
        [
            left[EDGE:],
            jnp.concatenate(own, axis=1),
            right[:EDGE],
            left[:EDGE],
            jnp.zeros((EDGE, 128), F32),
        ],
        axis=0,
    )
    def code(i):
        own = 1024 + token_key(i - EDGE, rows)
        late = jnp.where(i < rows + 3 * EDGE, i - rows - 2 * EDGE, 3072)
        tail = jnp.where(i < rows + 2 * EDGE, 2048 + i - rows - EDGE, late)
        return jnp.where(i < EDGE, i + EDGE, jnp.where(i < rows + EDGE, own, tail))

    line = lax.broadcasted_iota(jnp.int32, (span, 1), 0)
    line_code = code(line)
    other = code(lax.broadcasted_iota(jnp.int32, (1, span), 1))
    earlier = (other < line_code) & (other >= (line_code >> 10) * 1024)
    before = line_code < 1024
    after = (line_code >= 2048) & (line_code < 3072)
    lost = (before & ((me == 0) | (me == size // 2))) | (
        after & ((me == size - 1) | (me == size // 2 - 1))
    )
    base_ref[...] = jnp.where(lost, 0.0, info[:, :lat])
    ids = info[:, lat : lat + 2].astype(jnp.int32) ^ me
    ids = jnp.where(lost | (line_code >= 3072), -1, ids)
    step = lax.broadcasted_iota(jnp.int32, (span, 128), 1)
    first = ids[:, 0:1] == step
    second = ids[:, 1:2] == step
    named = first | second
    rank = jnp.dot(one_hot(earlier), one_hot(named), preferred_element_type=F32)
    rank = rank + jnp.where(before, capacity, jnp.where(after, capacity + EDGE_ROWS, 0)).astype(F32)
    rank = jnp.where(named, rank, -1.0)
    scale_ref[...] = jnp.where(
        first, info[:, lat + 2 : lat + 3], jnp.where(second, info[:, lat + 3 : lat + 4], 0.0)
    )
    slot = lax.broadcasted_iota(jnp.int32, (span, columns), 1).astype(F32)
    for k in range(n):
        pick_ref[k] = one_hot(slot == rank[:, k : k + 1])


def make_table(place, frames, out_w_t, ids_t, gates_t, neighbours, n, capacity):
    span = frames.shape[0] + 4 * EDGE
    lat = out_w_t.shape[0]
    links = tuple(neighbours)
    return pl.pallas_call(
        functools.partial(table_kernel, links),
        out_shape=[
            jax.ShapeDtypeStruct((n, span, capacity + 2 * EDGE_ROWS), BF16),
            jax.ShapeDtypeStruct((span, 128), F32),
            jax.ShapeDtypeStruct((span, lat), F32),
        ],
        in_specs=[pl.BlockSpec(memory_space=pltpu.SMEM)] + [whole()] * (4 + len(links)),
        out_specs=[whole()] * 3,
        compiler_params=params(16),
        cost_estimate=FREE,
    )(place, frames, out_w_t, ids_t, gates_t, *[neighbours[k] for k in links])


def expert_rows(rows, up_ref, folded_ref):
    hid = up_ref.shape[1]
    block = 256 if hid % 256 == 0 else hid
    total = None
    for at in range(0, hid, block):
        v = jnp.dot(rows, up_ref[:, at : at + block], preferred_element_type=F32)
        inner = v * (0.7978845608 + (0.7978845608 * 0.044715) * (v * v))
        hidden = (0.5 * v * (1.0 + jnp.tanh(inner))).astype(BF16)
        part = jnp.dot(hidden, folded_ref[at : at + block, :], preferred_element_type=F32)
        total = part if total is None else total + part
    lat = folded_ref.shape[1] // 2
    value = total[:, :lat] + total[:, lat:]
    high = value.astype(BF16)
    low = (value - high.astype(F32)).astype(BF16)
    return jnp.concatenate([high, low], axis=1)


def write_returns(n, me, held, first, outs):
    capacity = held.shape[1]
    half = n // 2
    for j, ref in enumerate(outs):
        k = first + j
        to = me ^ k
        place = to % half
        left = me ^ jnp.where(place > 0, to - 1, to)
        right = me ^ jnp.where(place < half - 1, to + 1, to)
        ref[0:capacity] = held[k]
        ref[capacity : capacity + EDGE_ROWS] = held[left, 0:EDGE_ROWS]
        ref[capacity + EDGE_ROWS :] = held[right, 0:EDGE_ROWS]


def group_kernel(n, far, place_ref, local_ref, *refs):
    quarter, half = n // 4, n // 2
    chunk_refs = refs[: half - 1 + far]
    up_ref, folded_ref = refs[half - 1 + far : half + 1 + far]
    outs, held = refs[half + 1 + far : -1], refs[-1]
    capacity = local_ref.shape[0]
    me = place_ref[0]
    chunks = [ref[...] for ref in chunk_refs]
    if far:
        is_inner = (me >= quarter) & (me < 3 * quarter)
        chunks[quarter] = jnp.where(is_inner, local_ref[...], chunks[quarter])
    else:
        chunks = [local_ref[...]] + [chunk[:capacity] for chunk in chunks]
    both = expert_rows(jnp.concatenate(chunks, axis=0), up_ref, folded_ref)
    first = half if far else 0
    for j in range(half):
        held[first + j] = both[j * capacity : (j + 1) * capacity]
    write_returns(n, me, held, first, outs)


def run_group(n, far, place, local_chunk, chunks, up, folded):
    capacity = local_chunk.shape[0]
    lanes = folded.shape[1]
    return pl.pallas_call(
        functools.partial(group_kernel, n, far),
        out_shape=[jax.ShapeDtypeStruct((capacity + 2 * EDGE_ROWS, lanes), BF16)] * (n // 2),
        in_specs=[pl.BlockSpec(memory_space=pltpu.SMEM)] + [whole()] * (len(chunks) + 3),
        out_specs=[whole()] * (n // 2),
        scratch_shapes=[pltpu.VMEM((n, capacity, lanes), BF16)],
        compiler_params=params(24),
        cost_estimate=FREE,
    )(place, local_chunk, *chunks, up, folded)


def combine_kernel(n, place_ref, *refs):
    part_refs = refs[:n]
    pick_ref, scale_ref, base_ref, low_ref, middle_ref = refs[n:]
    span, lat = base_ref.shape
    total = None
    for k in range(n):
        picked = jnp.dot(pick_ref[k], part_refs[k][...], preferred_element_type=F32)
        scaled = scale_ref[:, k : k + 1] * picked
        total = scaled if total is None else total + scaled
    low = (base_ref[...] + (total[:, :lat] + total[:, lat:])).astype(BF16)
    low_ref[...] = low
    middle_ref[...] = jnp.where(
        place_ref[0] >= place_ref[1] // 2, low[:EDGE_ROWS], low[span - EDGE_ROWS :]
    )


def combine(place, parts, pick, scale, base):
    n = len(parts)
    return pl.pallas_call(
        functools.partial(combine_kernel, n),
        out_shape=[
            jax.ShapeDtypeStruct(base.shape, BF16),
            jax.ShapeDtypeStruct((EDGE_ROWS, base.shape[1]), BF16),
        ],
        in_specs=[pl.BlockSpec(memory_space=pltpu.SMEM)] + [whole()] * (n + 3),
        out_specs=[whole()] * 2,
        compiler_params=params(16),
        cost_estimate=FREE,
    )(place, *parts, pick, scale, base)


def snake(v, turns_row, inverse_row):
    turns = v * turns_row
    part = turns - ((turns + ROUNDER) - ROUNDER)
    s = part * part
    poly = SIN2[-1]
    for c in SIN2[-2::-1]:
        poly = poly * s + c
    return v + (poly * s) * inverse_row


def decoder_kernel(segs, place_ref, *refs):
    lat_refs, middle_refs = refs[:segs], refs[segs : 2 * segs]
    conv_ref, alpha_ref, up_hbm, out_ref = refs[2 * segs : 2 * segs + 4]
    padded, windows, act, up_ref, rows_out, sems, up_sem = refs[2 * segs + 4 :]
    span, channels = act.shape[1:]
    length = span - 16
    width = up_ref.shape[2]
    lat = lat_refs[0].shape[1]
    taps = conv_ref.shape[0] // lat
    block = 256
    own = place_ref[0]
    is_first = place_ref[1] == 0
    is_last = place_ref[1] == place_ref[2] - 1
    up_copy = pltpu.make_async_copy(up_hbm, up_ref, up_sem)
    up_copy.start()

    def out_copy(k):
        return pltpu.make_async_copy(rows_out.at[k], out_ref.at[own ^ k], sems.at[k])

    row = lax.broadcasted_iota(jnp.int32, (16, taps * lat), 0)
    edge_row = lax.broadcasted_iota(jnp.int32, (16, block), 0)
    gone = ((edge_row == 0) & is_first) | ((edge_row == 1) & is_last)
    for k in range(segs):
        padded[k] = lat_refs[k][...].astype(F32)
    end = length + EDGE

    @pl.when(place_ref[1] == place_ref[2] // 2)
    def _():
        for k in range(segs):
            padded[k, 0:EDGE] = middle_refs[k][...].astype(F32)[:EDGE]

    @pl.when(place_ref[1] == place_ref[2] // 2 - 1)
    def _():
        for k in range(segs):
            padded[k, end : end + EDGE] = middle_refs[k][...].astype(F32)[EDGE : 2 * EDGE]

    for k in range(segs):

        def window(start, rows):
            parts = [padded[k, start + j : start + j + rows] for j in range(taps)]
            return jnp.concatenate(parts, axis=1)

        windows[k, 0:length] = window(1, length).astype(BF16)
        edges = jnp.where(row == 0, window(0, 1), jnp.where(row == 1, window(length + 1, 1), 0.0))
        windows[k, length:] = edges.astype(BF16)
        for at in range(0, channels, block):
            cols = slice(at, at + block)
            v = jnp.dot(windows[k], conv_ref[:, cols], preferred_element_type=F32)
            value = snake(v, alpha_ref[0:1, cols], alpha_ref[1:2, cols])
            act[k, 0:length, cols] = value[:length].astype(BF16)
            act[k, length:, cols] = jnp.where(gone, 0.0, value[length:]).astype(BF16)
    up_copy.wait()
    for k in range(segs):
        for r in range(0, 8, 2):
            far = r + 12 if r < 4 else r - 4
            near_w = jnp.concatenate([up_ref[r + 4], up_ref[r + 5]], axis=1)
            far_w = jnp.concatenate([up_ref[far], up_ref[far + 1]], axis=1)
            near = jnp.dot(act[k, 0:length], near_w, preferred_element_type=F32)
            side = jnp.dot(act[k], far_w, preferred_element_type=F32)
            if r < 4:
                moved = [side[length : length + 1], side[: length - 1]]
            else:
                moved = [side[1:length], side[length + 1 : length + 2]]
            res = near + jnp.concatenate(moved, axis=0)
            rows_out[k, pl.ds(r, length, stride=8), :] = res[:, :width]
            rows_out[k, pl.ds(r + 1, length, stride=8), :] = res[:, width:]
        out_copy(k).start()
    for k in range(segs):
        out_copy(k).wait()


def decode(place, slabs, conv, alpha, first_up):
    segs = len(slabs) // 2
    length = slabs[0].shape[0] - 4 * EDGE
    channels = conv.shape[1]
    width = first_up.shape[2]
    lat = slabs[0].shape[1]
    return pl.pallas_call(
        functools.partial(decoder_kernel, segs),
        out_shape=jax.ShapeDtypeStruct((segs, 8 * length, width), F32),
        in_specs=[pl.BlockSpec(memory_space=pltpu.SMEM)]
        + [whole()] * (2 * segs + 2)
        + [pl.BlockSpec(memory_space=pl.ANY)],
        out_specs=pl.BlockSpec(memory_space=pl.ANY),
        scratch_shapes=[
            pltpu.VMEM((segs, length + 16, lat), F32),
            pltpu.VMEM((segs, length + 16, conv.shape[0]), BF16),
            pltpu.VMEM((segs, length + 16, channels), BF16),
            pltpu.VMEM(first_up.shape, BF16),
            pltpu.VMEM((segs, 8 * length, width), F32),
            pltpu.SemaphoreType.DMA((segs,)),
            pltpu.SemaphoreType.DMA,
        ],
        compiler_params=params(52),
        cost_estimate=FREE,
    )(place, *slabs, conv, alpha, first_up)


def local(
    frames,
    expert_ids,
    gate_weights,
    up_weight,
    down_weight,
    out_weight,
    in_conv,
    snake_first,
    first_up,
):
    rows, _ = frames.shape
    n = lax.axis_size("expert")
    segs = lax.axis_size("seg")
    quarter, half = n // 4, n // 2
    capacity = -(-(3 * rows // n) // 16) * 16
    me = lax.axis_index("expert")
    place = jnp.stack([me, jnp.int32(n)]).astype(jnp.int32)
    inner = range(quarter, 3 * quarter)
    across_by = 3 * quarter
    is_inner = ((me >= quarter) & (me < across_by)).astype(jnp.int32)

    def swap(value, k, members=range(n)):
        return lax.ppermute(value, "expert", [(i, i ^ k) for i in members])

    across = swap(frames, across_by, inner)
    ids_t = expert_ids.T
    across_ids = swap(ids_t, across_by, inner)
    own = jnp.stack([me, 0]).astype(jnp.int32)
    gates_t, out_w_t = gate_weights.T, out_weight.T
    chunks = make_slots(own, range(half), (ids_t, frames, gates_t), capacity)
    near = [swap(chunks[k], k) for k in range(1, half)]
    origin = jnp.stack([me ^ (is_inner * across_by), is_inner]).astype(jnp.int32)
    sent = make_slots(
        origin, range(half, n), (ids_t, frames, across_ids, across), capacity
    )

    def cross(value, k):
        pairs = [(i, i ^ (k ^ across_by if i in inner else k)) for i in range(n)]
        return lax.ppermute(value, "expert", [(i, j) for i, j in pairs if i != j])

    far = [cross(sent[k - half], k) for k in range(across_by, n)]
    late, near = lax.optimization_barrier((sent[:quarter], near))
    far = [cross(late[k - half], k) for k in range(half, across_by)] + far
    up = up_weight[0]
    gates_t, chunk, down, late = lax.optimization_barrier(
        (gates_t, chunks[0], down_weight[0], late)
    )
    folded = fold_weights(down, out_w_t)
    neighbours = {k: near[k - 1] for k in range(1, half) if is_neighbour(k)}
    pick, scale, base = make_table(
        place, frames, out_w_t, ids_t, gates_t, neighbours, n, capacity
    )
    back = run_group(n, False, place, chunk, near, up, folded)
    parts = [back[0]] + [swap(back[k], k) for k in range(1, half)]
    place, pick, scale, base = lax.optimization_barrier((place, pick, scale, base))
    back = run_group(n, True, place, sent[quarter], far, up, folded)
    parts += [swap(back[k], half + k) for k in range(half)]
    slab, middle = combine(place, parts, pick, scale, base)

    def over_middle(k):
        ends = ((half - 1, half), (half, half - 1))
        pairs = [(i * n + a, (i ^ k) * n + b) for i in range(segs) for a, b in ends]
        return lax.ppermute(middle, ("seg", "expert"), pairs)

    slabs = [slab] + [
        lax.ppermute(slab, "seg", [(i, i ^ k) for i in range(segs)]) for k in range(1, segs)
    ]
    slabs += [over_middle(k) for k in range(segs)]
    spot = jnp.stack([lax.axis_index("seg"), me, jnp.int32(n)]).astype(jnp.int32)
    alpha = jnp.stack([snake_first * (1.0 / math.pi), 1.0 / snake_first])
    conv = in_conv.reshape(-1, in_conv.shape[2])
    return decode(spot, slabs, conv, alpha, first_up)


def solution(mesh):
    placed = (
        P(("seg", "expert"), None),
        P(("seg", "expert"), None),
        P(("seg", "expert"), None),
        P("expert", None, None),
        P("expert", None, None),
        P(),
        P(),
        P(),
        P(None, None, "seg"),
    )
    return jax.shard_map(
        local, mesh=mesh, in_specs=placed, out_specs=P(None, "expert", "seg"), check_vma=False
    )
```

```python
import functools
import math

import jax
import jax.numpy as jnp
from jax import lax
from jax.experimental import pallas as pl
from jax.experimental.pallas import tpu as pltpu
from jax.sharding import PartitionSpec as P

F32 = jnp.float32
BF16 = jnp.bfloat16
VMEM = pltpu.VMEM
SIN2 = (
    9.869603157043457,
    -32.469581604003906,
    42.72538375854492,
    -30.085954666137695,
    12.99073314666748,
    -3.2729504108428955,
)


FREE = pl.CostEstimate(flops=0, bytes_accessed=0, transcendentals=0)


def whole():
    return pl.BlockSpec(memory_space=VMEM)


def params(mib):
    return pltpu.CompilerParams(vmem_limit_bytes=mib * 1024 * 1024)


EDGE = 4
EDGE_ROWS = 16


def token_key(token, rows):
    rest = jnp.where(token >= rows - EDGE, token - (rows - 2 * EDGE), token + EDGE)
    return jnp.where(token < EDGE, token, rest)


def one_hot(mask):
    return mask.astype(F32).astype(BF16)


def is_neighbour(k):
    return k & (k + 1) == 0 and k > 0


def edge_rows(frames, ids, gates):
    rows, width = frames.shape
    parts = []
    for choice in range(2):
        rest = gates[choice : choice + 1]
        for _ in range(3):
            part = rest.astype(BF16).astype(F32)
            parts.append(part)
            rest = rest - part
    meta = jnp.concatenate([ids.astype(F32)] + parts, axis=0)
    meta = jnp.concatenate([meta, jnp.zeros((8, width - rows), F32)], axis=1)
    ends = [frames[:16].astype(F32)[:EDGE], frames[rows - 16 :].astype(F32)[16 - EDGE :]]
    return jnp.concatenate(ends + [meta], axis=0).astype(BF16)


def slots_kernel(steps, origin_ref, *refs):
    sources, out_refs = refs[: -len(steps)], refs[-len(steps) :]
    ids, frames = sources[0][...], sources[1][...]
    if len(sources) == 3:
        capacity = out_refs[0].shape[0]
        extra = edge_rows(frames, ids, sources[2][...])
        for k, ref in zip(steps, out_refs):
            if is_neighbour(k):
                ref[capacity:] = extra
    else:
        second = origin_ref[1] == 1
        ids = jnp.where(second, sources[2][...], ids)
        frames = jnp.where(second, sources[3][...], frames)
    rows = frames.shape[0]
    capacity = out_refs[0].shape[0]
    ids = ids ^ origin_ref[0]
    count = -(-len(steps) // 16) * 16
    step = lax.broadcasted_iota(jnp.int32, (count, rows), 0) + steps[0]
    named = (ids[0:1] == step) | (ids[1:2] == step)
    earlier = token_key(lax.broadcasted_iota(jnp.int32, (rows, rows), 0), rows) < token_key(
        lax.broadcasted_iota(jnp.int32, (rows, rows), 1), rows
    )
    rank = jnp.dot(one_hot(named), one_hot(earlier), preferred_element_type=F32)
    rank = jnp.where(named, rank, -1.0)
    slot = lax.broadcasted_iota(jnp.int32, (capacity, rows), 0).astype(F32)
    for j, ref in enumerate(out_refs):
        pick = one_hot(slot == rank[j : j + 1])
        ref[0:capacity] = jnp.dot(pick, frames, preferred_element_type=F32).astype(BF16)


def make_slots(origin, steps, sources, capacity):
    width = sources[1].shape[1]
    return pl.pallas_call(
        functools.partial(slots_kernel, steps),
        out_shape=[
            jax.ShapeDtypeStruct(
                (capacity + EDGE_ROWS * (len(sources) == 3 and is_neighbour(k)), width), BF16
            )
            for k in steps
        ],
        in_specs=[pl.BlockSpec(memory_space=pltpu.SMEM)] + [whole()] * len(sources),
        out_specs=[whole()] * len(steps),
        compiler_params=params(24),
        cost_estimate=FREE,
    )(origin, *sources)


def fold_kernel(down_ref, out_w_ref, folded_ref):
    full = lax.dot_general(
        down_ref[...], out_w_ref[...], (((1,), (1,)), ((), ())), preferred_element_type=F32
    )
    high = full.astype(BF16)
    low = (full - high.astype(F32)).astype(BF16)
    folded_ref[...] = jnp.concatenate([high, low], axis=1)


def fold_weights(down, out_w_t):
    hid, width = down.shape
    lat = out_w_t.shape[0]
    block = 512 if hid % 512 == 0 else hid
    return pl.pallas_call(
        fold_kernel,
        grid=(hid // block,),
        out_shape=jax.ShapeDtypeStruct((hid, 2 * lat), BF16),
        in_specs=[
            pl.BlockSpec((block, width), lambda i: (i, 0)),
            pl.BlockSpec((lat, width), lambda i: (0, 0)),
        ],
        out_specs=pl.BlockSpec((block, 2 * lat), lambda i: (i, 0)),
        compiler_params=params(16),
        cost_estimate=FREE,
    )(down, out_w_t)


def table_kernel(
    links, place_ref, frames_ref, out_w_ref, ids_ref, gates_ref, *refs
):
    link_refs = refs[: len(links)]
    pick_ref, scale_ref, base_ref = refs[len(links) :]
    n, span, columns = pick_ref.shape
    rows, width = frames_ref.shape
    lat = out_w_ref.shape[0]
    capacity = columns - 2 * EDGE_ROWS
    me, size = place_ref[0], place_ref[1]

    def rows_of(frames, lines):
        base = lax.dot_general(
            frames, out_w_ref[...], (((1,), (1,)), ((), ())), preferred_element_type=F32
        )
        lines = jnp.concatenate([lines, jnp.zeros((128 - lines.shape[0], rows), F32)], axis=0)
        return base, jnp.transpose(lines)[:, : 128 - lat]

    def neighbour(other):
        extra = link_refs[0][capacity:]
        for k, ref in zip(links[1:], link_refs[1:]):
            extra = jnp.where((me ^ other) == k, ref[capacity:], extra)
        meta = extra[:, :rows].astype(F32)[2 * EDGE :]
        gates = [meta[j : j + 1] + meta[j + 1 : j + 2] + meta[j + 2 : j + 3] for j in (2, 5)]
        base, lines = rows_of(extra, jnp.concatenate([meta[:2]] + gates, axis=0))
        return jnp.concatenate(
            [
                jnp.concatenate([base[:EDGE], lines[:EDGE]], axis=1),
                jnp.concatenate([base[EDGE : 2 * EDGE], lines[rows - EDGE :]], axis=1),
            ],
            axis=0,
        )

    left, right = neighbour(me - 1), neighbour(me + 1)
    own = rows_of(
        frames_ref[...], jnp.concatenate([ids_ref[...].astype(F32), gates_ref[...]], axis=0)
    )
    info = jnp.concatenate(
        [
            left[EDGE:],
            jnp.concatenate(own, axis=1),
            right[:EDGE],
            left[:EDGE],
            jnp.zeros((EDGE, 128), F32),
        ],
        axis=0,
    )
    def code(i):
        own = 1024 + token_key(i - EDGE, rows)
        late = jnp.where(i < rows + 3 * EDGE, i - rows - 2 * EDGE, 3072)
        tail = jnp.where(i < rows + 2 * EDGE, 2048 + i - rows - EDGE, late)
        return jnp.where(i < EDGE, i + EDGE, jnp.where(i < rows + EDGE, own, tail))

    line = lax.broadcasted_iota(jnp.int32, (span, 1), 0)
    line_code = code(line)
    other = code(lax.broadcasted_iota(jnp.int32, (1, span), 1))
    earlier = (other < line_code) & (other >= (line_code >> 10) * 1024)
    before = line_code < 1024
    after = (line_code >= 2048) & (line_code < 3072)
    lost = (before & ((me == 0) | (me == size // 2))) | (
        after & ((me == size - 1) | (me == size // 2 - 1))
    )
    base_ref[...] = jnp.where(lost, 0.0, info[:, :lat])
    ids = info[:, lat : lat + 2].astype(jnp.int32) ^ me
    ids = jnp.where(lost | (line_code >= 3072), -1, ids)
    step = lax.broadcasted_iota(jnp.int32, (span, 128), 1)
    first = ids[:, 0:1] == step
    second = ids[:, 1:2] == step
    named = first | second
    rank = jnp.dot(one_hot(earlier), one_hot(named), preferred_element_type=F32)
    rank = rank + jnp.where(before, capacity, jnp.where(after, capacity + EDGE_ROWS, 0)).astype(F32)
    rank = jnp.where(named, rank, -1.0)
    scale_ref[...] = jnp.where(
        first, info[:, lat + 2 : lat + 3], jnp.where(second, info[:, lat + 3 : lat + 4], 0.0)
    )
    slot = lax.broadcasted_iota(jnp.int32, (span, columns), 1).astype(F32)
    for k in range(n):
        pick_ref[k] = one_hot(slot == rank[:, k : k + 1])


def make_table(place, frames, out_w_t, ids_t, gates_t, neighbours, n, capacity):
    span = frames.shape[0] + 4 * EDGE
    lat = out_w_t.shape[0]
    links = tuple(neighbours)
    return pl.pallas_call(
        functools.partial(table_kernel, links),
        out_shape=[
            jax.ShapeDtypeStruct((n, span, capacity + 2 * EDGE_ROWS), BF16),
            jax.ShapeDtypeStruct((span, 128), F32),
            jax.ShapeDtypeStruct((span, lat), F32),
        ],
        in_specs=[pl.BlockSpec(memory_space=pltpu.SMEM)] + [whole()] * (4 + len(links)),
        out_specs=[whole()] * 3,
        compiler_params=params(16),
        cost_estimate=FREE,
    )(place, frames, out_w_t, ids_t, gates_t, *[neighbours[k] for k in links])


def expert_rows(rows, up_ref, folded_ref):
    hid = up_ref.shape[1]
    block = 256 if hid % 256 == 0 else hid
    total = None
    for at in range(0, hid, block):
        v = jnp.dot(rows, up_ref[:, at : at + block], preferred_element_type=F32)
        inner = v * (0.7978845608 + (0.7978845608 * 0.044715) * (v * v))
        hidden = (0.5 * v * (1.0 + jnp.tanh(inner))).astype(BF16)
        part = jnp.dot(hidden, folded_ref[at : at + block, :], preferred_element_type=F32)
        total = part if total is None else total + part
    lat = folded_ref.shape[1] // 2
    value = total[:, :lat] + total[:, lat:]
    high = value.astype(BF16)
    low = (value - high.astype(F32)).astype(BF16)
    return jnp.concatenate([high, low], axis=1)


def write_returns(n, me, held, first, outs):
    capacity = held.shape[1]
    half = n // 2
    for j, ref in enumerate(outs):
        k = first + j
        to = me ^ k
        place = to % half
        left = me ^ jnp.where(place > 0, to - 1, to)
        right = me ^ jnp.where(place < half - 1, to + 1, to)
        ref[0:capacity] = held[k]
        ref[capacity : capacity + EDGE_ROWS] = held[left, 0:EDGE_ROWS]
        ref[capacity + EDGE_ROWS :] = held[right, 0:EDGE_ROWS]


def group_kernel(n, far, place_ref, local_ref, *refs):
    quarter, half = n // 4, n // 2
    chunk_refs = refs[: half - 1 + far]
    up_ref, folded_ref = refs[half - 1 + far : half + 1 + far]
    outs, held = refs[half + 1 + far : -1], refs[-1]
    capacity = local_ref.shape[0]
    me = place_ref[0]
    chunks = [ref[...] for ref in chunk_refs]
    if far:
        is_inner = (me >= quarter) & (me < 3 * quarter)
        chunks[quarter] = jnp.where(is_inner, local_ref[...], chunks[quarter])
    else:
        chunks = [local_ref[...]] + [chunk[:capacity] for chunk in chunks]
    both = expert_rows(jnp.concatenate(chunks, axis=0), up_ref, folded_ref)
    first = half if far else 0
    for j in range(half):
        held[first + j] = both[j * capacity : (j + 1) * capacity]
    write_returns(n, me, held, first, outs)


def run_group(n, far, place, local_chunk, chunks, up, folded):
    capacity = local_chunk.shape[0]
    lanes = folded.shape[1]
    return pl.pallas_call(
        functools.partial(group_kernel, n, far),
        out_shape=[jax.ShapeDtypeStruct((capacity + 2 * EDGE_ROWS, lanes), BF16)] * (n // 2),
        in_specs=[pl.BlockSpec(memory_space=pltpu.SMEM)] + [whole()] * (len(chunks) + 3),
        out_specs=[whole()] * (n // 2),
        scratch_shapes=[pltpu.VMEM((n, capacity, lanes), BF16)],
        compiler_params=params(24),
        cost_estimate=FREE,
    )(place, local_chunk, *chunks, up, folded)


def combine_kernel(n, place_ref, *refs):
    part_refs = refs[:n]
    pick_ref, scale_ref, base_ref, low_ref, middle_ref = refs[n:]
    span, lat = base_ref.shape
    packed = low_ref.shape[0]
    total = None
    for k in range(n):
        picked = jnp.dot(pick_ref[k], part_refs[k][...], preferred_element_type=F32)
        scaled = scale_ref[:, k : k + 1] * picked
        total = scaled if total is None else total + scaled
    low = (base_ref[...] + (total[:, :lat] + total[:, lat:])).astype(BF16)
    low_ref[...] = jnp.concatenate([low[:packed], low[span - packed :]], axis=1)
    edge = jnp.where(
        place_ref[0] >= place_ref[1] // 2, low[:EDGE_ROWS], low[span - EDGE_ROWS :]
    )
    middle_ref[...] = jnp.concatenate([edge, edge], axis=1)


def combine(place, parts, pick, scale, base):
    n = len(parts)
    span, lat = base.shape
    packed = -(-span // 32) * 16
    return pl.pallas_call(
        functools.partial(combine_kernel, n),
        out_shape=[
            jax.ShapeDtypeStruct((packed, 2 * lat), BF16),
            jax.ShapeDtypeStruct((EDGE_ROWS, 2 * lat), BF16),
        ],
        in_specs=[pl.BlockSpec(memory_space=pltpu.SMEM)] + [whole()] * (n + 3),
        out_specs=[whole()] * 2,
        compiler_params=params(16),
        cost_estimate=FREE,
    )(place, *parts, pick, scale, base)


def snake(v, turns_row, inverse_row):
    turns = v * turns_row
    part = turns - jnp.round(turns)
    s = part * part
    poly = SIN2[-1]
    for c in SIN2[-2::-1]:
        poly = poly * s + c
    return v + (poly * s) * inverse_row


def unpack_slab(place_ref, slab_ref, padded):
    span, lat = padded.shape
    packed = slab_ref.shape[0] - EDGE_ROWS
    end = span - 3 * EDGE
    padded[0:packed] = slab_ref[0:packed, :lat].astype(F32)
    padded[span - packed :] = slab_ref[0:packed, lat:].astype(F32)

    @pl.when(place_ref[1] == place_ref[2] // 2)
    def _():
        padded[0:EDGE] = slab_ref[packed:, :lat].astype(F32)[:EDGE]

    @pl.when(place_ref[1] == place_ref[2] // 2 - 1)
    def _():
        padded[end : end + EDGE] = slab_ref[packed:, :lat].astype(F32)[EDGE : 2 * EDGE]


def convolve(place_ref, padded, windows, conv_ref, alpha_ref, act):
    span, lat = padded.shape
    length = span - 4 * EDGE
    channels = conv_ref.shape[1]
    taps = conv_ref.shape[0] // lat
    block = 256
    is_first = place_ref[1] == 0
    is_last = place_ref[1] == place_ref[2] - 1
    row = lax.broadcasted_iota(jnp.int32, (16, taps * lat), 0)
    edge_row = lax.broadcasted_iota(jnp.int32, (16, block), 0)
    gone = ((edge_row == 0) & is_first) | ((edge_row == 1) & is_last)

    def window(start, rows):
        return jnp.concatenate([padded[start + j : start + j + rows] for j in range(taps)], axis=1)

    windows[0:length] = window(1, length).astype(BF16)
    edges = jnp.where(row == 0, window(0, 1), jnp.where(row == 1, window(length + 1, 1), 0.0))
    windows[length:] = edges.astype(BF16)
    for at in range(0, channels, block):
        cols = slice(at, at + block)
        v = jnp.dot(windows[...], conv_ref[:, cols], preferred_element_type=F32)
        value = snake(v, alpha_ref[0:1, cols], alpha_ref[1:2, cols])
        act[0:length, cols] = value[:length].astype(BF16)
        act[length:, cols] = jnp.where(gone, 0.0, value[length:]).astype(BF16)


def own_kernel(place_ref, slab_ref, conv_ref, alpha_ref, act_ref, padded, windows):
    unpack_slab(place_ref, slab_ref, padded)
    convolve(place_ref, padded, windows, conv_ref, alpha_ref, act_ref)


def activate_own(place, slab, conv, alpha, span):
    lat = slab.shape[1] // 2
    taps_lat, channels = conv.shape
    return pl.pallas_call(
        own_kernel,
        out_shape=jax.ShapeDtypeStruct((span, channels), BF16),
        in_specs=[pl.BlockSpec(memory_space=pltpu.SMEM)] + [whole()] * 3,
        out_specs=whole(),
        scratch_shapes=[pltpu.VMEM((span, lat), F32), pltpu.VMEM((span, taps_lat), BF16)],
        compiler_params=params(16),
        cost_estimate=FREE,
    )(place, slab, conv, alpha)


def decoder_kernel(segs, place_ref, own_ref, *refs):
    slab_refs = refs[: segs - 1]
    conv_ref, alpha_ref, up_hbm, out_ref = refs[segs - 1 : segs + 3]
    padded, windows, others, up_ref, rows_out, sems, up_sem = refs[segs + 3 :]
    span = own_ref.shape[0]
    length = span - 4 * EDGE
    width = up_ref.shape[2]
    own = place_ref[0]
    up_copy = pltpu.make_async_copy(up_hbm, up_ref, up_sem)
    up_copy.start()

    def out_copy(k):
        return pltpu.make_async_copy(rows_out.at[k], out_ref.at[own ^ k], sems.at[k])

    for k in range(segs - 1):
        unpack_slab(place_ref, slab_refs[k], padded.at[k])
    for k in range(segs - 1):
        convolve(place_ref, padded.at[k], windows.at[k], conv_ref, alpha_ref, others.at[k])
    up_copy.wait()
    for k in range(segs):
        act = own_ref if k == 0 else others.at[k - 1]
        for r in range(0, 8, 2):
            far = r + 12 if r < 4 else r - 4
            near_w = jnp.concatenate([up_ref[r + 4], up_ref[r + 5]], axis=1)
            far_w = jnp.concatenate([up_ref[far], up_ref[far + 1]], axis=1)
            near = jnp.dot(act[0:length], near_w, preferred_element_type=F32)
            side = jnp.dot(act[...], far_w, preferred_element_type=F32)
            if r < 4:
                moved = [side[length : length + 1], side[: length - 1]]
            else:
                moved = [side[1:length], side[length + 1 : length + 2]]
            res = near + jnp.concatenate(moved, axis=0)
            rows_out[k, pl.ds(r, length, stride=8), :] = res[:, :width]
            rows_out[k, pl.ds(r + 1, length, stride=8), :] = res[:, width:]
        out_copy(k).start()
    for k in range(segs):
        out_copy(k).wait()


def decode(place, own, slabs, conv, alpha, first_up):
    segs = len(slabs) + 1
    span, channels = own.shape
    length = span - 4 * EDGE
    width = first_up.shape[2]
    lat = slabs[0].shape[1] // 2
    return pl.pallas_call(
        functools.partial(decoder_kernel, segs),
        out_shape=jax.ShapeDtypeStruct((segs, 8 * length, width), F32),
        in_specs=[pl.BlockSpec(memory_space=pltpu.SMEM)]
        + [whole()] * (segs + 2)
        + [pl.BlockSpec(memory_space=pl.ANY)],
        out_specs=pl.BlockSpec(memory_space=pl.ANY),
        scratch_shapes=[
            pltpu.VMEM((segs - 1, span, lat), F32),
            pltpu.VMEM((segs - 1, span, conv.shape[0]), BF16),
            pltpu.VMEM((segs - 1, span, channels), BF16),
            pltpu.VMEM(first_up.shape, BF16),
            pltpu.VMEM((segs, 8 * length, width), F32),
            pltpu.SemaphoreType.DMA((segs,)),
            pltpu.SemaphoreType.DMA,
        ],
        compiler_params=params(52),
        cost_estimate=FREE,
    )(place, own, *slabs, conv, alpha, first_up)


def local(
    frames,
    expert_ids,
    gate_weights,
    up_weight,
    down_weight,
    out_weight,
    in_conv,
    snake_first,
    first_up,
):
    rows, _ = frames.shape
    n = lax.axis_size("expert")
    segs = lax.axis_size("seg")
    quarter, half = n // 4, n // 2
    capacity = -(-(3 * rows // n) // 16) * 16
    me = lax.axis_index("expert")
    place = jnp.stack([me, jnp.int32(n)]).astype(jnp.int32)
    inner = range(quarter, 3 * quarter)
    across_by = 3 * quarter
    is_inner = ((me >= quarter) & (me < across_by)).astype(jnp.int32)

    def swap(value, k, members=range(n)):
        return lax.ppermute(value, "expert", [(i, i ^ k) for i in members])

    across = swap(frames, across_by, inner)
    ids_t = expert_ids.T
    across_ids = swap(ids_t, across_by, inner)
    own = jnp.stack([me, 0]).astype(jnp.int32)
    gates_t, out_w_t = gate_weights.T, out_weight.T
    chunks = make_slots(own, range(half), (ids_t, frames, gates_t), capacity)
    near = [swap(chunks[k], k) for k in range(1, half)]
    origin = jnp.stack([me ^ (is_inner * across_by), is_inner]).astype(jnp.int32)
    sent = make_slots(
        origin, range(half, n), (ids_t, frames, across_ids, across), capacity
    )

    def cross(value, k):
        pairs = [(i, i ^ (k ^ across_by if i in inner else k)) for i in range(n)]
        return lax.ppermute(value, "expert", [(i, j) for i, j in pairs if i != j])

    far = [cross(sent[k - half], k) for k in range(across_by, n)]
    late, near = lax.optimization_barrier((sent[:quarter], near))
    far = [cross(late[k - half], k) for k in range(half, across_by)] + far
    up = up_weight[0]
    gates_t, chunk, down, late = lax.optimization_barrier(
        (gates_t, chunks[0], down_weight[0], late)
    )
    folded = fold_weights(down, out_w_t)
    neighbours = {k: near[k - 1] for k in range(1, half) if is_neighbour(k)}
    pick, scale, base = make_table(
        place, frames, out_w_t, ids_t, gates_t, neighbours, n, capacity
    )
    back = run_group(n, False, place, chunk, near, up, folded)
    parts = [back[0]] + [swap(back[k], k) for k in range(1, half)]
    place, pick, scale, base = lax.optimization_barrier((place, pick, scale, base))
    back = run_group(n, True, place, sent[quarter], far, up, folded)
    parts += [swap(back[k], half + k) for k in range(half)]
    slab, middle = combine(place, parts, pick, scale, base)
    middle = lax.ppermute(middle, "expert", [(half - 1, half), (half, half - 1)])
    slab = jnp.concatenate([slab, middle], axis=0)

    others = [
        lax.ppermute(slab, "seg", [(i, i ^ k) for i in range(segs)]) for k in range(1, segs)
    ]
    spot = jnp.stack([lax.axis_index("seg"), me, jnp.int32(n)]).astype(jnp.int32)
    alpha = jnp.stack([snake_first * (1.0 / math.pi), 1.0 / snake_first])
    conv = in_conv.reshape(-1, in_conv.shape[2])
    act = activate_own(spot, slab, conv, alpha, base.shape[0])
    return decode(spot, act, others, conv, alpha, first_up)


def solution(mesh):
    placed = (
        P(("seg", "expert"), None),
        P(("seg", "expert"), None),
        P(("seg", "expert"), None),
        P("expert", None, None),
        P("expert", None, None),
        P(),
        P(),
        P(),
        P(None, None, "seg"),
    )
    return jax.shard_map(
        local, mesh=mesh, in_specs=placed, out_specs=P(None, "expert", "seg"), check_vma=False
    )
```

```python
import functools
import math

import jax
import jax.numpy as jnp
from jax import lax
from jax.experimental import pallas as pl
from jax.experimental.pallas import tpu as pltpu
from jax.sharding import PartitionSpec as P

F32 = jnp.float32
BF16 = jnp.bfloat16
VMEM = pltpu.VMEM
SIN2 = (
    9.869603157043457,
    -32.469581604003906,
    42.72538375854492,
    -30.085954666137695,
    12.99073314666748,
    -3.2729504108428955,
)


FREE = pl.CostEstimate(flops=0, bytes_accessed=0, transcendentals=0)


def whole():
    return pl.BlockSpec(memory_space=VMEM)


def params(mib):
    return pltpu.CompilerParams(vmem_limit_bytes=mib * 1024 * 1024)


EDGE = 4
EDGE_ROWS = 16


def token_key(token, rows):
    rest = jnp.where(token >= rows - EDGE, token - (rows - 2 * EDGE), token + EDGE)
    return jnp.where(token < EDGE, token, rest)


def one_hot(mask):
    return mask.astype(F32).astype(BF16)


def is_neighbour(k):
    return k & (k + 1) == 0 and k > 0


def edge_rows(frames, ids, gates):
    rows, width = frames.shape
    parts = []
    for choice in range(2):
        rest = gates[choice : choice + 1]
        for _ in range(3):
            part = rest.astype(BF16).astype(F32)
            parts.append(part)
            rest = rest - part
    meta = jnp.concatenate([ids.astype(F32)] + parts, axis=0)
    meta = jnp.concatenate([meta, jnp.zeros((8, width - rows), F32)], axis=1)
    ends = [frames[:16].astype(F32)[:EDGE], frames[rows - 16 :].astype(F32)[16 - EDGE :]]
    return jnp.concatenate(ends + [meta], axis=0).astype(BF16)


def slots_kernel(steps, origin_ref, *refs):
    sources, out_refs = refs[: -len(steps)], refs[-len(steps) :]
    ids, frames = sources[0][...], sources[1][...]
    if len(sources) == 3:
        capacity = out_refs[0].shape[0]
        extra = edge_rows(frames, ids, sources[2][...])
        for k, ref in zip(steps, out_refs):
            if is_neighbour(k):
                ref[capacity:] = extra
    else:
        second = origin_ref[1] == 1
        ids = jnp.where(second, sources[2][...], ids)
        frames = jnp.where(second, sources[3][...], frames)
    rows = frames.shape[0]
    capacity = out_refs[0].shape[0]
    ids = ids ^ origin_ref[0]
    count = -(-len(steps) // 16) * 16
    step = lax.broadcasted_iota(jnp.int32, (count, rows), 0) + steps[0]
    named = (ids[0:1] == step) | (ids[1:2] == step)
    earlier = token_key(lax.broadcasted_iota(jnp.int32, (rows, rows), 0), rows) < token_key(
        lax.broadcasted_iota(jnp.int32, (rows, rows), 1), rows
    )
    rank = jnp.dot(one_hot(named), one_hot(earlier), preferred_element_type=F32)
    rank = jnp.where(named, rank, -1.0)
    slot = lax.broadcasted_iota(jnp.int32, (capacity, rows), 0).astype(F32)
    for j, ref in enumerate(out_refs):
        pick = one_hot(slot == rank[j : j + 1])
        ref[0:capacity] = jnp.dot(pick, frames, preferred_element_type=F32).astype(BF16)


def make_slots(origin, steps, sources, capacity):
    width = sources[1].shape[1]
    return pl.pallas_call(
        functools.partial(slots_kernel, steps),
        out_shape=[
            jax.ShapeDtypeStruct(
                (capacity + EDGE_ROWS * (len(sources) == 3 and is_neighbour(k)), width), BF16
            )
            for k in steps
        ],
        in_specs=[pl.BlockSpec(memory_space=pltpu.SMEM)] + [whole()] * len(sources),
        out_specs=[whole()] * len(steps),
        compiler_params=params(24),
        cost_estimate=FREE,
    )(origin, *sources)


def fold_kernel(down_ref, out_w_ref, folded_ref):
    full = lax.dot_general(
        down_ref[...], out_w_ref[...], (((1,), (1,)), ((), ())), preferred_element_type=F32
    )
    high = full.astype(BF16)
    low = (full - high.astype(F32)).astype(BF16)
    folded_ref[...] = jnp.concatenate([high, low], axis=1)


def fold_weights(down, out_w_t):
    hid, width = down.shape
    lat = out_w_t.shape[0]
    block = 512 if hid % 512 == 0 else hid
    return pl.pallas_call(
        fold_kernel,
        grid=(hid // block,),
        out_shape=jax.ShapeDtypeStruct((hid, 2 * lat), BF16),
        in_specs=[
            pl.BlockSpec((block, width), lambda i: (i, 0)),
            pl.BlockSpec((lat, width), lambda i: (0, 0)),
        ],
        out_specs=pl.BlockSpec((block, 2 * lat), lambda i: (i, 0)),
        compiler_params=params(16),
        cost_estimate=FREE,
    )(down, out_w_t)


def table_kernel(
    links, place_ref, frames_ref, out_w_ref, ids_ref, gates_ref, *refs
):
    link_refs = refs[: len(links)]
    pick_ref, scale_ref, base_ref = refs[len(links) :]
    n, span, columns = pick_ref.shape
    rows, width = frames_ref.shape
    lat = out_w_ref.shape[0]
    capacity = columns - 2 * EDGE_ROWS
    me, size = place_ref[0], place_ref[1]

    def rows_of(frames, lines):
        base = lax.dot_general(
            frames, out_w_ref[...], (((1,), (1,)), ((), ())), preferred_element_type=F32
        )
        lines = jnp.concatenate([lines, jnp.zeros((128 - lines.shape[0], rows), F32)], axis=0)
        return base, jnp.transpose(lines)[:, : 128 - lat]

    def neighbour(other):
        extra = link_refs[0][capacity:]
        for k, ref in zip(links[1:], link_refs[1:]):
            extra = jnp.where((me ^ other) == k, ref[capacity:], extra)
        meta = extra[:, :rows].astype(F32)[2 * EDGE :]
        gates = [meta[j : j + 1] + meta[j + 1 : j + 2] + meta[j + 2 : j + 3] for j in (2, 5)]
        base, lines = rows_of(extra, jnp.concatenate([meta[:2]] + gates, axis=0))
        return jnp.concatenate(
            [
                jnp.concatenate([base[:EDGE], lines[:EDGE]], axis=1),
                jnp.concatenate([base[EDGE : 2 * EDGE], lines[rows - EDGE :]], axis=1),
            ],
            axis=0,
        )

    left, right = neighbour(me - 1), neighbour(me + 1)
    own = rows_of(
        frames_ref[...], jnp.concatenate([ids_ref[...].astype(F32), gates_ref[...]], axis=0)
    )
    info = jnp.concatenate(
        [
            left[EDGE:],
            jnp.concatenate(own, axis=1),
            right[:EDGE],
            left[:EDGE],
            jnp.zeros((EDGE, 128), F32),
        ],
        axis=0,
    )
    def code(i):
        own = 1024 + token_key(i - EDGE, rows)
        late = jnp.where(i < rows + 3 * EDGE, i - rows - 2 * EDGE, 3072)
        tail = jnp.where(i < rows + 2 * EDGE, 2048 + i - rows - EDGE, late)
        return jnp.where(i < EDGE, i + EDGE, jnp.where(i < rows + EDGE, own, tail))

    line = lax.broadcasted_iota(jnp.int32, (span, 1), 0)
    line_code = code(line)
    other = code(lax.broadcasted_iota(jnp.int32, (1, span), 1))
    earlier = (other < line_code) & (other >= (line_code >> 10) * 1024)
    before = line_code < 1024
    after = (line_code >= 2048) & (line_code < 3072)
    lost = (before & ((me == 0) | (me == size // 2))) | (
        after & ((me == size - 1) | (me == size // 2 - 1))
    )
    base_ref[...] = jnp.where(lost, 0.0, info[:, :lat])
    ids = info[:, lat : lat + 2].astype(jnp.int32) ^ me
    ids = jnp.where(lost | (line_code >= 3072), -1, ids)
    step = lax.broadcasted_iota(jnp.int32, (span, 128), 1)
    first = ids[:, 0:1] == step
    second = ids[:, 1:2] == step
    named = first | second
    rank = jnp.dot(one_hot(earlier), one_hot(named), preferred_element_type=F32)
    rank = rank + jnp.where(before, capacity, jnp.where(after, capacity + EDGE_ROWS, 0)).astype(F32)
    rank = jnp.where(named, rank, -1.0)
    scale_ref[...] = jnp.where(
        first, info[:, lat + 2 : lat + 3], jnp.where(second, info[:, lat + 3 : lat + 4], 0.0)
    )
    slot = lax.broadcasted_iota(jnp.int32, (span, columns), 1).astype(F32)
    for k in range(n):
        pick_ref[k] = one_hot(slot == rank[:, k : k + 1])


def make_table(place, frames, out_w_t, ids_t, gates_t, neighbours, n, capacity):
    span = frames.shape[0] + 4 * EDGE
    lat = out_w_t.shape[0]
    links = tuple(neighbours)
    return pl.pallas_call(
        functools.partial(table_kernel, links),
        out_shape=[
            jax.ShapeDtypeStruct((n, span, capacity + 2 * EDGE_ROWS), BF16),
            jax.ShapeDtypeStruct((span, 128), F32),
            jax.ShapeDtypeStruct((span, lat), F32),
        ],
        in_specs=[pl.BlockSpec(memory_space=pltpu.SMEM)] + [whole()] * (4 + len(links)),
        out_specs=[whole()] * 3,
        compiler_params=params(16),
        cost_estimate=FREE,
    )(place, frames, out_w_t, ids_t, gates_t, *[neighbours[k] for k in links])


def expert_rows(rows, up_ref, folded_ref):
    hid = up_ref.shape[1]
    block = 256 if hid % 256 == 0 else hid
    total = None
    for at in range(0, hid, block):
        v = jnp.dot(rows, up_ref[:, at : at + block], preferred_element_type=F32)
        inner = v * (0.7978845608 + (0.7978845608 * 0.044715) * (v * v))
        hidden = (0.5 * v * (1.0 + jnp.tanh(inner))).astype(BF16)
        part = jnp.dot(hidden, folded_ref[at : at + block, :], preferred_element_type=F32)
        total = part if total is None else total + part
    lat = folded_ref.shape[1] // 2
    value = total[:, :lat] + total[:, lat:]
    high = value.astype(BF16)
    low = (value - high.astype(F32)).astype(BF16)
    return jnp.concatenate([high, low], axis=1)


def write_returns(n, me, held, first, outs):
    capacity = held.shape[1]
    half = n // 2
    for j, ref in enumerate(outs):
        k = first + j
        to = me ^ k
        place = to % half
        left = me ^ jnp.where(place > 0, to - 1, to)
        right = me ^ jnp.where(place < half - 1, to + 1, to)
        ref[0:capacity] = held[k]
        ref[capacity : capacity + EDGE_ROWS] = held[left, 0:EDGE_ROWS]
        ref[capacity + EDGE_ROWS :] = held[right, 0:EDGE_ROWS]


def group_kernel(n, far, place_ref, local_ref, *refs):
    quarter, half = n // 4, n // 2
    chunk_refs = refs[: half - 1 + far]
    up_ref, folded_ref = refs[half - 1 + far : half + 1 + far]
    outs, held = refs[half + 1 + far : -1], refs[-1]
    capacity = local_ref.shape[0]
    me = place_ref[0]
    chunks = [ref[...] for ref in chunk_refs]
    if far:
        is_inner = (me >= quarter) & (me < 3 * quarter)
        chunks[quarter] = jnp.where(is_inner, local_ref[...], chunks[quarter])
    else:
        chunks = [local_ref[...]] + [chunk[:capacity] for chunk in chunks]
    both = expert_rows(jnp.concatenate(chunks, axis=0), up_ref, folded_ref)
    first = half if far else 0
    for j in range(half):
        held[first + j] = both[j * capacity : (j + 1) * capacity]
    write_returns(n, me, held, first, outs)


def run_group(n, far, place, local_chunk, chunks, up, folded):
    capacity = local_chunk.shape[0]
    lanes = folded.shape[1]
    return pl.pallas_call(
        functools.partial(group_kernel, n, far),
        out_shape=[jax.ShapeDtypeStruct((capacity + 2 * EDGE_ROWS, lanes), BF16)] * (n // 2),
        in_specs=[pl.BlockSpec(memory_space=pltpu.SMEM)] + [whole()] * (len(chunks) + 3),
        out_specs=[whole()] * (n // 2),
        scratch_shapes=[pltpu.VMEM((n, capacity, lanes), BF16)],
        compiler_params=params(24),
        cost_estimate=FREE,
    )(place, local_chunk, *chunks, up, folded)


def combine_kernel(n, place_ref, *refs):
    part_refs = refs[:n]
    pick_ref, scale_ref, base_ref, low_ref, middle_ref = refs[n:]
    span, lat = base_ref.shape
    packed = low_ref.shape[0]
    total = None
    for k in range(n):
        picked = jnp.dot(pick_ref[k], part_refs[k][...], preferred_element_type=F32)
        scaled = scale_ref[:, k : k + 1] * picked
        total = scaled if total is None else total + scaled
    low = (base_ref[...] + (total[:, :lat] + total[:, lat:])).astype(BF16)
    low_ref[...] = jnp.concatenate([low[:packed], low[span - packed :]], axis=1)
    edge = jnp.where(
        place_ref[0] >= place_ref[1] // 2, low[:EDGE_ROWS], low[span - EDGE_ROWS :]
    )
    middle_ref[...] = jnp.concatenate([edge, edge], axis=1)


def combine(place, parts, pick, scale, base):
    n = len(parts)
    span, lat = base.shape
    packed = -(-span // 32) * 16
    return pl.pallas_call(
        functools.partial(combine_kernel, n),
        out_shape=[
            jax.ShapeDtypeStruct((packed, 2 * lat), BF16),
            jax.ShapeDtypeStruct((EDGE_ROWS, 2 * lat), BF16),
        ],
        in_specs=[pl.BlockSpec(memory_space=pltpu.SMEM)] + [whole()] * (n + 3),
        out_specs=[whole()] * 2,
        compiler_params=params(16),
        cost_estimate=FREE,
    )(place, *parts, pick, scale, base)


def snake(v, turns_row, inverse_row):
    turns = v * turns_row
    part = turns - jnp.round(turns)
    s = part * part
    poly = SIN2[-1]
    for c in SIN2[-2::-1]:
        poly = poly * s + c
    return v + (poly * s) * inverse_row


def unpack_slab(place_ref, slab_ref, padded):
    span, lat = padded.shape
    packed = slab_ref.shape[0] - EDGE_ROWS
    end = span - 3 * EDGE
    padded[0:packed] = slab_ref[0:packed, :lat].astype(F32)
    padded[span - packed :] = slab_ref[0:packed, lat:].astype(F32)

    @pl.when(place_ref[1] == place_ref[2] // 2)
    def _():
        padded[0:EDGE] = slab_ref[packed:, :lat].astype(F32)[:EDGE]

    @pl.when(place_ref[1] == place_ref[2] // 2 - 1)
    def _():
        padded[end : end + EDGE] = slab_ref[packed:, :lat].astype(F32)[EDGE : 2 * EDGE]


def convolve(place_ref, padded, windows, conv_ref, alpha_ref, act):
    span, lat = padded.shape
    length = span - 4 * EDGE
    channels = conv_ref.shape[1]
    taps = conv_ref.shape[0] // lat
    block = 256
    is_first = place_ref[1] == 0
    is_last = place_ref[1] == place_ref[2] - 1
    row = lax.broadcasted_iota(jnp.int32, (16, taps * lat), 0)
    edge_row = lax.broadcasted_iota(jnp.int32, (16, block), 0)
    gone = ((edge_row == 0) & is_first) | ((edge_row == 1) & is_last)

    def window(start, rows):
        return jnp.concatenate([padded[start + j : start + j + rows] for j in range(taps)], axis=1)

    windows[0:length] = window(1, length).astype(BF16)
    edges = jnp.where(row == 0, window(0, 1), jnp.where(row == 1, window(length + 1, 1), 0.0))
    windows[length:] = edges.astype(BF16)
    for at in range(0, channels, block):
        cols = slice(at, at + block)
        v = jnp.dot(windows[...], conv_ref[:, cols], preferred_element_type=F32)
        value = snake(v, alpha_ref[0:1, cols], alpha_ref[1:2, cols])
        act[0:length, cols] = value[:length].astype(BF16)
        act[length:, cols] = jnp.where(gone, 0.0, value[length:]).astype(BF16)


def own_kernel(place_ref, slab_ref, conv_ref, alpha_ref, act_ref, padded, windows):
    unpack_slab(place_ref, slab_ref, padded)
    convolve(place_ref, padded, windows, conv_ref, alpha_ref, act_ref)


def activate_own(place, slab, conv, alpha, span):
    lat = slab.shape[1] // 2
    taps_lat, channels = conv.shape
    return pl.pallas_call(
        own_kernel,
        out_shape=jax.ShapeDtypeStruct((span, channels), BF16),
        in_specs=[pl.BlockSpec(memory_space=pltpu.SMEM)] + [whole()] * 3,
        out_specs=whole(),
        scratch_shapes=[pltpu.VMEM((span, lat), F32), pltpu.VMEM((span, taps_lat), BF16)],
        compiler_params=params(16),
        cost_estimate=FREE,
    )(place, slab, conv, alpha)


def stage_kernel(source_ref, target_ref, sem):
    copy = pltpu.make_async_copy(source_ref, target_ref, sem)
    copy.start()
    copy.wait()


def stage(value):
    return pl.pallas_call(
        stage_kernel,
        out_shape=jax.ShapeDtypeStruct(value.shape, value.dtype),
        in_specs=[pl.BlockSpec(memory_space=pl.ANY)],
        out_specs=whole(),
        scratch_shapes=[pltpu.SemaphoreType.DMA],
        compiler_params=params(16),
        cost_estimate=FREE,
    )(value)


def decoder_kernel(segs, place_ref, own_ref, *refs):
    slab_refs = refs[: segs - 1]
    conv_ref, alpha_ref, up_ref, out_ref = refs[segs - 1 : segs + 3]
    padded, windows, others, rows_out, sems = refs[segs + 3 :]
    span = own_ref.shape[0]
    length = span - 4 * EDGE
    width = up_ref.shape[2]
    own = place_ref[0]

    def out_copy(k):
        return pltpu.make_async_copy(rows_out.at[k], out_ref.at[own ^ k], sems.at[k])

    for k in range(segs - 1):
        unpack_slab(place_ref, slab_refs[k], padded.at[k])
    for k in range(segs - 1):
        convolve(place_ref, padded.at[k], windows.at[k], conv_ref, alpha_ref, others.at[k])
    for k in range(segs):
        act = own_ref if k == 0 else others.at[k - 1]
        for r in range(0, 8, 2):
            far = r + 12 if r < 4 else r - 4
            near_w = jnp.concatenate([up_ref[r + 4], up_ref[r + 5]], axis=1)
            far_w = jnp.concatenate([up_ref[far], up_ref[far + 1]], axis=1)
            near = jnp.dot(act[0:length], near_w, preferred_element_type=F32)
            side = jnp.dot(act[...], far_w, preferred_element_type=F32)
            if r < 4:
                moved = [side[length : length + 1], side[: length - 1]]
            else:
                moved = [side[1:length], side[length + 1 : length + 2]]
            res = near + jnp.concatenate(moved, axis=0)
            rows_out[k, pl.ds(r, length, stride=8), :] = res[:, :width]
            rows_out[k, pl.ds(r + 1, length, stride=8), :] = res[:, width:]
        out_copy(k).start()
    for k in range(segs):
        out_copy(k).wait()


def decode(place, own, slabs, conv, alpha, first_up):
    segs = len(slabs) + 1
    span, channels = own.shape
    length = span - 4 * EDGE
    width = first_up.shape[2]
    lat = slabs[0].shape[1] // 2
    return pl.pallas_call(
        functools.partial(decoder_kernel, segs),
        out_shape=jax.ShapeDtypeStruct((segs, 8 * length, width), F32),
        in_specs=[pl.BlockSpec(memory_space=pltpu.SMEM)]
        + [whole()] * (segs + 3),
        out_specs=pl.BlockSpec(memory_space=pl.ANY),
        scratch_shapes=[
            pltpu.VMEM((segs - 1, span, lat), F32),
            pltpu.VMEM((segs - 1, span, conv.shape[0]), BF16),
            pltpu.VMEM((segs - 1, span, channels), BF16),
            pltpu.VMEM((segs, 8 * length, width), F32),
            pltpu.SemaphoreType.DMA((segs,)),
        ],
        compiler_params=params(32),
        cost_estimate=FREE,
    )(place, own, *slabs, conv, alpha, first_up)


def local(
    frames,
    expert_ids,
    gate_weights,
    up_weight,
    down_weight,
    out_weight,
    in_conv,
    snake_first,
    first_up,
):
    rows, _ = frames.shape
    n = lax.axis_size("expert")
    segs = lax.axis_size("seg")
    quarter, half = n // 4, n // 2
    capacity = -(-(3 * rows // n) // 16) * 16
    me = lax.axis_index("expert")
    place = jnp.stack([me, jnp.int32(n)]).astype(jnp.int32)
    inner = range(quarter, 3 * quarter)
    across_by = 3 * quarter
    is_inner = ((me >= quarter) & (me < across_by)).astype(jnp.int32)

    def swap(value, k, members=range(n)):
        return lax.ppermute(value, "expert", [(i, i ^ k) for i in members])

    across = swap(frames, across_by, inner)
    ids_t = expert_ids.T
    across_ids = swap(ids_t, across_by, inner)
    own = jnp.stack([me, 0]).astype(jnp.int32)
    gates_t, out_w_t = gate_weights.T, out_weight.T
    chunks = make_slots(own, range(half), (ids_t, frames, gates_t), capacity)
    near = [swap(chunks[k], k) for k in range(1, half)]
    origin = jnp.stack([me ^ (is_inner * across_by), is_inner]).astype(jnp.int32)
    sent = make_slots(
        origin, range(half, n), (ids_t, frames, across_ids, across), capacity
    )

    def cross(value, k):
        pairs = [(i, i ^ (k ^ across_by if i in inner else k)) for i in range(n)]
        return lax.ppermute(value, "expert", [(i, j) for i, j in pairs if i != j])

    far = [cross(sent[k - half], k) for k in range(across_by, n)]
    late, near = lax.optimization_barrier((sent[:quarter], near))
    far = [cross(late[k - half], k) for k in range(half, across_by)] + far
    up = up_weight[0]
    gates_t, chunk, down, late = lax.optimization_barrier(
        (gates_t, chunks[0], down_weight[0], late)
    )
    folded = fold_weights(down, out_w_t)
    neighbours = {k: near[k - 1] for k in range(1, half) if is_neighbour(k)}
    pick, scale, base = make_table(
        place, frames, out_w_t, ids_t, gates_t, neighbours, n, capacity
    )
    back = run_group(n, False, place, chunk, near, up, folded)
    back, first_up = lax.optimization_barrier((back, first_up))
    staged = stage(first_up)
    parts = [back[0]] + [swap(back[k], k) for k in range(1, half)]
    place, pick, scale, base, staged = lax.optimization_barrier((place, pick, scale, base, staged))
    back = run_group(n, True, place, sent[quarter], far, up, folded)
    parts += [swap(back[k], half + k) for k in range(half)]
    slab, middle = combine(place, parts, pick, scale, base)
    middle = lax.ppermute(middle, "expert", [(half - 1, half), (half, half - 1)])
    slab = jnp.concatenate([slab, middle], axis=0)

    others = [
        lax.ppermute(slab, "seg", [(i, i ^ k) for i in range(segs)]) for k in range(1, segs)
    ]
    spot = jnp.stack([lax.axis_index("seg"), me, jnp.int32(n)]).astype(jnp.int32)
    alpha = jnp.stack([snake_first * (1.0 / math.pi), 1.0 / snake_first])
    conv = in_conv.reshape(-1, in_conv.shape[2])
    act = activate_own(spot, slab, conv, alpha, base.shape[0])
    return decode(spot, act, others, conv, alpha, staged)


def solution(mesh):
    placed = (
        P(("seg", "expert"), None),
        P(("seg", "expert"), None),
        P(("seg", "expert"), None),
        P("expert", None, None),
        P("expert", None, None),
        P(),
        P(),
        P(),
        P(None, None, "seg"),
    )
    return jax.shard_map(
        local, mesh=mesh, in_specs=placed, out_specs=P(None, "expert", "seg"), check_vma=False
    )
```

```python
import functools
import math

import jax
import jax.numpy as jnp
from jax import lax
from jax.experimental import pallas as pl
from jax.experimental.pallas import tpu as pltpu
from jax.sharding import PartitionSpec as P

F32 = jnp.float32
BF16 = jnp.bfloat16
VMEM = pltpu.VMEM
SIN2 = (
    9.869603157043457,
    -32.469581604003906,
    42.72538375854492,
    -30.085954666137695,
    12.99073314666748,
    -3.2729504108428955,
)


FREE = pl.CostEstimate(flops=0, bytes_accessed=0, transcendentals=0)


def whole():
    return pl.BlockSpec(memory_space=VMEM)


def params(mib):
    return pltpu.CompilerParams(vmem_limit_bytes=mib * 1024 * 1024)


EDGE = 4
EDGE_ROWS = 16


def token_key(token, rows):
    rest = jnp.where(token >= rows - EDGE, token - (rows - 2 * EDGE), token + EDGE)
    return jnp.where(token < EDGE, token, rest)


def one_hot(mask):
    return mask.astype(F32).astype(BF16)


def is_neighbour(k):
    return k & (k + 1) == 0 and k > 0


def edge_rows(frames, ids, gates):
    rows, width = frames.shape
    parts = []
    for choice in range(2):
        rest = gates[choice : choice + 1]
        for _ in range(3):
            part = rest.astype(BF16).astype(F32)
            parts.append(part)
            rest = rest - part
    meta = jnp.concatenate([ids.astype(F32)] + parts, axis=0)
    meta = jnp.concatenate([meta, jnp.zeros((8, width - rows), F32)], axis=1)
    ends = [frames[:16].astype(F32)[:EDGE], frames[rows - 16 :].astype(F32)[16 - EDGE :]]
    return jnp.concatenate(ends + [meta], axis=0).astype(BF16)


def slots_kernel(steps, origin_ref, *refs):
    sources, out_refs = refs[: -len(steps)], refs[-len(steps) :]
    ids, frames = sources[0][...], sources[1][...]
    if len(sources) == 3:
        capacity = out_refs[0].shape[0]
        extra = edge_rows(frames, ids, sources[2][...])
        for k, ref in zip(steps, out_refs):
            if is_neighbour(k):
                ref[capacity:] = extra
    else:
        second = origin_ref[1] == 1
        ids = jnp.where(second, sources[2][...], ids)
        frames = jnp.where(second, sources[3][...], frames)
    rows = frames.shape[0]
    capacity = out_refs[0].shape[0]
    ids = ids ^ origin_ref[0]
    count = -(-len(steps) // 16) * 16
    step = lax.broadcasted_iota(jnp.int32, (count, rows), 0) + steps[0]
    named = (ids[0:1] == step) | (ids[1:2] == step)
    earlier = token_key(lax.broadcasted_iota(jnp.int32, (rows, rows), 0), rows) < token_key(
        lax.broadcasted_iota(jnp.int32, (rows, rows), 1), rows
    )
    rank = jnp.dot(one_hot(named), one_hot(earlier), preferred_element_type=F32)
    rank = jnp.where(named, rank, -1.0)
    slot = lax.broadcasted_iota(jnp.int32, (capacity, rows), 0).astype(F32)
    for j, ref in enumerate(out_refs):
        pick = one_hot(slot == rank[j : j + 1])
        ref[0:capacity] = jnp.dot(pick, frames, preferred_element_type=F32).astype(BF16)


def make_slots(origin, steps, sources, capacity):
    width = sources[1].shape[1]
    return pl.pallas_call(
        functools.partial(slots_kernel, steps),
        out_shape=[
            jax.ShapeDtypeStruct(
                (capacity + EDGE_ROWS * (len(sources) == 3 and is_neighbour(k)), width), BF16
            )
            for k in steps
        ],
        in_specs=[pl.BlockSpec(memory_space=pltpu.SMEM)] + [whole()] * len(sources),
        out_specs=[whole()] * len(steps),
        compiler_params=params(24),
        cost_estimate=FREE,
    )(origin, *sources)


def fold_kernel(down_ref, out_w_ref, folded_ref):
    full = lax.dot_general(
        down_ref[...], out_w_ref[...], (((1,), (1,)), ((), ())), preferred_element_type=F32
    )
    high = full.astype(BF16)
    low = (full - high.astype(F32)).astype(BF16)
    folded_ref[...] = jnp.concatenate([high, low], axis=1)


def fold_weights(down, out_w_t):
    hid, width = down.shape
    lat = out_w_t.shape[0]
    block = 512 if hid % 512 == 0 else hid
    return pl.pallas_call(
        fold_kernel,
        grid=(hid // block,),
        out_shape=jax.ShapeDtypeStruct((hid, 2 * lat), BF16),
        in_specs=[
            pl.BlockSpec((block, width), lambda i: (i, 0)),
            pl.BlockSpec((lat, width), lambda i: (0, 0)),
        ],
        out_specs=pl.BlockSpec((block, 2 * lat), lambda i: (i, 0)),
        compiler_params=params(16),
        cost_estimate=FREE,
    )(down, out_w_t)


def table_kernel(
    links, place_ref, frames_ref, out_w_ref, ids_ref, gates_ref, *refs
):
    link_refs = refs[: len(links)]
    pick_ref, scale_ref, base_ref = refs[len(links) :]
    n, span, columns = pick_ref.shape
    rows, width = frames_ref.shape
    lat = out_w_ref.shape[0]
    capacity = columns - 2 * EDGE_ROWS
    me, size = place_ref[0], place_ref[1]

    def rows_of(frames, lines):
        base = lax.dot_general(
            frames, out_w_ref[...], (((1,), (1,)), ((), ())), preferred_element_type=F32
        )
        lines = jnp.concatenate([lines, jnp.zeros((128 - lines.shape[0], rows), F32)], axis=0)
        return base, jnp.transpose(lines)[:, : 128 - lat]

    def neighbour(other):
        extra = link_refs[0][capacity:]
        for k, ref in zip(links[1:], link_refs[1:]):
            extra = jnp.where((me ^ other) == k, ref[capacity:], extra)
        meta = extra[:, :rows].astype(F32)[2 * EDGE :]
        gates = [meta[j : j + 1] + meta[j + 1 : j + 2] + meta[j + 2 : j + 3] for j in (2, 5)]
        base, lines = rows_of(extra, jnp.concatenate([meta[:2]] + gates, axis=0))
        return jnp.concatenate(
            [
                jnp.concatenate([base[:EDGE], lines[:EDGE]], axis=1),
                jnp.concatenate([base[EDGE : 2 * EDGE], lines[rows - EDGE :]], axis=1),
            ],
            axis=0,
        )

    left, right = neighbour(me - 1), neighbour(me + 1)
    own = rows_of(
        frames_ref[...], jnp.concatenate([ids_ref[...].astype(F32), gates_ref[...]], axis=0)
    )
    info = jnp.concatenate(
        [
            left[EDGE:],
            jnp.concatenate(own, axis=1),
            right[:EDGE],
            left[:EDGE],
            jnp.zeros((EDGE, 128), F32),
        ],
        axis=0,
    )
    def code(i):
        own = 1024 + token_key(i - EDGE, rows)
        late = jnp.where(i < rows + 3 * EDGE, i - rows - 2 * EDGE, 3072)
        tail = jnp.where(i < rows + 2 * EDGE, 2048 + i - rows - EDGE, late)
        return jnp.where(i < EDGE, i + EDGE, jnp.where(i < rows + EDGE, own, tail))

    line = lax.broadcasted_iota(jnp.int32, (span, 1), 0)
    line_code = code(line)
    other = code(lax.broadcasted_iota(jnp.int32, (1, span), 1))
    earlier = (other < line_code) & (other >= (line_code >> 10) * 1024)
    before = line_code < 1024
    after = (line_code >= 2048) & (line_code < 3072)
    lost = (before & ((me == 0) | (me == size // 2))) | (
        after & ((me == size - 1) | (me == size // 2 - 1))
    )
    base_ref[...] = jnp.where(lost, 0.0, info[:, :lat])
    ids = info[:, lat : lat + 2].astype(jnp.int32) ^ me
    ids = jnp.where(lost | (line_code >= 3072), -1, ids)
    step = lax.broadcasted_iota(jnp.int32, (span, 128), 1)
    first = ids[:, 0:1] == step
    second = ids[:, 1:2] == step
    named = first | second
    rank = jnp.dot(one_hot(earlier), one_hot(named), preferred_element_type=F32)
    rank = rank + jnp.where(before, capacity, jnp.where(after, capacity + EDGE_ROWS, 0)).astype(F32)
    rank = jnp.where(named, rank, -1.0)
    scale_ref[...] = jnp.where(
        first, info[:, lat + 2 : lat + 3], jnp.where(second, info[:, lat + 3 : lat + 4], 0.0)
    )
    slot = lax.broadcasted_iota(jnp.int32, (span, columns), 1).astype(F32)
    for k in range(n):
        pick_ref[k] = one_hot(slot == rank[:, k : k + 1])


def make_table(place, frames, out_w_t, ids_t, gates_t, neighbours, n, capacity):
    span = frames.shape[0] + 4 * EDGE
    lat = out_w_t.shape[0]
    links = tuple(neighbours)
    return pl.pallas_call(
        functools.partial(table_kernel, links),
        out_shape=[
            jax.ShapeDtypeStruct((n, span, capacity + 2 * EDGE_ROWS), BF16),
            jax.ShapeDtypeStruct((span, 128), F32),
            jax.ShapeDtypeStruct((span, lat), F32),
        ],
        in_specs=[pl.BlockSpec(memory_space=pltpu.SMEM)] + [whole()] * (4 + len(links)),
        out_specs=[whole()] * 3,
        compiler_params=params(16),
        cost_estimate=FREE,
    )(place, frames, out_w_t, ids_t, gates_t, *[neighbours[k] for k in links])


def expert_rows(rows, up_ref, folded_ref):
    hid = up_ref.shape[1]
    block = 256 if hid % 256 == 0 else hid
    total = None
    for at in range(0, hid, block):
        v = jnp.dot(rows, up_ref[:, at : at + block], preferred_element_type=F32)
        inner = v * (0.7978845608 + (0.7978845608 * 0.044715) * (v * v))
        hidden = (0.5 * v * (1.0 + jnp.tanh(inner))).astype(BF16)
        part = jnp.dot(hidden, folded_ref[at : at + block, :], preferred_element_type=F32)
        total = part if total is None else total + part
    lat = folded_ref.shape[1] // 2
    value = total[:, :lat] + total[:, lat:]
    high = value.astype(BF16)
    low = (value - high.astype(F32)).astype(BF16)
    return jnp.concatenate([high, low], axis=1)


def write_returns(n, me, held, first, outs):
    capacity = held.shape[1]
    half = n // 2
    for j, ref in enumerate(outs):
        k = first + j
        to = me ^ k
        place = to % half
        left = me ^ jnp.where(place > 0, to - 1, to)
        right = me ^ jnp.where(place < half - 1, to + 1, to)
        ref[0:capacity] = held[k]
        ref[capacity : capacity + EDGE_ROWS] = held[left, 0:EDGE_ROWS]
        ref[capacity + EDGE_ROWS :] = held[right, 0:EDGE_ROWS]


def group_kernel(n, far, place_ref, local_ref, *refs):
    quarter, half = n // 4, n // 2
    chunk_refs = refs[: half - 1 + far]
    up_ref, folded_ref = refs[half - 1 + far : half + 1 + far]
    outs, held = refs[half + 1 + far : -1], refs[-1]
    capacity = local_ref.shape[0]
    me = place_ref[0]
    chunks = [ref[...] for ref in chunk_refs]
    if far:
        is_inner = (me >= quarter) & (me < 3 * quarter)
        chunks[quarter] = jnp.where(is_inner, local_ref[...], chunks[quarter])
    else:
        chunks = [local_ref[...]] + [chunk[:capacity] for chunk in chunks]
    both = expert_rows(jnp.concatenate(chunks, axis=0), up_ref, folded_ref)
    first = half if far else 0
    for j in range(half):
        held[first + j] = both[j * capacity : (j + 1) * capacity]
    write_returns(n, me, held, first, outs)


def run_group(n, far, place, local_chunk, chunks, up, folded):
    capacity = local_chunk.shape[0]
    lanes = folded.shape[1]
    return pl.pallas_call(
        functools.partial(group_kernel, n, far),
        out_shape=[jax.ShapeDtypeStruct((capacity + 2 * EDGE_ROWS, lanes), BF16)] * (n // 2),
        in_specs=[pl.BlockSpec(memory_space=pltpu.SMEM)] + [whole()] * (len(chunks) + 3),
        out_specs=[whole()] * (n // 2),
        scratch_shapes=[pltpu.VMEM((n, capacity, lanes), BF16)],
        compiler_params=params(24),
        cost_estimate=FREE,
    )(place, local_chunk, *chunks, up, folded)


def combine_kernel(n, place_ref, *refs):
    part_refs = refs[:n]
    pick_ref, scale_ref, base_ref, low_ref, middle_ref = refs[n:]
    span, lat = base_ref.shape
    packed = low_ref.shape[0]
    total = None
    for k in range(n):
        picked = jnp.dot(pick_ref[k], part_refs[k][...], preferred_element_type=F32)
        scaled = scale_ref[:, k : k + 1] * picked
        total = scaled if total is None else total + scaled
    low = (base_ref[...] + (total[:, :lat] + total[:, lat:])).astype(BF16)
    low_ref[...] = jnp.concatenate([low[:packed], low[span - packed :]], axis=1)
    edge = jnp.where(
        place_ref[0] >= place_ref[1] // 2, low[:EDGE_ROWS], low[span - EDGE_ROWS :]
    )
    middle_ref[...] = jnp.concatenate([edge, edge], axis=1)


def combine(place, parts, pick, scale, base):
    n = len(parts)
    span, lat = base.shape
    packed = -(-span // 32) * 16
    return pl.pallas_call(
        functools.partial(combine_kernel, n),
        out_shape=[
            jax.ShapeDtypeStruct((packed, 2 * lat), BF16),
            jax.ShapeDtypeStruct((EDGE_ROWS, 2 * lat), BF16),
        ],
        in_specs=[pl.BlockSpec(memory_space=pltpu.SMEM)] + [whole()] * (n + 3),
        out_specs=[whole()] * 2,
        compiler_params=params(16),
        cost_estimate=FREE,
    )(place, *parts, pick, scale, base)


def snake(v, turns_row, inverse_row):
    turns = v * turns_row
    part = turns - jnp.round(turns)
    s = part * part
    poly = SIN2[-1]
    for c in SIN2[-2::-1]:
        poly = poly * s + c
    return v + (poly * s) * inverse_row


def unpack_slab(place_ref, slab_ref, padded):
    span, lat = padded.shape
    packed = slab_ref.shape[0] - EDGE_ROWS
    end = span - 3 * EDGE
    padded[0:packed] = slab_ref[0:packed, :lat].astype(F32)
    padded[span - packed :] = slab_ref[0:packed, lat:].astype(F32)

    @pl.when(place_ref[1] == place_ref[2] // 2)
    def _():
        padded[0:EDGE] = slab_ref[packed:, :lat].astype(F32)[:EDGE]

    @pl.when(place_ref[1] == place_ref[2] // 2 - 1)
    def _():
        padded[end : end + EDGE] = slab_ref[packed:, :lat].astype(F32)[EDGE : 2 * EDGE]


def convolve(place_ref, padded, windows, conv_ref, alpha_ref, act):
    span, lat = padded.shape
    length = span - 4 * EDGE
    channels = conv_ref.shape[1]
    taps = conv_ref.shape[0] // lat
    block = 256
    is_first = place_ref[1] == 0
    is_last = place_ref[1] == place_ref[2] - 1
    row = lax.broadcasted_iota(jnp.int32, (16, taps * lat), 0)
    edge_row = lax.broadcasted_iota(jnp.int32, (16, block), 0)
    gone = ((edge_row == 0) & is_first) | ((edge_row == 1) & is_last)

    def window(start, rows):
        return jnp.concatenate([padded[start + j : start + j + rows] for j in range(taps)], axis=1)

    windows[0:length] = window(1, length).astype(BF16)
    edges = jnp.where(row == 0, window(0, 1), jnp.where(row == 1, window(length + 1, 1), 0.0))
    windows[length:] = edges.astype(BF16)
    for at in range(0, channels, block):
        cols = slice(at, at + block)
        v = jnp.dot(windows[...], conv_ref[:, cols], preferred_element_type=F32)
        value = snake(v, alpha_ref[0:1, cols], alpha_ref[1:2, cols])
        act[0:length, cols] = value[:length].astype(BF16)
        act[length:, cols] = jnp.where(gone, 0.0, value[length:]).astype(BF16)


def own_kernel(place_ref, slab_ref, conv_ref, alpha_ref, up_ref, act_ref, staged_ref, *scratch):
    padded, windows, sem = scratch
    copy = pltpu.make_async_copy(up_ref, staged_ref, sem)
    copy.start()
    unpack_slab(place_ref, slab_ref, padded)
    convolve(place_ref, padded, windows, conv_ref, alpha_ref, act_ref)
    copy.wait()


def activate_own(place, slab, conv, alpha, first_up, span):
    lat = slab.shape[1] // 2
    taps_lat, channels = conv.shape
    return pl.pallas_call(
        own_kernel,
        out_shape=[
            jax.ShapeDtypeStruct((span, channels), BF16),
            jax.ShapeDtypeStruct(first_up.shape, BF16),
        ],
        in_specs=[pl.BlockSpec(memory_space=pltpu.SMEM)]
        + [whole()] * 3
        + [pl.BlockSpec(memory_space=pl.ANY)],
        out_specs=[whole()] * 2,
        scratch_shapes=[
            pltpu.VMEM((span, lat), F32),
            pltpu.VMEM((span, taps_lat), BF16),
            pltpu.SemaphoreType.DMA,
        ],
        compiler_params=params(24),
        cost_estimate=FREE,
    )(place, slab, conv, alpha, first_up)


def decoder_kernel(segs, place_ref, own_ref, *refs):
    slab_refs = refs[: segs - 1]
    conv_ref, alpha_ref, up_ref, out_ref = refs[segs - 1 : segs + 3]
    padded, windows, others, rows_out, sems = refs[segs + 3 :]
    span = own_ref.shape[0]
    length = span - 4 * EDGE
    width = up_ref.shape[2]
    own = place_ref[0]

    def out_copy(k):
        return pltpu.make_async_copy(rows_out.at[k], out_ref.at[own ^ k], sems.at[k])

    for k in range(segs - 1):
        unpack_slab(place_ref, slab_refs[k], padded.at[k])
    for k in range(segs - 1):
        convolve(place_ref, padded.at[k], windows.at[k], conv_ref, alpha_ref, others.at[k])
    for k in range(segs):
        act = own_ref if k == 0 else others.at[k - 1]
        for r in range(0, 8, 2):
            far = r + 12 if r < 4 else r - 4
            near_w = jnp.concatenate([up_ref[r + 4], up_ref[r + 5]], axis=1)
            far_w = jnp.concatenate([up_ref[far], up_ref[far + 1]], axis=1)
            near = jnp.dot(act[0:length], near_w, preferred_element_type=F32)
            side = jnp.dot(act[...], far_w, preferred_element_type=F32)
            if r < 4:
                moved = [side[length : length + 1], side[: length - 1]]
            else:
                moved = [side[1:length], side[length + 1 : length + 2]]
            res = near + jnp.concatenate(moved, axis=0)
            rows_out[k, pl.ds(r, length, stride=8), :] = res[:, :width]
            rows_out[k, pl.ds(r + 1, length, stride=8), :] = res[:, width:]
        out_copy(k).start()
    for k in range(segs):
        out_copy(k).wait()


def decode(place, own, slabs, conv, alpha, first_up):
    segs = len(slabs) + 1
    span, channels = own.shape
    length = span - 4 * EDGE
    width = first_up.shape[2]
    lat = slabs[0].shape[1] // 2
    return pl.pallas_call(
        functools.partial(decoder_kernel, segs),
        out_shape=jax.ShapeDtypeStruct((segs, 8 * length, width), F32),
        in_specs=[pl.BlockSpec(memory_space=pltpu.SMEM)]
        + [whole()] * (segs + 3),
        out_specs=pl.BlockSpec(memory_space=pl.ANY),
        scratch_shapes=[
            pltpu.VMEM((segs - 1, span, lat), F32),
            pltpu.VMEM((segs - 1, span, conv.shape[0]), BF16),
            pltpu.VMEM((segs - 1, span, channels), BF16),
            pltpu.VMEM((segs, 8 * length, width), F32),
            pltpu.SemaphoreType.DMA((segs,)),
        ],
        compiler_params=params(32),
        cost_estimate=FREE,
    )(place, own, *slabs, conv, alpha, first_up)


def local(
    frames,
    expert_ids,
    gate_weights,
    up_weight,
    down_weight,
    out_weight,
    in_conv,
    snake_first,
    first_up,
):
    rows, _ = frames.shape
    n = lax.axis_size("expert")
    segs = lax.axis_size("seg")
    quarter, half = n // 4, n // 2
    capacity = -(-(3 * rows // n) // 16) * 16
    me = lax.axis_index("expert")
    place = jnp.stack([me, jnp.int32(n)]).astype(jnp.int32)
    inner = range(quarter, 3 * quarter)
    across_by = 3 * quarter
    is_inner = ((me >= quarter) & (me < across_by)).astype(jnp.int32)

    def swap(value, k, members=range(n)):
        return lax.ppermute(value, "expert", [(i, i ^ k) for i in members])

    across = swap(frames, across_by, inner)
    ids_t = expert_ids.T
    across_ids = swap(ids_t, across_by, inner)
    own = jnp.stack([me, 0]).astype(jnp.int32)
    gates_t, out_w_t = gate_weights.T, out_weight.T
    chunks = make_slots(own, range(half), (ids_t, frames, gates_t), capacity)
    near = [swap(chunks[k], k) for k in range(1, half)]
    origin = jnp.stack([me ^ (is_inner * across_by), is_inner]).astype(jnp.int32)
    sent = make_slots(
        origin, range(half, n), (ids_t, frames, across_ids, across), capacity
    )

    def cross(value, k):
        pairs = [(i, i ^ (k ^ across_by if i in inner else k)) for i in range(n)]
        return lax.ppermute(value, "expert", [(i, j) for i, j in pairs if i != j])

    far = [cross(sent[k - half], k) for k in range(across_by, n)]
    late, near = lax.optimization_barrier((sent[:quarter], near))
    far = [cross(late[k - half], k) for k in range(half, across_by)] + far
    up = up_weight[0]
    gates_t, chunk, down, late = lax.optimization_barrier(
        (gates_t, chunks[0], down_weight[0], late)
    )
    folded = fold_weights(down, out_w_t)
    neighbours = {k: near[k - 1] for k in range(1, half) if is_neighbour(k)}
    pick, scale, base = make_table(
        place, frames, out_w_t, ids_t, gates_t, neighbours, n, capacity
    )
    back = run_group(n, False, place, chunk, near, up, folded)
    parts = [back[0]] + [swap(back[k], k) for k in range(1, half)]
    place, pick, scale, base = lax.optimization_barrier((place, pick, scale, base))
    back = run_group(n, True, place, sent[quarter], far, up, folded)
    parts += [swap(back[k], half + k) for k in range(half)]
    slab, middle = combine(place, parts, pick, scale, base)
    middle = lax.ppermute(middle, "expert", [(half - 1, half), (half, half - 1)])
    slab = jnp.concatenate([slab, middle], axis=0)

    others = [
        lax.ppermute(slab, "seg", [(i, i ^ k) for i in range(segs)]) for k in range(1, segs)
    ]
    spot = jnp.stack([lax.axis_index("seg"), me, jnp.int32(n)]).astype(jnp.int32)
    alpha = jnp.stack([snake_first * (1.0 / math.pi), 1.0 / snake_first])
    conv = in_conv.reshape(-1, in_conv.shape[2])
    act, staged = activate_own(spot, slab, conv, alpha, first_up, base.shape[0])
    return decode(spot, act, others, conv, alpha, staged)


def solution(mesh):
    placed = (
        P(("seg", "expert"), None),
        P(("seg", "expert"), None),
        P(("seg", "expert"), None),
        P("expert", None, None),
        P("expert", None, None),
        P(),
        P(),
        P(),
        P(None, None, "seg"),
    )
    return jax.shard_map(
        local, mesh=mesh, in_specs=placed, out_specs=P(None, "expert", "seg"), check_vma=False
    )
```

```python
import functools
import math

import jax
import jax.numpy as jnp
from jax import lax
from jax.experimental import pallas as pl
from jax.experimental.pallas import tpu as pltpu
from jax.sharding import PartitionSpec as P

F32 = jnp.float32
BF16 = jnp.bfloat16
VMEM = pltpu.VMEM
SIN2 = (
    9.869603157043457,
    -32.469581604003906,
    42.72538375854492,
    -30.085954666137695,
    12.99073314666748,
    -3.2729504108428955,
)


FREE = pl.CostEstimate(flops=0, bytes_accessed=0, transcendentals=0)


def whole():
    return pl.BlockSpec(memory_space=VMEM)


def params(mib):
    return pltpu.CompilerParams(vmem_limit_bytes=mib * 1024 * 1024)


EDGE = 4
EDGE_ROWS = 16


def token_key(token, rows):
    rest = jnp.where(token >= rows - EDGE, token - (rows - 2 * EDGE), token + EDGE)
    return jnp.where(token < EDGE, token, rest)


def one_hot(mask):
    return mask.astype(F32).astype(BF16)


def is_neighbour(k):
    return k & (k + 1) == 0 and k > 0


def edge_rows(frames, ids, gates):
    rows, width = frames.shape
    parts = []
    for choice in range(2):
        rest = gates[choice : choice + 1]
        for _ in range(3):
            part = rest.astype(BF16).astype(F32)
            parts.append(part)
            rest = rest - part
    meta = jnp.concatenate([ids.astype(F32)] + parts, axis=0)
    meta = jnp.concatenate([meta, jnp.zeros((8, width - rows), F32)], axis=1)
    ends = [frames[:16].astype(F32)[:EDGE], frames[rows - 16 :].astype(F32)[16 - EDGE :]]
    return jnp.concatenate(ends + [meta], axis=0).astype(BF16)


def slots_kernel(steps, origin_ref, *refs):
    sources, out_refs = refs[: -len(steps)], refs[-len(steps) :]
    ids, frames = sources[0][...], sources[1][...]
    if len(sources) == 3:
        capacity = out_refs[0].shape[0]
        extra = edge_rows(frames, ids, sources[2][...])
        for k, ref in zip(steps, out_refs):
            if is_neighbour(k):
                ref[capacity:] = extra
    else:
        second = origin_ref[1] == 1
        ids = jnp.where(second, sources[2][...], ids)
        frames = jnp.where(second, sources[3][...], frames)
    rows = frames.shape[0]
    capacity = out_refs[0].shape[0]
    ids = ids ^ origin_ref[0]
    count = -(-len(steps) // 16) * 16
    step = lax.broadcasted_iota(jnp.int32, (count, rows), 0) + steps[0]
    named = (ids[0:1] == step) | (ids[1:2] == step)
    earlier = token_key(lax.broadcasted_iota(jnp.int32, (rows, rows), 0), rows) < token_key(
        lax.broadcasted_iota(jnp.int32, (rows, rows), 1), rows
    )
    rank = jnp.dot(one_hot(named), one_hot(earlier), preferred_element_type=F32)
    rank = jnp.where(named, rank, -1.0)
    slot = lax.broadcasted_iota(jnp.int32, (capacity, rows), 0).astype(F32)
    for j, ref in enumerate(out_refs):
        pick = one_hot(slot == rank[j : j + 1])
        ref[0:capacity] = jnp.dot(pick, frames, preferred_element_type=F32).astype(BF16)


def make_slots(origin, steps, sources, capacity):
    width = sources[1].shape[1]
    return pl.pallas_call(
        functools.partial(slots_kernel, steps),
        out_shape=[
            jax.ShapeDtypeStruct(
                (capacity + EDGE_ROWS * (len(sources) == 3 and is_neighbour(k)), width), BF16
            )
            for k in steps
        ],
        in_specs=[pl.BlockSpec(memory_space=pltpu.SMEM)] + [whole()] * len(sources),
        out_specs=[whole()] * len(steps),
        compiler_params=params(24),
        cost_estimate=FREE,
    )(origin, *sources)


def fold_kernel(down_ref, out_w_ref, folded_ref):
    full = lax.dot_general(
        down_ref[...], out_w_ref[...], (((1,), (1,)), ((), ())), preferred_element_type=F32
    )
    high = full.astype(BF16)
    low = (full - high.astype(F32)).astype(BF16)
    folded_ref[...] = jnp.concatenate([high, low], axis=1)


def fold_weights(down, out_w_t):
    hid, width = down.shape
    lat = out_w_t.shape[0]
    block = 512 if hid % 512 == 0 else hid
    return pl.pallas_call(
        fold_kernel,
        grid=(hid // block,),
        out_shape=jax.ShapeDtypeStruct((hid, 2 * lat), BF16),
        in_specs=[
            pl.BlockSpec((block, width), lambda i: (i, 0)),
            pl.BlockSpec((lat, width), lambda i: (0, 0)),
        ],
        out_specs=pl.BlockSpec((block, 2 * lat), lambda i: (i, 0)),
        compiler_params=params(16),
        cost_estimate=FREE,
    )(down, out_w_t)


def table_kernel(
    links, place_ref, frames_ref, out_w_ref, ids_ref, gates_ref, *refs
):
    link_refs = refs[: len(links)]
    pick_ref, scale_ref, base_ref = refs[len(links) :]
    n, span, columns = pick_ref.shape
    rows, width = frames_ref.shape
    lat = out_w_ref.shape[0]
    capacity = columns - 2 * EDGE_ROWS
    me, size = place_ref[0], place_ref[1]

    def rows_of(frames, lines):
        base = lax.dot_general(
            frames, out_w_ref[...], (((1,), (1,)), ((), ())), preferred_element_type=F32
        )
        lines = jnp.concatenate([lines, jnp.zeros((128 - lines.shape[0], rows), F32)], axis=0)
        return base, jnp.transpose(lines)[:, : 128 - lat]

    def neighbour(other):
        extra = link_refs[0][capacity:]
        for k, ref in zip(links[1:], link_refs[1:]):
            extra = jnp.where((me ^ other) == k, ref[capacity:], extra)
        meta = extra[:, :rows].astype(F32)[2 * EDGE :]
        gates = [meta[j : j + 1] + meta[j + 1 : j + 2] + meta[j + 2 : j + 3] for j in (2, 5)]
        base, lines = rows_of(extra, jnp.concatenate([meta[:2]] + gates, axis=0))
        return jnp.concatenate(
            [
                jnp.concatenate([base[:EDGE], lines[:EDGE]], axis=1),
                jnp.concatenate([base[EDGE : 2 * EDGE], lines[rows - EDGE :]], axis=1),
            ],
            axis=0,
        )

    left, right = neighbour(me - 1), neighbour(me + 1)
    own = rows_of(
        frames_ref[...], jnp.concatenate([ids_ref[...].astype(F32), gates_ref[...]], axis=0)
    )
    info = jnp.concatenate(
        [
            left[EDGE:],
            jnp.concatenate(own, axis=1),
            right[:EDGE],
            left[:EDGE],
            jnp.zeros((EDGE, 128), F32),
        ],
        axis=0,
    )
    def code(i):
        own = 1024 + token_key(i - EDGE, rows)
        late = jnp.where(i < rows + 3 * EDGE, i - rows - 2 * EDGE, 3072)
        tail = jnp.where(i < rows + 2 * EDGE, 2048 + i - rows - EDGE, late)
        return jnp.where(i < EDGE, i + EDGE, jnp.where(i < rows + EDGE, own, tail))

    line = lax.broadcasted_iota(jnp.int32, (span, 1), 0)
    line_code = code(line)
    other = code(lax.broadcasted_iota(jnp.int32, (1, span), 1))
    earlier = (other < line_code) & (other >= (line_code >> 10) * 1024)
    before = line_code < 1024
    after = (line_code >= 2048) & (line_code < 3072)
    lost = (before & ((me == 0) | (me == size // 2))) | (
        after & ((me == size - 1) | (me == size // 2 - 1))
    )
    base_ref[...] = jnp.where(lost, 0.0, info[:, :lat])
    ids = info[:, lat : lat + 2].astype(jnp.int32) ^ me
    ids = jnp.where(lost | (line_code >= 3072), -1, ids)
    step = lax.broadcasted_iota(jnp.int32, (span, 128), 1)
    first = ids[:, 0:1] == step
    second = ids[:, 1:2] == step
    named = first | second
    rank = jnp.dot(one_hot(earlier), one_hot(named), preferred_element_type=F32)
    rank = rank + jnp.where(before, capacity, jnp.where(after, capacity + EDGE_ROWS, 0)).astype(F32)
    rank = jnp.where(named, rank, -1.0)
    scale_ref[...] = jnp.where(
        first, info[:, lat + 2 : lat + 3], jnp.where(second, info[:, lat + 3 : lat + 4], 0.0)
    )
    slot = lax.broadcasted_iota(jnp.int32, (span, columns), 1).astype(F32)
    for k in range(n):
        pick_ref[k] = one_hot(slot == rank[:, k : k + 1])


def make_table(place, frames, out_w_t, ids_t, gates_t, neighbours, n, capacity):
    span = frames.shape[0] + 4 * EDGE
    lat = out_w_t.shape[0]
    links = tuple(neighbours)
    return pl.pallas_call(
        functools.partial(table_kernel, links),
        out_shape=[
            jax.ShapeDtypeStruct((n, span, capacity + 2 * EDGE_ROWS), BF16),
            jax.ShapeDtypeStruct((span, 128), F32),
            jax.ShapeDtypeStruct((span, lat), F32),
        ],
        in_specs=[pl.BlockSpec(memory_space=pltpu.SMEM)] + [whole()] * (4 + len(links)),
        out_specs=[whole()] * 3,
        compiler_params=params(16),
        cost_estimate=FREE,
    )(place, frames, out_w_t, ids_t, gates_t, *[neighbours[k] for k in links])


def expert_rows(rows, up_ref, folded_ref):
    hid = up_ref.shape[1]
    block = 256 if hid % 256 == 0 else hid
    total = None
    for at in range(0, hid, block):
        v = jnp.dot(rows, up_ref[:, at : at + block], preferred_element_type=F32)
        inner = v * (0.7978845608 + (0.7978845608 * 0.044715) * (v * v))
        hidden = (0.5 * v * (1.0 + jnp.tanh(inner))).astype(BF16)
        part = jnp.dot(hidden, folded_ref[at : at + block, :], preferred_element_type=F32)
        total = part if total is None else total + part
    lat = folded_ref.shape[1] // 2
    value = total[:, :lat] + total[:, lat:]
    high = value.astype(BF16)
    low = (value - high.astype(F32)).astype(BF16)
    return jnp.concatenate([high, low], axis=1)


def write_returns(n, me, held, first, outs):
    capacity = held.shape[1]
    half = n // 2
    for j, ref in enumerate(outs):
        k = first + j
        to = me ^ k
        place = to % half
        left = me ^ jnp.where(place > 0, to - 1, to)
        right = me ^ jnp.where(place < half - 1, to + 1, to)
        ref[0:capacity] = held[k]
        ref[capacity : capacity + EDGE_ROWS] = held[left, 0:EDGE_ROWS]
        ref[capacity + EDGE_ROWS :] = held[right, 0:EDGE_ROWS]


def group_kernel(n, far, place_ref, local_ref, *refs):
    quarter, half = n // 4, n // 2
    chunk_refs = refs[: half - 1 + far]
    up_ref, folded_ref = refs[half - 1 + far : half + 1 + far]
    outs, held = refs[half + 1 + far : -1], refs[-1]
    capacity = local_ref.shape[0]
    me = place_ref[0]
    chunks = [ref[...] for ref in chunk_refs]
    if far:
        is_inner = (me >= quarter) & (me < 3 * quarter)
        chunks[quarter] = jnp.where(is_inner, local_ref[...], chunks[quarter])
    else:
        chunks = [local_ref[...]] + [chunk[:capacity] for chunk in chunks]
    both = expert_rows(jnp.concatenate(chunks, axis=0), up_ref, folded_ref)
    first = half if far else 0
    for j in range(half):
        held[first + j] = both[j * capacity : (j + 1) * capacity]
    write_returns(n, me, held, first, outs)


def run_group(n, far, place, local_chunk, chunks, up, folded):
    capacity = local_chunk.shape[0]
    lanes = folded.shape[1]
    return pl.pallas_call(
        functools.partial(group_kernel, n, far),
        out_shape=[jax.ShapeDtypeStruct((capacity + 2 * EDGE_ROWS, lanes), BF16)] * (n // 2),
        in_specs=[pl.BlockSpec(memory_space=pltpu.SMEM)] + [whole()] * (len(chunks) + 3),
        out_specs=[whole()] * (n // 2),
        scratch_shapes=[pltpu.VMEM((n, capacity, lanes), BF16)],
        compiler_params=params(24),
        cost_estimate=FREE,
    )(place, local_chunk, *chunks, up, folded)


def combine_kernel(n, place_ref, *refs):
    part_refs = refs[:n]
    pick_ref, scale_ref, base_ref, low_ref, middle_ref = refs[n:]
    span, lat = base_ref.shape
    packed = low_ref.shape[0]
    total = None
    for k in range(n):
        picked = jnp.dot(pick_ref[k], part_refs[k][...], preferred_element_type=F32)
        scaled = scale_ref[:, k : k + 1] * picked
        total = scaled if total is None else total + scaled
    low = (base_ref[...] + (total[:, :lat] + total[:, lat:])).astype(BF16)
    low_ref[...] = jnp.concatenate([low[:packed], low[span - packed :]], axis=1)
    edge = jnp.where(
        place_ref[0] >= place_ref[1] // 2, low[:EDGE_ROWS], low[span - EDGE_ROWS :]
    )
    middle_ref[...] = jnp.concatenate([edge, edge], axis=1)


def combine(place, parts, pick, scale, base):
    n = len(parts)
    span, lat = base.shape
    packed = -(-span // 32) * 16
    return pl.pallas_call(
        functools.partial(combine_kernel, n),
        out_shape=[
            jax.ShapeDtypeStruct((packed, 2 * lat), BF16),
            jax.ShapeDtypeStruct((EDGE_ROWS, 2 * lat), BF16),
        ],
        in_specs=[pl.BlockSpec(memory_space=pltpu.SMEM)] + [whole()] * (n + 3),
        out_specs=[whole()] * 2,
        compiler_params=params(16),
        cost_estimate=FREE,
    )(place, *parts, pick, scale, base)


def snake(v, turns_row, inverse_row):
    turns = v * turns_row
    part = turns - jnp.round(turns)
    s = part * part
    poly = SIN2[-1]
    for c in SIN2[-2::-1]:
        poly = poly * s + c
    return v + (poly * s) * inverse_row


def unpack_slab(place_ref, slab_ref, padded):
    span, lat = padded.shape
    packed = slab_ref.shape[0] - EDGE_ROWS
    end = span - 3 * EDGE
    padded[0:packed] = slab_ref[0:packed, :lat].astype(F32)
    padded[span - packed :] = slab_ref[0:packed, lat:].astype(F32)

    @pl.when(place_ref[1] == place_ref[2] // 2)
    def _():
        padded[0:EDGE] = slab_ref[packed:, :lat].astype(F32)[:EDGE]

    @pl.when(place_ref[1] == place_ref[2] // 2 - 1)
    def _():
        padded[end : end + EDGE] = slab_ref[packed:, :lat].astype(F32)[EDGE : 2 * EDGE]


def convolve(place_ref, padded, windows, conv_ref, alpha_ref, act):
    span, lat = padded.shape
    length = span - 4 * EDGE
    channels = conv_ref.shape[1]
    taps = conv_ref.shape[0] // lat
    block = 256
    is_first = place_ref[1] == 0
    is_last = place_ref[1] == place_ref[2] - 1
    row = lax.broadcasted_iota(jnp.int32, (16, taps * lat), 0)
    edge_row = lax.broadcasted_iota(jnp.int32, (16, block), 0)
    gone = ((edge_row == 0) & is_first) | ((edge_row == 1) & is_last)

    def window(start, rows):
        return jnp.concatenate([padded[start + j : start + j + rows] for j in range(taps)], axis=1)

    windows[0:length] = window(1, length).astype(BF16)
    edges = jnp.where(row == 0, window(0, 1), jnp.where(row == 1, window(length + 1, 1), 0.0))
    windows[length:] = edges.astype(BF16)
    for at in range(0, channels, block):
        cols = slice(at, at + block)
        v = jnp.dot(windows[...], conv_ref[:, cols], preferred_element_type=F32)
        value = snake(v, alpha_ref[0:1, cols], alpha_ref[1:2, cols])
        act[0:length, cols] = value[:length].astype(BF16)
        act[length:, cols] = jnp.where(gone, 0.0, value[length:]).astype(BF16)


def own_kernel(place_ref, slab_ref, conv_ref, alpha_ref, up_ref, act_ref, staged_ref, *scratch):
    padded, windows, sem = scratch
    copy = pltpu.make_async_copy(up_ref, staged_ref, sem)
    copy.start()
    unpack_slab(place_ref, slab_ref, padded)
    convolve(place_ref, padded, windows, conv_ref, alpha_ref, act_ref)
    copy.wait()


def activate_own(place, slab, conv, alpha, first_up, span):
    lat = slab.shape[1] // 2
    taps_lat, channels = conv.shape
    return pl.pallas_call(
        own_kernel,
        out_shape=[
            jax.ShapeDtypeStruct((span, channels), BF16),
            jax.ShapeDtypeStruct(first_up.shape, BF16),
        ],
        in_specs=[pl.BlockSpec(memory_space=pltpu.SMEM)]
        + [whole()] * 3
        + [pl.BlockSpec(memory_space=pl.ANY)],
        out_specs=[whole()] * 2,
        scratch_shapes=[
            pltpu.VMEM((span, lat), F32),
            pltpu.VMEM((span, taps_lat), BF16),
            pltpu.SemaphoreType.DMA,
        ],
        compiler_params=params(47),
        cost_estimate=FREE,
    )(place, slab, conv, alpha, first_up)


def decoder_kernel(segs, place_ref, own_ref, *refs):
    slab_refs = refs[: segs - 1]
    conv_ref, alpha_ref, up_ref, out_ref = refs[segs - 1 : segs + 3]
    padded, windows, others, rows_out, sems = refs[segs + 3 :]
    span = own_ref.shape[0]
    length = span - 4 * EDGE
    width = up_ref.shape[2]
    own = place_ref[0]

    def out_copy(k):
        return pltpu.make_async_copy(rows_out.at[k], out_ref.at[own ^ k], sems.at[k])

    for k in range(segs - 1):
        unpack_slab(place_ref, slab_refs[k], padded.at[k])
    for k in range(segs - 1):
        convolve(place_ref, padded.at[k], windows.at[k], conv_ref, alpha_ref, others.at[k])
    for k in range(segs):
        act = own_ref if k == 0 else others.at[k - 1]
        for r in range(0, 8, 2):
            far = r + 12 if r < 4 else r - 4
            near_w = jnp.concatenate([up_ref[r + 4], up_ref[r + 5]], axis=1)
            far_w = jnp.concatenate([up_ref[far], up_ref[far + 1]], axis=1)
            near = jnp.dot(act[0:length], near_w, preferred_element_type=F32)
            side = jnp.dot(act[...], far_w, preferred_element_type=F32)
            if r < 4:
                moved = [side[length : length + 1], side[: length - 1]]
            else:
                moved = [side[1:length], side[length + 1 : length + 2]]
            res = near + jnp.concatenate(moved, axis=0)
            rows_out[k, pl.ds(r, length, stride=8), :] = res[:, :width]
            rows_out[k, pl.ds(r + 1, length, stride=8), :] = res[:, width:]
        out_copy(k).start()
    for k in range(segs):
        out_copy(k).wait()


def decode(place, own, slabs, conv, alpha, first_up):
    segs = len(slabs) + 1
    span, channels = own.shape
    length = span - 4 * EDGE
    width = first_up.shape[2]
    lat = slabs[0].shape[1] // 2
    return pl.pallas_call(
        functools.partial(decoder_kernel, segs),
        out_shape=jax.ShapeDtypeStruct((segs, 8 * length, width), F32),
        in_specs=[pl.BlockSpec(memory_space=pltpu.SMEM)]
        + [whole()] * (segs + 3),
        out_specs=pl.BlockSpec(memory_space=pl.ANY),
        scratch_shapes=[
            pltpu.VMEM((segs - 1, span, lat), F32),
            pltpu.VMEM((segs - 1, span, conv.shape[0]), BF16),
            pltpu.VMEM((segs - 1, span, channels), BF16),
            pltpu.VMEM((segs, 8 * length, width), F32),
            pltpu.SemaphoreType.DMA((segs,)),
        ],
        compiler_params=params(32),
        cost_estimate=FREE,
    )(place, own, *slabs, conv, alpha, first_up)


def local(
    frames,
    expert_ids,
    gate_weights,
    up_weight,
    down_weight,
    out_weight,
    in_conv,
    snake_first,
    first_up,
):
    rows, _ = frames.shape
    n = lax.axis_size("expert")
    segs = lax.axis_size("seg")
    quarter, half = n // 4, n // 2
    capacity = -(-(3 * rows // n) // 16) * 16
    me = lax.axis_index("expert")
    place = jnp.stack([me, jnp.int32(n)]).astype(jnp.int32)
    inner = range(quarter, 3 * quarter)
    across_by = 3 * quarter
    is_inner = ((me >= quarter) & (me < across_by)).astype(jnp.int32)

    def swap(value, k, members=range(n)):
        return lax.ppermute(value, "expert", [(i, i ^ k) for i in members])

    across = swap(frames, across_by, inner)
    ids_t = expert_ids.T
    across_ids = swap(ids_t, across_by, inner)
    own = jnp.stack([me, 0]).astype(jnp.int32)
    gates_t, out_w_t = gate_weights.T, out_weight.T
    chunks = make_slots(own, range(half), (ids_t, frames, gates_t), capacity)
    near = [swap(chunks[k], k) for k in range(1, half)]
    origin = jnp.stack([me ^ (is_inner * across_by), is_inner]).astype(jnp.int32)
    sent = make_slots(
        origin, range(half, n), (ids_t, frames, across_ids, across), capacity
    )

    def cross(value, k):
        pairs = [(i, i ^ (k ^ across_by if i in inner else k)) for i in range(n)]
        return lax.ppermute(value, "expert", [(i, j) for i, j in pairs if i != j])

    far = [cross(sent[k - half], k) for k in range(across_by, n)]
    late, near = lax.optimization_barrier((sent[:quarter], near))
    far = [cross(late[k - half], k) for k in range(half, across_by)] + far
    up = up_weight[0]
    gates_t, chunk, down, late = lax.optimization_barrier(
        (gates_t, chunks[0], down_weight[0], late)
    )
    folded = fold_weights(down, out_w_t)
    neighbours = {k: near[k - 1] for k in range(1, half) if is_neighbour(k)}
    pick, scale, base = make_table(
        place, frames, out_w_t, ids_t, gates_t, neighbours, n, capacity
    )
    back = run_group(n, False, place, chunk, near, up, folded)
    parts = [back[0]] + [swap(back[k], k) for k in range(1, half)]
    place, pick, scale, base = lax.optimization_barrier((place, pick, scale, base))
    back = run_group(n, True, place, sent[quarter], far, up, folded)
    parts += [swap(back[k], half + k) for k in range(half)]
    slab, middle = combine(place, parts, pick, scale, base)
    middle = lax.ppermute(middle, "expert", [(half - 1, half), (half, half - 1)])
    slab = jnp.concatenate([slab, middle], axis=0)

    others = [
        lax.ppermute(slab, "seg", [(i, i ^ k) for i in range(segs)]) for k in range(1, segs)
    ]
    spot = jnp.stack([lax.axis_index("seg"), me, jnp.int32(n)]).astype(jnp.int32)
    alpha = jnp.stack([snake_first * (1.0 / math.pi), 1.0 / snake_first])
    conv = in_conv.reshape(-1, in_conv.shape[2])
    act, staged = activate_own(spot, slab, conv, alpha, first_up, base.shape[0])
    return decode(spot, act, others, conv, alpha, staged)


def solution(mesh):
    placed = (
        P(("seg", "expert"), None),
        P(("seg", "expert"), None),
        P(("seg", "expert"), None),
        P("expert", None, None),
        P("expert", None, None),
        P(),
        P(),
        P(),
        P(None, None, "seg"),
    )
    return jax.shard_map(
        local, mesh=mesh, in_specs=placed, out_specs=P(None, "expert", "seg"), check_vma=False
    )
```

```python
import functools
import math

import jax
import jax.numpy as jnp
from jax import lax
from jax.experimental import pallas as pl
from jax.experimental.pallas import tpu as pltpu
from jax.sharding import PartitionSpec as P

F32 = jnp.float32
BF16 = jnp.bfloat16
VMEM = pltpu.VMEM
SIN2 = (
    9.869603157043457,
    -32.469581604003906,
    42.72538375854492,
    -30.085954666137695,
    12.99073314666748,
    -3.2729504108428955,
)


FREE = pl.CostEstimate(flops=0, bytes_accessed=0, transcendentals=0)


def whole():
    return pl.BlockSpec(memory_space=VMEM)


def params(mib):
    return pltpu.CompilerParams(vmem_limit_bytes=mib * 1024 * 1024)


EDGE = 4
EDGE_ROWS = 16


def token_key(token, rows):
    rest = jnp.where(token >= rows - EDGE, token - (rows - 2 * EDGE), token + EDGE)
    return jnp.where(token < EDGE, token, rest)


def one_hot(mask):
    return mask.astype(F32).astype(BF16)


def is_neighbour(k):
    return k & (k + 1) == 0 and k > 0


def edge_rows(frames, ids, gates):
    rows, width = frames.shape
    parts = []
    for choice in range(2):
        rest = gates[choice : choice + 1]
        for _ in range(3):
            part = rest.astype(BF16).astype(F32)
            parts.append(part)
            rest = rest - part
    meta = jnp.concatenate([ids.astype(F32)] + parts, axis=0)
    meta = jnp.concatenate([meta, jnp.zeros((8, width - rows), F32)], axis=1)
    ends = [frames[:16].astype(F32)[:EDGE], frames[rows - 16 :].astype(F32)[16 - EDGE :]]
    return jnp.concatenate(ends + [meta], axis=0).astype(BF16)


def slots_kernel(steps, origin_ref, *refs):
    sources, out_refs = refs[: -len(steps)], refs[-len(steps) :]
    ids, frames = sources[0][...], sources[1][...]
    if len(sources) == 3:
        capacity = out_refs[0].shape[0]
        extra = edge_rows(frames, ids, sources[2][...])
        for k, ref in zip(steps, out_refs):
            if is_neighbour(k):
                ref[capacity:] = extra
    else:
        second = origin_ref[1] == 1
        ids = jnp.where(second, sources[2][...], ids)
        frames = jnp.where(second, sources[3][...], frames)
    rows = frames.shape[0]
    capacity = out_refs[0].shape[0]
    ids = ids ^ origin_ref[0]
    count = -(-len(steps) // 16) * 16
    step = lax.broadcasted_iota(jnp.int32, (count, rows), 0) + steps[0]
    named = (ids[0:1] == step) | (ids[1:2] == step)
    earlier = token_key(lax.broadcasted_iota(jnp.int32, (rows, rows), 0), rows) < token_key(
        lax.broadcasted_iota(jnp.int32, (rows, rows), 1), rows
    )
    rank = jnp.dot(one_hot(named), one_hot(earlier), preferred_element_type=F32)
    rank = jnp.where(named, rank, -1.0)
    slot = lax.broadcasted_iota(jnp.int32, (capacity, rows), 0).astype(F32)
    for j, ref in enumerate(out_refs):
        pick = one_hot(slot == rank[j : j + 1])
        ref[0:capacity] = jnp.dot(pick, frames, preferred_element_type=F32).astype(BF16)


def make_slots(origin, steps, sources, capacity):
    width = sources[1].shape[1]
    return pl.pallas_call(
        functools.partial(slots_kernel, steps),
        out_shape=[
            jax.ShapeDtypeStruct(
                (capacity + EDGE_ROWS * (len(sources) == 3 and is_neighbour(k)), width), BF16
            )
            for k in steps
        ],
        in_specs=[pl.BlockSpec(memory_space=pltpu.SMEM)] + [whole()] * len(sources),
        out_specs=[whole()] * len(steps),
        compiler_params=params(24),
        cost_estimate=FREE,
    )(origin, *sources)


def fold_kernel(down_ref, out_w_ref, folded_ref):
    full = lax.dot_general(
        down_ref[...], out_w_ref[...], (((1,), (1,)), ((), ())), preferred_element_type=F32
    )
    high = full.astype(BF16)
    low = (full - high.astype(F32)).astype(BF16)
    folded_ref[...] = jnp.concatenate([high, low], axis=1)


def fold_weights(down, out_w_t):
    hid, width = down.shape
    lat = out_w_t.shape[0]
    block = 512 if hid % 512 == 0 else hid
    return pl.pallas_call(
        fold_kernel,
        grid=(hid // block,),
        out_shape=jax.ShapeDtypeStruct((hid, 2 * lat), BF16),
        in_specs=[
            pl.BlockSpec((block, width), lambda i: (i, 0)),
            pl.BlockSpec((lat, width), lambda i: (0, 0)),
        ],
        out_specs=pl.BlockSpec((block, 2 * lat), lambda i: (i, 0)),
        compiler_params=params(16),
        cost_estimate=FREE,
    )(down, out_w_t)


def table_kernel(
    links, place_ref, frames_ref, out_w_ref, ids_ref, gates_ref, *refs
):
    link_refs = refs[: len(links)]
    pick_ref, scale_ref, base_ref = refs[len(links) :]
    n, span, columns = pick_ref.shape
    rows, width = frames_ref.shape
    lat = out_w_ref.shape[0]
    capacity = columns - 2 * EDGE_ROWS
    me, size = place_ref[0], place_ref[1]

    def rows_of(frames, lines):
        base = lax.dot_general(
            frames, out_w_ref[...], (((1,), (1,)), ((), ())), preferred_element_type=F32
        )
        lines = jnp.concatenate([lines, jnp.zeros((128 - lines.shape[0], rows), F32)], axis=0)
        return base, jnp.transpose(lines)[:, : 128 - lat]

    def neighbour(other):
        extra = link_refs[0][capacity:]
        for k, ref in zip(links[1:], link_refs[1:]):
            extra = jnp.where((me ^ other) == k, ref[capacity:], extra)
        meta = extra[:, :rows].astype(F32)[2 * EDGE :]
        gates = [meta[j : j + 1] + meta[j + 1 : j + 2] + meta[j + 2 : j + 3] for j in (2, 5)]
        base, lines = rows_of(extra, jnp.concatenate([meta[:2]] + gates, axis=0))
        return jnp.concatenate(
            [
                jnp.concatenate([base[:EDGE], lines[:EDGE]], axis=1),
                jnp.concatenate([base[EDGE : 2 * EDGE], lines[rows - EDGE :]], axis=1),
            ],
            axis=0,
        )

    left, right = neighbour(me - 1), neighbour(me + 1)
    own = rows_of(
        frames_ref[...], jnp.concatenate([ids_ref[...].astype(F32), gates_ref[...]], axis=0)
    )
    info = jnp.concatenate(
        [
            left[EDGE:],
            jnp.concatenate(own, axis=1),
            right[:EDGE],
            left[:EDGE],
            jnp.zeros((EDGE, 128), F32),
        ],
        axis=0,
    )
    def code(i):
        own = 1024 + token_key(i - EDGE, rows)
        late = jnp.where(i < rows + 3 * EDGE, i - rows - 2 * EDGE, 3072)
        tail = jnp.where(i < rows + 2 * EDGE, 2048 + i - rows - EDGE, late)
        return jnp.where(i < EDGE, i + EDGE, jnp.where(i < rows + EDGE, own, tail))

    line = lax.broadcasted_iota(jnp.int32, (span, 1), 0)
    line_code = code(line)
    other = code(lax.broadcasted_iota(jnp.int32, (1, span), 1))
    earlier = (other < line_code) & (other >= (line_code >> 10) * 1024)
    before = line_code < 1024
    after = (line_code >= 2048) & (line_code < 3072)
    lost = (before & ((me == 0) | (me == size // 2))) | (
        after & ((me == size - 1) | (me == size // 2 - 1))
    )
    base_ref[...] = jnp.where(lost, 0.0, info[:, :lat])
    ids = info[:, lat : lat + 2].astype(jnp.int32) ^ me
    ids = jnp.where(lost | (line_code >= 3072), -1, ids)
    step = lax.broadcasted_iota(jnp.int32, (span, 128), 1)
    first = ids[:, 0:1] == step
    second = ids[:, 1:2] == step
    named = first | second
    rank = jnp.dot(one_hot(earlier), one_hot(named), preferred_element_type=F32)
    rank = rank + jnp.where(before, capacity, jnp.where(after, capacity + EDGE_ROWS, 0)).astype(F32)
    rank = jnp.where(named, rank, -1.0)
    scale_ref[...] = jnp.where(
        first, info[:, lat + 2 : lat + 3], jnp.where(second, info[:, lat + 3 : lat + 4], 0.0)
    )
    slot = lax.broadcasted_iota(jnp.int32, (span, columns), 1).astype(F32)
    for k in range(n):
        pick_ref[k] = one_hot(slot == rank[:, k : k + 1])


def make_table(place, frames, out_w_t, ids_t, gates_t, neighbours, n, capacity):
    span = frames.shape[0] + 4 * EDGE
    lat = out_w_t.shape[0]
    links = tuple(neighbours)
    return pl.pallas_call(
        functools.partial(table_kernel, links),
        out_shape=[
            jax.ShapeDtypeStruct((n, span, capacity + 2 * EDGE_ROWS), BF16),
            jax.ShapeDtypeStruct((span, 128), F32),
            jax.ShapeDtypeStruct((span, lat), F32),
        ],
        in_specs=[pl.BlockSpec(memory_space=pltpu.SMEM)] + [whole()] * (4 + len(links)),
        out_specs=[whole()] * 3,
        compiler_params=params(16),
        cost_estimate=FREE,
    )(place, frames, out_w_t, ids_t, gates_t, *[neighbours[k] for k in links])


def expert_rows(rows, up_ref, folded_ref):
    hid = up_ref.shape[1]
    block = 256 if hid % 256 == 0 else hid
    total = None
    for at in range(0, hid, block):
        v = jnp.dot(rows, up_ref[:, at : at + block], preferred_element_type=F32)
        inner = v * (0.7978845608 + (0.7978845608 * 0.044715) * (v * v))
        hidden = (0.5 * v * (1.0 + jnp.tanh(inner))).astype(BF16)
        part = jnp.dot(hidden, folded_ref[at : at + block, :], preferred_element_type=F32)
        total = part if total is None else total + part
    lat = folded_ref.shape[1] // 2
    value = total[:, :lat] + total[:, lat:]
    high = value.astype(BF16)
    low = (value - high.astype(F32)).astype(BF16)
    return jnp.concatenate([high, low], axis=1)


def write_returns(n, me, held, first, outs):
    capacity = held.shape[1]
    half = n // 2
    for j, ref in enumerate(outs):
        k = first + j
        to = me ^ k
        place = to % half
        left = me ^ jnp.where(place > 0, to - 1, to)
        right = me ^ jnp.where(place < half - 1, to + 1, to)
        ref[0:capacity] = held[k]
        ref[capacity : capacity + EDGE_ROWS] = held[left, 0:EDGE_ROWS]
        ref[capacity + EDGE_ROWS :] = held[right, 0:EDGE_ROWS]


def group_kernel(n, far, place_ref, local_ref, *refs):
    quarter, half = n // 4, n // 2
    chunk_refs = refs[: half - 1 + far]
    up_ref, folded_ref = refs[half - 1 + far : half + 1 + far]
    outs, held = refs[half + 1 + far : -1], refs[-1]
    capacity = local_ref.shape[0]
    me = place_ref[0]
    chunks = [ref[...] for ref in chunk_refs]
    if far:
        is_inner = (me >= quarter) & (me < 3 * quarter)
        chunks[quarter] = jnp.where(is_inner, local_ref[...], chunks[quarter])
    else:
        chunks = [local_ref[...]] + [chunk[:capacity] for chunk in chunks]
    both = expert_rows(jnp.concatenate(chunks, axis=0), up_ref, folded_ref)
    first = half if far else 0
    for j in range(half):
        held[first + j] = both[j * capacity : (j + 1) * capacity]
    write_returns(n, me, held, first, outs)


def run_group(n, far, place, local_chunk, chunks, up, folded):
    capacity = local_chunk.shape[0]
    lanes = folded.shape[1]
    return pl.pallas_call(
        functools.partial(group_kernel, n, far),
        out_shape=[jax.ShapeDtypeStruct((capacity + 2 * EDGE_ROWS, lanes), BF16)] * (n // 2),
        in_specs=[pl.BlockSpec(memory_space=pltpu.SMEM)] + [whole()] * (len(chunks) + 3),
        out_specs=[whole()] * (n // 2),
        scratch_shapes=[pltpu.VMEM((n, capacity, lanes), BF16)],
        compiler_params=params(24),
        cost_estimate=FREE,
    )(place, local_chunk, *chunks, up, folded)


def combine_kernel(n, place_ref, *refs):
    part_refs = refs[:n]
    pick_ref, scale_ref, base_ref, low_ref, middle_ref = refs[n:]
    span, lat = base_ref.shape
    packed = low_ref.shape[0]
    total = None
    for k in range(n):
        picked = jnp.dot(pick_ref[k], part_refs[k][...], preferred_element_type=F32)
        scaled = scale_ref[:, k : k + 1] * picked
        total = scaled if total is None else total + scaled
    low = (base_ref[...] + (total[:, :lat] + total[:, lat:])).astype(BF16)
    low_ref[...] = jnp.concatenate([low[:packed], low[span - packed :]], axis=1)
    edge = jnp.where(
        place_ref[0] >= place_ref[1] // 2, low[:EDGE_ROWS], low[span - EDGE_ROWS :]
    )
    middle_ref[...] = jnp.concatenate([edge, edge], axis=1)


def combine(place, parts, pick, scale, base):
    n = len(parts)
    span, lat = base.shape
    packed = -(-span // 32) * 16
    return pl.pallas_call(
        functools.partial(combine_kernel, n),
        out_shape=[
            jax.ShapeDtypeStruct((packed, 2 * lat), BF16),
            jax.ShapeDtypeStruct((EDGE_ROWS, 2 * lat), BF16),
        ],
        in_specs=[pl.BlockSpec(memory_space=pltpu.SMEM)] + [whole()] * (n + 3),
        out_specs=[whole()] * 2,
        compiler_params=params(16),
        cost_estimate=FREE,
    )(place, *parts, pick, scale, base)


def snake(v, turns_row, inverse_row):
    turns = v * turns_row
    part = turns - jnp.round(turns)
    s = part * part
    poly = SIN2[-1]
    for c in SIN2[-2::-1]:
        poly = poly * s + c
    return v + (poly * s) * inverse_row


def unpack_slab(place_ref, slab_ref, padded):
    span, lat = padded.shape
    packed = slab_ref.shape[0] - EDGE_ROWS
    end = span - 3 * EDGE
    padded[0:packed] = slab_ref[0:packed, :lat].astype(F32)
    padded[span - packed :] = slab_ref[0:packed, lat:].astype(F32)

    @pl.when(place_ref[1] == place_ref[2] // 2)
    def _():
        padded[0:EDGE] = slab_ref[packed:, :lat].astype(F32)[:EDGE]

    @pl.when(place_ref[1] == place_ref[2] // 2 - 1)
    def _():
        padded[end : end + EDGE] = slab_ref[packed:, :lat].astype(F32)[EDGE : 2 * EDGE]


def convolve(place_ref, padded, windows, conv_ref, alpha_ref, act):
    span, lat = padded.shape
    length = span - 4 * EDGE
    channels = conv_ref.shape[1]
    taps = conv_ref.shape[0] // lat
    block = 256
    is_first = place_ref[1] == 0
    is_last = place_ref[1] == place_ref[2] - 1
    row = lax.broadcasted_iota(jnp.int32, (16, taps * lat), 0)
    edge_row = lax.broadcasted_iota(jnp.int32, (16, block), 0)
    gone = ((edge_row == 0) & is_first) | ((edge_row == 1) & is_last)

    def window(start, rows):
        return jnp.concatenate([padded[start + j : start + j + rows] for j in range(taps)], axis=1)

    windows[0:length] = window(1, length).astype(BF16)
    edges = jnp.where(row == 0, window(0, 1), jnp.where(row == 1, window(length + 1, 1), 0.0))
    windows[length:] = edges.astype(BF16)
    for at in range(0, channels, block):
        cols = slice(at, at + block)
        v = jnp.dot(windows[...], conv_ref[:, cols], preferred_element_type=F32)
        value = snake(v, alpha_ref[0:1, cols], alpha_ref[1:2, cols])
        act[0:length, cols] = value[:length].astype(BF16)
        act[length:, cols] = jnp.where(gone, 0.0, value[length:]).astype(BF16)


def own_kernel(place_ref, slab_ref, conv_ref, alpha_ref, act_ref, padded, windows):
    unpack_slab(place_ref, slab_ref, padded)
    convolve(place_ref, padded, windows, conv_ref, alpha_ref, act_ref)


def activate_own(place, slab, conv, alpha, span):
    lat = slab.shape[1] // 2
    taps_lat, channels = conv.shape
    return pl.pallas_call(
        own_kernel,
        out_shape=jax.ShapeDtypeStruct((span, channels), BF16),
        in_specs=[pl.BlockSpec(memory_space=pltpu.SMEM)] + [whole()] * 3,
        out_specs=whole(),
        scratch_shapes=[pltpu.VMEM((span, lat), F32), pltpu.VMEM((span, taps_lat), BF16)],
        compiler_params=params(16),
        cost_estimate=FREE,
    )(place, slab, conv, alpha)


def decoder_kernel(segs, place_ref, own_ref, *refs):
    slab_refs = refs[: segs - 1]
    conv_ref, alpha_ref, up_hbm, out_ref = refs[segs - 1 : segs + 3]
    padded, windows, others, up_ref, rows_out, sems, up_sems = refs[segs + 3 :]
    span = own_ref.shape[0]
    length = span - 4 * EDGE
    width = up_ref.shape[2]
    own = place_ref[0]
    pairs = [first for r in range(0, 8, 2) for first in (r + 4, r + 12 if r < 4 else r - 4)]
    up_copies = [
        pltpu.make_async_copy(
            up_hbm.at[pl.ds(first, 2)], up_ref.at[pl.ds(first, 2)], up_sems.at[j]
        )
        for j, first in enumerate(pairs)
    ]
    for copy in up_copies:
        copy.start()

    def out_copy(k):
        return pltpu.make_async_copy(rows_out.at[k], out_ref.at[own ^ k], sems.at[k])

    for k in range(segs - 1):
        unpack_slab(place_ref, slab_refs[k], padded.at[k])
    for k in range(segs - 1):
        convolve(place_ref, padded.at[k], windows.at[k], conv_ref, alpha_ref, others.at[k])
    for k in range(segs):
        act = own_ref if k == 0 else others.at[k - 1]
        for r in range(0, 8, 2):
            far = r + 12 if r < 4 else r - 4
            if k == 0:
                up_copies[r].wait()
                up_copies[r + 1].wait()
            near_w = jnp.concatenate([up_ref[r + 4], up_ref[r + 5]], axis=1)
            far_w = jnp.concatenate([up_ref[far], up_ref[far + 1]], axis=1)
            near = jnp.dot(act[0:length], near_w, preferred_element_type=F32)
            side = jnp.dot(act[...], far_w, preferred_element_type=F32)
            if r < 4:
                moved = [side[length : length + 1], side[: length - 1]]
            else:
                moved = [side[1:length], side[length + 1 : length + 2]]
            res = near + jnp.concatenate(moved, axis=0)
            rows_out[k, pl.ds(r, length, stride=8), :] = res[:, :width]
            rows_out[k, pl.ds(r + 1, length, stride=8), :] = res[:, width:]
        out_copy(k).start()
    for k in range(segs):
        out_copy(k).wait()


def decode(place, own, slabs, conv, alpha, first_up):
    segs = len(slabs) + 1
    span, channels = own.shape
    length = span - 4 * EDGE
    width = first_up.shape[2]
    lat = slabs[0].shape[1] // 2
    return pl.pallas_call(
        functools.partial(decoder_kernel, segs),
        out_shape=jax.ShapeDtypeStruct((segs, 8 * length, width), F32),
        in_specs=[pl.BlockSpec(memory_space=pltpu.SMEM)]
        + [whole()] * (segs + 2)
        + [pl.BlockSpec(memory_space=pl.ANY)],
        out_specs=pl.BlockSpec(memory_space=pl.ANY),
        scratch_shapes=[
            pltpu.VMEM((segs - 1, span, lat), F32),
            pltpu.VMEM((segs - 1, span, conv.shape[0]), BF16),
            pltpu.VMEM((segs - 1, span, channels), BF16),
            pltpu.VMEM(first_up.shape, BF16),
            pltpu.VMEM((segs, 8 * length, width), F32),
            pltpu.SemaphoreType.DMA((segs,)),
            pltpu.SemaphoreType.DMA((8,)),
        ],
        compiler_params=params(52),
        cost_estimate=FREE,
    )(place, own, *slabs, conv, alpha, first_up)


def local(
    frames,
    expert_ids,
    gate_weights,
    up_weight,
    down_weight,
    out_weight,
    in_conv,
    snake_first,
    first_up,
):
    rows, _ = frames.shape
    n = lax.axis_size("expert")
    segs = lax.axis_size("seg")
    quarter, half = n // 4, n // 2
    capacity = -(-(3 * rows // n) // 16) * 16
    me = lax.axis_index("expert")
    place = jnp.stack([me, jnp.int32(n)]).astype(jnp.int32)
    inner = range(quarter, 3 * quarter)
    across_by = 3 * quarter
    is_inner = ((me >= quarter) & (me < across_by)).astype(jnp.int32)

    def swap(value, k, members=range(n)):
        return lax.ppermute(value, "expert", [(i, i ^ k) for i in members])

    across = swap(frames, across_by, inner)
    ids_t = expert_ids.T
    across_ids = swap(ids_t, across_by, inner)
    own = jnp.stack([me, 0]).astype(jnp.int32)
    gates_t, out_w_t = gate_weights.T, out_weight.T
    chunks = make_slots(own, range(half), (ids_t, frames, gates_t), capacity)
    near = [swap(chunks[k], k) for k in range(1, half)]
    origin = jnp.stack([me ^ (is_inner * across_by), is_inner]).astype(jnp.int32)
    sent = make_slots(
        origin, range(half, n), (ids_t, frames, across_ids, across), capacity
    )

    def cross(value, k):
        pairs = [(i, i ^ (k ^ across_by if i in inner else k)) for i in range(n)]
        return lax.ppermute(value, "expert", [(i, j) for i, j in pairs if i != j])

    far = [cross(sent[k - half], k) for k in range(across_by, n)]
    late, near = lax.optimization_barrier((sent[:quarter], near))
    far = [cross(late[k - half], k) for k in range(half, across_by)] + far
    up = up_weight[0]
    gates_t, chunk, down, late = lax.optimization_barrier(
        (gates_t, chunks[0], down_weight[0], late)
    )
    folded = fold_weights(down, out_w_t)
    neighbours = {k: near[k - 1] for k in range(1, half) if is_neighbour(k)}
    pick, scale, base = make_table(
        place, frames, out_w_t, ids_t, gates_t, neighbours, n, capacity
    )
    back = run_group(n, False, place, chunk, near, up, folded)
    parts = [back[0]] + [swap(back[k], k) for k in range(1, half)]
    place, pick, scale, base = lax.optimization_barrier((place, pick, scale, base))
    back = run_group(n, True, place, sent[quarter], far, up, folded)
    parts += [swap(back[k], half + k) for k in range(half)]
    slab, middle = combine(place, parts, pick, scale, base)
    middle = lax.ppermute(middle, "expert", [(half - 1, half), (half, half - 1)])
    slab = jnp.concatenate([slab, middle], axis=0)

    others = [
        lax.ppermute(slab, "seg", [(i, i ^ k) for i in range(segs)]) for k in range(1, segs)
    ]
    spot = jnp.stack([lax.axis_index("seg"), me, jnp.int32(n)]).astype(jnp.int32)
    alpha = jnp.stack([snake_first * (1.0 / math.pi), 1.0 / snake_first])
    conv = in_conv.reshape(-1, in_conv.shape[2])
    act = activate_own(spot, slab, conv, alpha, base.shape[0])
    return decode(spot, act, others, conv, alpha, first_up)


def solution(mesh):
    placed = (
        P(("seg", "expert"), None),
        P(("seg", "expert"), None),
        P(("seg", "expert"), None),
        P("expert", None, None),
        P("expert", None, None),
        P(),
        P(),
        P(),
        P(None, None, "seg"),
    )
    return jax.shard_map(
        local, mesh=mesh, in_specs=placed, out_specs=P(None, "expert", "seg"), check_vma=False
    )
```
